256 devices in a mesh: tm: 16 (over x, y), rows: 8 (over z), clip: 2 (over core).
Axes of the slice: x: 4, y: 4, z: 8, core: 2. Of those that a mesh axis runs over, the one named last changes fastest.
Arguments:
- activations: bfloat16 [2, 192, 48, 32, 128], P('clip', None, 'tm', 'rows'), may hold values from -30 to 30
- norm_gain: float32 [192], replicated, may hold values from 0.5 to 1.5
- conv_weights: bfloat16 [192, 27, 192], replicated, may hold values from -0.078125 to 0.078125
- packed_grads: bfloat16 [2, 128, 128, 4608], P('clip', ('tm', 'rows')), may hold values from -12 to 12
- piece_lengths: int32 [2, 128, 128], P('clip', ('tm', 'rows')), may hold values from 1 to 24, 1536 in all within a row
Outputs:
- input_grad: bfloat16 [2, 192, 48, 32, 128], P('clip', None, 'tm', 'rows')
- weight_grad: float32 [192, 27, 192], replicated
- gain_grad: float32 [192], replicated
The draws below stay inside these ranges and needn't reach their ends.
Inputs may be any that keep to these rules, and one draw needn't show every extreme that they name: piece_lengths[c, d, :] sums to 1536 for every clip and destination; its largest entry is 24.
All inputs are finite; a program needn't handle non-finite values.
Results may differ from the reference program's by a relative error of at most 0.0045.
Values may be sent and summed in bfloat16 or wider, within the bound.
No kernel may reach another device: no remote copies, remote signals or barrier semaphores. Data moves between devices by JAX's collectives and lax.ppermute only.
A program may use at most 128 MiB of HBM per device.

```python
import functools
import math
import jax
import jax.numpy as jnp
import numpy as np
from jax import lax

CH = 192
FR_DEV = 3
ROWS_DEV = 4
WID = 128
CLIPS = 2
FRAMES = 48
ROWS = 32
VOX = 1536
GROUP = 128
MOST = 24
ALLVOX = 393216
N_TM = 16
N_ROWS = 8


def draw_activations(key, part):
    key = jax.random.fold_in(key, 5)
    first, second, third = jax.random.split(key, 3)
    shape = (CLIPS, CH, FRAMES, ROWS, WID)
    chan_scale = jnp.exp(jax.random.uniform(second, (1, CH, 1, 1, 1), jnp.float32, 0.0, math.log(10.0)))
    cell_scale = jnp.exp(jax.random.uniform(third, (CLIPS, 1, FRAMES, ROWS, WID), jnp.float32, 0.0, math.log(10.0)))
    base = jax.random.normal(first, shape, jnp.float32)
    return jnp.clip(base * chan_scale * cell_scale / 3.0, -30.0, 30.0).astype(jnp.bfloat16)


def draw_packed_grads(key, part):
    key = jax.random.fold_in(key, 7)
    first = jax.random.fold_in(key, 0)
    shape = (CLIPS, GROUP, GROUP, MOST * CH)
    rising = 0.5 + jnp.arange(GROUP, dtype=jnp.float32).reshape(1, 1, GROUP, 1) / max(GROUP - 1, 1)
    base = jax.random.normal(first, shape, jnp.float32)
    return jnp.clip(base * rising, -12.0, 12.0).astype(jnp.bfloat16)


def split_up(number_of, total, most, slope):
    portions = [(1 << 20) // math.isqrt(rank ** slope) + 1 for rank in range(2, number_of + 1)]
    spare, counts = total - most - (number_of - 1), [1] * (number_of - 1)
    while spare > 0:
        candidates = [i for i in range(number_of - 1) if counts[i] < most]
        pool, budget = sum([portions[i] for i in candidates]), spare
        for i in candidates:
            extra = min(most - counts[i], max(1, budget * portions[i] // pool), spare)
            counts[i] = counts[i] + extra
            spare = spare - extra
    return np.array([most] + counts)


def uneven_parts(rng, amount, total, most, skew):
    if amount == 2:
        one = jax.random.randint(rng, (), max(1, total - most), min(most, total - 1) + 1)
        return jnp.stack([one, total - one])
    tallies = jnp.asarray(split_up(amount, total, most, skew), jnp.int32)
    pairs = (amount - 1) // 2
    donor, taker = tallies[1:1 + 2 * pairs:2], tallies[2:2 + 2 * pairs:2]
    slack = jnp.minimum(donor - 1, most - taker)
    moved = jax.random.randint(jax.random.fold_in(rng, 1), (pairs,), 0, 1 << 20) % (slack + 1)
    tallies = tallies.at[1:1 + 2 * pairs:2].set(donor - moved).at[2:2 + 2 * pairs:2].set(taker + moved)
    return tallies[jax.random.permutation(jax.random.fold_in(rng, 2), amount)]


def bell_draw(stream_key, dims, width, most, kind=jnp.bfloat16):
    result = jax.random.normal(stream_key, dims, jnp.float32) * width
    return jnp.minimum(jnp.maximum(result, -most), most).astype(kind)


def setup_inputs(seed: int = 0) -> dict:
    key_list = jax.random.split(jax.random.key(seed), 6)
    return {
        "activations": draw_activations(jax.random.fold_in(key_list[5], 71), 0),
        "norm_gain": jnp.clip(jax.random.uniform(key_list[1], (CH,), jnp.float32, 0.5, 1.5), 0.5, 1.5),
        "conv_weights": bell_draw(key_list[2], (CH, 27, CH), (27 * CH) ** -0.5, 0.078125),
        "packed_grads": draw_packed_grads(jax.random.fold_in(key_list[5], 71), 0),
        "piece_lengths": jax.vmap(lambda own: uneven_parts(own, GROUP, VOX, MOST, 2))(jax.random.split(key_list[4], CLIPS * GROUP)).reshape((CLIPS, GROUP, GROUP)).astype(jnp.int32),
    }


epsilon = 1e-06

def unpack_rows(arrived, lengths, capacity, voxels):
    owners = lengths.shape[0]
    channels = arrived.shape[1] // capacity
    ends_at = jnp.cumsum(lengths).astype(jnp.int32)
    voxel_ids = jnp.arange(voxels, dtype=jnp.int32)
    before = ends_at[None, :] <= voxel_ids[:, None]
    source = lax.optimization_barrier(jnp.sum(before.astype(jnp.int32), axis=1)).astype(jnp.int32)
    begins = lax.optimization_barrier(jnp.sum(jnp.where(before, lengths[None, :], 0), axis=1)).astype(jnp.int32)
    slot_index = (source * capacity + voxel_ids - begins).astype(jnp.int32)
    row_table = arrived.reshape(owners * capacity, channels)
    return jnp.take(row_table, slot_index, axis=0).T

def tap_window(padded, step_time, step_row, step_col, frame_span, row_span, col_span):
    piece = padded[:, step_time:step_time + frame_span, step_row:step_row + row_span, step_col:step_col + col_span]
    return piece.reshape(padded.shape[0], frame_span * row_span * col_span)

def reference(activations, norm_gain, conv_weights, packed_grads, piece_lengths):
    flipped = jnp.flip(conv_weights, 1).transpose(2, 1, 0)
    cells = FRAMES * ROWS * WID
    weight_sum = jnp.zeros((CH, 27, CH), jnp.float32)
    gain_sum = jnp.zeros((CH,), jnp.float32)
    gain_cols = norm_gain[:, None, None, None]
    unpack_all = jax.vmap(functools.partial(unpack_rows, capacity=MOST, voxels=VOX), in_axes=(1, 0))
    results = []
    for clip_index in range(CLIPS):
        widened = activations[clip_index].astype(jnp.float32)
        inverse = lax.rsqrt(lax.optimization_barrier(jnp.mean(widened * widened, axis=0, keepdims=True)) + epsilon)
        normed = widened * inverse
        preact = normed * gain_cols
        hidden = jax.nn.silu(preact).astype(jnp.bfloat16)
        padded = jnp.pad(hidden, ((0, 0), (2, 0), (1, 1), (1, 1)))
        per_dest = unpack_all(packed_grads[clip_index], piece_lengths[clip_index])
        cotangent = per_dest.reshape(N_TM, N_ROWS, CH, FR_DEV, ROWS_DEV, WID)
        cotangent = cotangent.transpose(2, 0, 3, 1, 4, 5).reshape(CH, FRAMES, ROWS, WID)
        flat_grad = cotangent.reshape(CH, cells)
        grad_pad = jnp.pad(cotangent, ((0, 0), (0, 2), (1, 1), (1, 1)))
        hidden_grad = jnp.zeros((CH, cells), jnp.float32)
        terms = []
        for step_time in range(3):
            for step_row in range(3):
                for step_col in range(3):
                    tap = step_time * 9 + step_row * 3 + step_col
                    window = tap_window(padded, step_time, step_row, step_col, FRAMES, ROWS, WID)
                    terms.append(lax.dot_general(flat_grad, window, (((1,), (1,)), ((), ())), preferred_element_type=jnp.float32))
                    grad_window = tap_window(grad_pad, step_time, step_row, step_col, FRAMES, ROWS, WID)
                    hidden_grad = hidden_grad + jnp.dot(flipped[:, tap, :], grad_window, preferred_element_type=jnp.float32)
        weight_sum = weight_sum + jnp.stack(terms, axis=1)
        hidden_grad = hidden_grad.reshape(CH, FRAMES, ROWS, WID)
        sigmoid_pre = jax.nn.sigmoid(preact)
        preact_grad = hidden_grad * sigmoid_pre * (1.0 + preact * (1.0 - sigmoid_pre))
        gain_sum = gain_sum + lax.optimization_barrier(jnp.sum(preact_grad * normed, axis=(1, 2, 3)))
        norm_grad = preact_grad * gain_cols
        projection = lax.optimization_barrier(jnp.mean(norm_grad * normed, axis=0, keepdims=True))
        input_grad = inverse * (norm_grad - normed * projection) + cotangent.astype(jnp.float32)
        results.append(input_grad.astype(jnp.bfloat16))
    grad_scale = 1.0 / math.sqrt(ALLVOX)
    return (jnp.stack(results, axis=0), weight_sum * grad_scale, gain_sum * grad_scale)
```

```python
import math

import jax
import jax.numpy as jnp
from jax import lax
from jax.experimental import pallas as pl
from jax.experimental.pallas import tpu as pltpu
from jax.sharding import PartitionSpec as P

EPSILON = 1e-06
BF = jnp.bfloat16
F32 = jnp.float32
COLS = 128
PIECES = 32
MAIN = 5184


def call(body, outs, *args, scratch=(), limit=40):
    outs = [jax.ShapeDtypeStruct(s, d) for s, d in outs]
    spec = pl.BlockSpec(memory_space=pltpu.VMEM)
    return pl.pallas_call(
        body,
        out_shape=outs,
        in_specs=[spec] * len(args),
        out_specs=[spec] * len(outs),
        scratch_shapes=list(scratch),
        compiler_params=pltpu.CompilerParams(vmem_limit_bytes=limit << 20),
    )(*args)


def swap_kernel(major, minor, src, out):
    n = major * minor
    to = lax.broadcasted_iota(jnp.int32, (n, n), 0)
    at = lax.broadcasted_iota(jnp.int32, (n, n), 1)
    pick = (at == (to % major) * minor + to // major).astype(F32).astype(BF)
    width = src.shape[1]
    for lo in range(0, width, 512):
        part = jnp.dot(pick, src[:, lo : lo + 512], preferred_element_type=F32)
        out[:, lo : lo + 512] = part.astype(BF)


def swap_rows(x, major, minor):
    def body(src, out):
        swap_kernel(major, minor, src, out)

    return call(body, [(x.shape, BF)], x)[0]


def sideways(x, by):
    lanes = lax.broadcasted_iota(jnp.int32, (x.shape[0], COLS), 1)
    edge = 0 if by == 1 else COLS - 1
    parts = []
    for lo in range(0, x.shape[1], COLS):
        turned = pltpu.roll(x[:, lo : lo + COLS], by % COLS, 1)
        parts.append(jnp.where(lanes == edge, 0.0, turned))
    return jnp.concatenate(parts, axis=1)


def unpack_body(n_tm, n_rows, capacity, arrived, lengths, cot3, to_tm, top, bot, dtop, dbot, turned):
    owners = n_tm * n_rows
    channels = arrived.shape[1] // capacity
    row = lax.broadcasted_iota(jnp.int32, (owners, owners), 0)
    col = lax.broadcasted_iota(jnp.int32, (owners, owners), 1)
    owner = (row % n_tm) * n_rows + row // n_tm
    held = jnp.broadcast_to(lengths[...], (owners, owners)).astype(F32)
    begins = jnp.sum(jnp.where(col < owner, held, 0.0), axis=1, keepdims=True)
    count = jnp.sum(jnp.where(col == owner, held, 0.0), axis=1, keepdims=True)
    for lo in range(0, arrived.shape[1], COLS):
        turned[lo : lo + COLS, :] = arrived[:, lo : lo + COLS].astype(F32).T.astype(BF)
    for f in range(3):
        voxel = lax.broadcasted_iota(jnp.int32, (owners, 512), 1).astype(F32) + float(f * 512)
        slot = voxel - begins
        slot = jnp.where((slot >= 0.0) & (slot < count), slot, -1.0).astype(BF)
        total = jnp.zeros((channels, 512), F32)
        for k in range(0, capacity, 8):
            left = jnp.concatenate(
                [turned[(k + i) * channels : (k + i + 1) * channels, :] for i in range(8)], axis=1
            )
            right = jnp.concatenate(
                [jnp.where(slot == jnp.asarray(k + i, BF), jnp.asarray(1, BF), jnp.asarray(0, BF)) for i in range(8)],
                axis=0,
            )
            total += jnp.dot(left, right, preferred_element_type=F32)
        lo = f * 512
        cot = total.astype(BF)
        cot3[0:channels, lo : lo + 512] = sideways(total, -1).astype(BF)
        cot3[channels : 2 * channels, lo : lo + 512] = cot
        cot3[2 * channels : 3 * channels, lo : lo + 512] = sideways(total, 1).astype(BF)
        top[:, f * COLS : (f + 1) * COLS] = cot[:, 0:COLS]
        bot[:, f * COLS : (f + 1) * COLS] = cot[:, 3 * COLS : 4 * COLS]
        if f < 2:
            to_tm[:, lo : lo + 512] = cot
            dtop[:, f * COLS : (f + 1) * COLS] = cot[:, 0:COLS]
            dbot[:, f * COLS : (f + 1) * COLS] = cot[:, 3 * COLS : 4 * COLS]


def unpack(arrived, lengths, n_tm, n_rows, capacity):
    channels = arrived.shape[1] // capacity

    def body(*refs):
        unpack_body(n_tm, n_rows, capacity, *refs)

    outs = [(3 * channels, 1536), (channels, 1024), (channels, 384), (channels, 384)]
    outs += [(channels, 256), (channels, 256)]
    return call(
        body,
        [(s, BF) for s in outs],
        arrived,
        lengths,
        scratch=[pltpu.VMEM((arrived.shape[1], arrived.shape[0]), BF)],
    )


def hidden_kernel(own, by_tm, top, bot, dtop, dbot, gain, out):
    for fe in range(5):
        if fe < 2:
            mid = by_tm[:, fe * 512 : (fe + 1) * 512]
            above = dtop[:, fe * COLS : (fe + 1) * COLS]
            below = dbot[:, fe * COLS : (fe + 1) * COLS]
        else:
            f = fe - 2
            mid = own[:, f * 512 : (f + 1) * 512]
            above = top[:, f * COLS : (f + 1) * COLS]
            below = bot[:, f * COLS : (f + 1) * COLS]
        x = jnp.concatenate([above, mid, below], axis=1).astype(F32)
        inverse = lax.rsqrt(jnp.mean(x * x, axis=0, keepdims=True) + EPSILON)
        preact = x * inverse * gain[...]
        hidden = preact * jax.nn.sigmoid(preact)
        wide = jnp.concatenate([hidden, jnp.zeros((64, 768), F32)], axis=0)
        out[fe * 768 : (fe + 1) * 768, :] = wide.T[:, :192].astype(BF)


def weight_kernel(cot3, hid, out):
    held = None
    for ab in range(9):
        a, b = divmod(ab, 3)
        right = jnp.concatenate(
            [hid[((f + a) * 6 + b) * COLS : ((f + a) * 6 + b + 4) * COLS, :] for f in range(3)], axis=0
        )
        part = jnp.dot(cot3[...], right, preferred_element_type=F32).astype(BF)
        out[ab * 576 : (ab + 1) * 576, :] = part[:, :COLS]
        rest = part[:, COLS:192]
        if ab == 8:
            out[MAIN + 4 * 576 : MAIN + 4 * 576 + 288, :] = jnp.concatenate([rest[:288], rest[288:]], axis=1)
        elif ab % 2:
            at = MAIN + (ab // 2) * 576
            out[at : at + 576, :] = jnp.concatenate([held, rest], axis=1)
        else:
            held = rest
    done = MAIN + MAIN // 2
    out[done:, :] = jnp.zeros((out.shape[0] - done, COLS), BF)


def input_kernel(own, gain, cot3, by_tm, top, bot, dtop, dbot, weights, out, gain_out, ext, rhs):
    for fe in range(5):
        lo = fe * 768
        if fe < 3:
            ext[:, lo : lo + COLS] = top[:, fe * COLS : (fe + 1) * COLS]
            ext[:, lo + COLS : lo + 5 * COLS] = cot3[192:384, fe * 512 : (fe + 1) * 512]
            ext[:, lo + 5 * COLS : lo + 6 * COLS] = bot[:, fe * COLS : (fe + 1) * COLS]
        else:
            f = fe - 3
            ext[:, lo : lo + COLS] = dtop[:, f * COLS : (f + 1) * COLS]
            ext[:, lo + COLS : lo + 5 * COLS] = by_tm[:, f * 512 : (f + 1) * 512]
            ext[:, lo + 5 * COLS : lo + 6 * COLS] = dbot[:, f * COLS : (f + 1) * COLS]
    gain_sum = jnp.zeros((192, COLS), F32)
    rhs[1728:, :] = jnp.zeros((64, 512), BF)
    for f in range(3):
        for ab in range(9):
            a, b = divmod(ab, 3)
            lo = ((f + a) * 6 + b) * COLS
            rhs[ab * 192 : (ab + 1) * 192, :] = ext[:, lo : lo + 512]
        spread = jnp.dot(weights[...], rhs[...], preferred_element_type=F32)
        grad = sideways(spread[0:192], 1) + spread[192:384] + sideways(spread[384:576], -1)
        x = own[:, f * 512 : (f + 1) * 512].astype(F32)
        inverse = lax.rsqrt(jnp.mean(x * x, axis=0, keepdims=True) + EPSILON)
        normed = x * inverse
        preact = normed * gain[...]
        s = jax.nn.sigmoid(preact)
        preact_grad = grad * s * (1.0 + preact * (1.0 - s))
        term = preact_grad * normed
        for lo in range(0, 512, COLS):
            gain_sum += term[:, lo : lo + COLS]
        projection = jnp.mean(term * gain[...], axis=0, keepdims=True)
        cot = cot3[192:384, f * 512 : (f + 1) * 512].astype(F32)
        result = inverse * (preact_grad * gain[...] - normed * projection) + cot
        out[:, f * 512 : (f + 1) * 512] = result.astype(BF)
    totals = jnp.broadcast_to(jnp.sum(gain_sum, axis=1, keepdims=True), (192, COLS))
    line = jnp.concatenate([totals, jnp.zeros((64, COLS), F32)], axis=0).T[0:1, :]
    high = line.astype(BF).astype(F32)
    low = line - high
    at = lax.broadcasted_iota(jnp.int32, (16, COLS), 0)
    block = jnp.zeros((16, COLS), F32)
    for i, piece in enumerate((high[:, :COLS], high[:, COLS:], low[:, :COLS], low[:, COLS:])):
        block = jnp.where(at == i, piece, block)
    gain_out[...] = block.astype(BF)


def final_kernel(half, scale, buf, out):
    for tap in range(27):
        ab, q = divmod(tap, 3)
        main = buf[tap * 192 : (tap + 1) * 192, :].astype(F32)
        if ab < 8:
            at = MAIN + (ab // 2) * 576 + q * 192
            side = buf[at : at + 192, :].astype(F32)
            side = side[:, 64 * (ab % 2) : 64 * (ab % 2) + 64]
        else:
            at = MAIN + 4 * 576
            first, second = buf[at : at + 288, 0:64].astype(F32), buf[at : at + 288, 64:128].astype(F32)
            if q == 0:
                side = first[0:192]
            elif q == 1:
                side = jnp.concatenate([first[192:288], second[0:96]], axis=0)
            else:
                side = second[96:288]
        out[tap, :, :] = jnp.concatenate([main, side], axis=1) * scale


def shifted(shard, tm_by, rows_by):
    n_tm, n_rows = lax.axis_size("tm"), lax.axis_size("rows")
    if rows_by == 0:
        return lax.ppermute(shard, "tm", [(i, i + tm_by) for i in range(n_tm) if 0 <= i + tm_by < n_tm])
    if tm_by == 0:
        return lax.ppermute(shard, "rows", [(j, j + rows_by) for j in range(n_rows) if 0 <= j + rows_by < n_rows])
    pairs = [
        (i * n_rows + j, (i + tm_by) * n_rows + j + rows_by)
        for i in range(n_tm)
        for j in range(n_rows)
        if 0 <= i + tm_by < n_tm and 0 <= j + rows_by < n_rows
    ]
    return lax.ppermute(shard, ("tm", "rows"), pairs)


def exchange(x, axis):
    return lax.all_to_all(x, axis, split_axis=0, concat_axis=0, tiled=True)


def shards(activations, norm_gain, conv_weights, packed_grads, piece_lengths):
    n_tm, n_rows, n_clip = lax.axis_size("tm"), lax.axis_size("rows"), lax.axis_size("clip")
    channels, frames, row_count, col_count = activations.shape[1:]
    voxels = frames * row_count * col_count
    owners = piece_lengths.shape[2]
    width = packed_grads.shape[3]
    capacity = width // channels
    grad_scale = 1.0 / math.sqrt(voxels * n_tm * n_rows * n_clip)
    gain_col = norm_gain[:, None]

    packed = packed_grads.reshape(owners, width)
    first = exchange(packed.reshape(n_tm, n_rows, width), "tm").reshape(owners, width)
    second = exchange(swap_rows(first, n_tm, n_rows).reshape(n_rows, n_tm, width), "rows")
    arrived = second.reshape(owners, width)

    own = activations.reshape(channels, voxels)
    own4 = own.reshape(channels, frames, row_count * col_count)
    last_two = own4[:, 1:].reshape(channels, 2 * row_count * col_count)
    first_row = own4[:, :, :col_count]
    last_row = own4[:, :, 3 * col_count :]
    act_tm = shifted(last_two, 1, 0)
    act_top = shifted(last_row.reshape(channels, 384), 0, 1)
    act_bot = shifted(first_row.reshape(channels, 384), 0, -1)
    act_dtop = shifted(last_row[:, 1:].reshape(channels, 256), 1, 1)
    act_dbot = shifted(first_row[:, 1:].reshape(channels, 256), 1, -1)
    hid = call(
        hidden_kernel, [((30 * COLS, channels), BF)], own, act_tm, act_top, act_bot, act_dtop, act_dbot, gain_col
    )[0]
    weights = jnp.flip(conv_weights, 1).reshape(channels, 9, 3, channels).transpose(2, 3, 1, 0)
    weights = jnp.pad(weights.reshape(3 * channels, 9 * channels), ((0, 0), (0, 64)))

    cot3, s_tm, s_top, s_bot, s_dtop, s_dbot = unpack(
        arrived, piece_lengths.reshape(1, owners), n_tm, n_rows, capacity
    )
    cot_tm = shifted(s_tm, -1, 0)
    cot_bot = shifted(s_top, 0, -1)
    cot_top = shifted(s_bot, 0, 1)
    cot_dbot = shifted(s_dtop, -1, -1)
    cot_dtop = shifted(s_dbot, -1, 1)

    buf = call(weight_kernel, [((8192, COLS), BF)], cot3, hid)[0]
    got = exchange(buf.reshape(n_clip, 8192 // n_clip, COLS), "clip")
    part = jnp.sum(got.astype(F32), axis=0).astype(BF)
    got = exchange(part.reshape(n_tm, part.shape[0] // n_tm, COLS), "tm")
    part = jnp.sum(got.astype(F32), axis=0).astype(BF)

    input_grad, gain_part = call(
        input_kernel,
        [((channels, voxels), BF), ((16, COLS), BF)],
        own,
        gain_col,
        cot3,
        cot_tm,
        cot_top,
        cot_bot,
        cot_dtop,
        cot_dbot,
        weights,
        scratch=[pltpu.VMEM((channels, 30 * COLS), BF), pltpu.VMEM((1792, 512), BF)],
    )

    def split(total):
        high = total.astype(BF)
        low = (total - high.astype(F32)).astype(BF)
        return jnp.concatenate([high, low, jnp.zeros((12, COLS), BF)], axis=0)

    share = part.shape[0]
    sent = jnp.concatenate([part, gain_part], axis=0)
    got = exchange(jnp.broadcast_to(sent[None], (n_rows, *sent.shape)), "rows")
    total = jnp.sum(got.astype(F32), axis=0)
    gain_total = total[share : share + 2] + total[share + 2 : share + 4]
    sent = jnp.concatenate([total[:share].astype(BF), split(gain_total)], axis=0)
    got = exchange(jnp.broadcast_to(sent[None], (n_tm, *sent.shape)), "tm")
    gains = jnp.sum(got[:, share:].astype(F32), axis=0)
    half = got[:, :share].reshape(n_tm * share, COLS)
    sent = jnp.concatenate([half, split(gains[0:2] + gains[2:4])], axis=0)
    got = exchange(jnp.broadcast_to(sent[None], (n_clip, *sent.shape)), "clip")
    gains = jnp.sum(got[:, n_tm * share :].astype(F32), axis=0)
    gain_grad = (gains[0:2] + gains[2:4]).reshape(2 * COLS)[:channels] * grad_scale
    whole = got[:, : n_tm * share].reshape(8192, COLS)

    def finish(src, out):
        final_kernel(None, grad_scale, src, out)

    weight_grad = call(finish, [((27, channels, channels), F32)], whole)[0].transpose(1, 0, 2)
    return (input_grad.reshape(activations.shape), weight_grad, gain_grad)


def solution(mesh):
    return jax.shard_map(
        shards,
        mesh=mesh,
        in_specs=(
            P("clip", None, "tm", "rows", None),
            P(),
            P(),
            P("clip", ("tm", "rows"), None, None),
            P("clip", ("tm", "rows"), None),
        ),
        out_specs=(P("clip", None, "tm", "rows", None), P(), P()),
        check_vma=False,
    )
```

```python
import math

import jax
import jax.numpy as jnp
from jax import lax
from jax.experimental import pallas as pl
from jax.experimental.pallas import tpu as pltpu
from jax.sharding import PartitionSpec as P

EPSILON = 1e-06
BF = jnp.bfloat16
F32 = jnp.float32
COLS = 128
MAIN = 5184


def call(body, outs, *args, scratch=(), limit=16):
    outs = [jax.ShapeDtypeStruct(s, d) for s, d in outs]
    spec = pl.BlockSpec(memory_space=pltpu.VMEM)
    return pl.pallas_call(
        body,
        out_shape=outs,
        in_specs=[spec] * len(args),
        out_specs=[spec] * len(outs),
        scratch_shapes=list(scratch),
        compiler_params=pltpu.CompilerParams(vmem_limit_bytes=limit << 20),
    )(*args)


def swap_kernel(major, minor, src, out):
    n = major * minor
    to = lax.broadcasted_iota(jnp.int32, (n, n), 0)
    at = lax.broadcasted_iota(jnp.int32, (n, n), 1)
    pick = (at == (to % major) * minor + to // major).astype(F32).astype(BF)
    width = src.shape[1]
    for lo in range(0, width, 512):
        part = jnp.dot(pick, src[:, lo : lo + 512], preferred_element_type=F32)
        out[:, lo : lo + 512] = part.astype(BF)


def swap_rows(x, major, minor):
    def body(src, out):
        swap_kernel(major, minor, src, out)

    return call(body, [(x.shape, BF)], x)[0]


def sideways(x, by):
    lanes = lax.broadcasted_iota(jnp.int32, (x.shape[0], COLS), 1)
    edge = 0 if by == 1 else COLS - 1
    parts = []
    for lo in range(0, x.shape[1], COLS):
        turned = pltpu.roll(x[:, lo : lo + COLS], by % COLS, 1)
        parts.append(jnp.where(lanes == edge, 0.0, turned))
    return jnp.concatenate(parts, axis=1)


def place(lengths, owner):
    owners = owner.shape[0]
    other = lax.broadcasted_iota(jnp.int32, (owners, owners), 1)
    held = jnp.broadcast_to(lengths[...], (owners, owners)).astype(F32)
    begins = jnp.sum(jnp.where(other < owner, held, 0.0), axis=1, keepdims=True)
    count = jnp.sum(jnp.where(other == owner, held, 0.0), axis=1, keepdims=True)
    return begins, count


def unpack_body(n_tm, n_rows, capacity, one, lengths, cot3, to_tm, top, bot, dtop, dbot, turned):
    owners = n_tm * n_rows
    width = one.shape[1]
    channels = width // capacity
    row = lax.broadcasted_iota(jnp.int32, (owners, owners), 0)
    begins, count = place(lengths, (row % n_tm) * n_rows + row // n_tm)
    for lo in range(0, width, COLS):
        turned[lo : lo + COLS, :] = one[:, lo : lo + COLS].astype(F32).T.astype(BF)
    group = capacity // 3
    for f in range(3):
        voxel = lax.broadcasted_iota(jnp.int32, (owners, 512), 1).astype(F32) + float(f * 512)
        slot = voxel - begins
        slot = jnp.where((slot >= 0.0) & (slot < count), slot, -1.0).astype(BF)
        total = jnp.zeros((channels, 512), F32)
        for k in range(0, capacity, group):
            left = jnp.concatenate(
                [turned[(k + i) * channels : (k + i + 1) * channels, :] for i in range(group)], axis=1
            )
            right = jnp.concatenate(
                [jnp.where(slot == jnp.asarray(k + i, BF), jnp.asarray(1, BF), jnp.asarray(0, BF)) for i in range(group)],
                axis=0,
            )
            total += jnp.dot(left, right, preferred_element_type=F32)
        lo = f * 512
        cot = total.astype(BF)
        cot3[0:channels, lo : lo + 512] = sideways(total, -1).astype(BF)
        cot3[channels : 2 * channels, lo : lo + 512] = cot
        cot3[2 * channels : 3 * channels, lo : lo + 512] = sideways(total, 1).astype(BF)
        top[:, f * COLS : (f + 1) * COLS] = cot[:, 0:COLS]
        bot[:, f * COLS : (f + 1) * COLS] = cot[:, 3 * COLS : 4 * COLS]
        if f < 2:
            to_tm[:, lo : lo + 512] = cot
            dtop[:, f * COLS : (f + 1) * COLS] = cot[:, 0:COLS]
            dbot[:, f * COLS : (f + 1) * COLS] = cot[:, 3 * COLS : 4 * COLS]


def unpack(one, lengths, n_tm, n_rows, capacity):
    channels = one.shape[1] // capacity

    def body(*refs):
        unpack_body(n_tm, n_rows, capacity, *refs)

    outs = [(3 * channels, 1536), (channels, 1024), (channels, 384), (channels, 384)]
    outs += [(channels, 256), (channels, 256)]
    return call(
        body,
        [(s, BF) for s in outs],
        one,
        lengths,
        scratch=[pltpu.VMEM((one.shape[1], one.shape[0]), BF)],
    )


def edges_kernel(own, to_tm, top, bot, dtop, dbot):
    to_tm[...] = own[:, 512:]
    for f in range(3):
        first = own[:, f * 512 : f * 512 + COLS]
        last = own[:, f * 512 + 3 * COLS : (f + 1) * 512]
        top[:, f * COLS : (f + 1) * COLS] = first
        bot[:, f * COLS : (f + 1) * COLS] = last
        if f:
            dtop[:, (f - 1) * COLS : f * COLS] = first
            dbot[:, (f - 1) * COLS : f * COLS] = last


def turn_weights_kernel(src, out):
    def turned(tap):
        wide = jnp.concatenate([src[26 - tap].astype(F32), jnp.zeros((64, 192), F32)], axis=0)
        wide = jnp.concatenate([wide, jnp.zeros((256, 64), F32)], axis=1).T
        return wide[:192, :192].astype(BF)

    for q in range(3):
        for ab in range(0, 9, 2):
            left = turned(ab * 3 + q)
            right = turned((ab + 1) * 3 + q) if ab < 8 else jnp.zeros((192, 64), BF)
            pair = jnp.concatenate([left, right], axis=1)
            out[q * 192 : (q + 1) * 192, ab * 192 : ab * 192 + pair.shape[1]] = pair


def add_kernel(got, out):
    out[...] = (got[0].astype(F32) + got[1].astype(F32)).astype(BF)


def share_kernel(got, gain_part, out):
    n, share = got.shape[0], got.shape[1]
    total = got[0].astype(F32)
    for i in range(1, n):
        total += got[i].astype(F32)
    total = total.astype(BF)
    for i in range(out.shape[0]):
        out[i, :share, :] = total
        out[i, share:, :] = gain_part[...]


def gain_of(total):
    return total[0:2] + total[2:4]


def gather_kernel(got, out):
    share = got.shape[1] - 16
    total = got[0].astype(F32)
    for i in range(1, got.shape[0]):
        total += got[i].astype(F32)
    weight = total[:share].astype(BF)
    line = gain_of(total[share:])
    high = line.astype(BF).astype(F32)
    block = jnp.concatenate([high, line - high, jnp.zeros((12, COLS), F32)], axis=0).astype(BF)
    for i in range(out.shape[0]):
        out[i, :share, :] = weight
        out[i, share:, :] = block


def hidden_kernel(own, by_tm, top, bot, dtop, dbot, gain, out):
    for fe in range(5):
        if fe < 2:
            mid = by_tm[:, fe * 512 : (fe + 1) * 512]
            above = dtop[:, fe * COLS : (fe + 1) * COLS]
            below = dbot[:, fe * COLS : (fe + 1) * COLS]
        else:
            f = fe - 2
            mid = own[:, f * 512 : (f + 1) * 512]
            above = top[:, f * COLS : (f + 1) * COLS]
            below = bot[:, f * COLS : (f + 1) * COLS]
        x = jnp.concatenate([above, mid, below], axis=1).astype(F32)
        inverse = lax.rsqrt(jnp.mean(x * x, axis=0, keepdims=True) + EPSILON)
        preact = x * inverse * gain[...]
        hidden = preact * jax.nn.sigmoid(preact)
        wide = jnp.concatenate([hidden, jnp.zeros((64, 768), F32)], axis=0)
        out[fe * 768 : (fe + 1) * 768, :] = wide.T[:, :192].astype(BF)


def weight_kernel(cot3, hid, out):
    held = None
    for ab in range(9):
        a, b = divmod(ab, 3)
        right = jnp.concatenate(
            [hid[((f + a) * 6 + b) * COLS : ((f + a) * 6 + b + 4) * COLS, :] for f in range(3)], axis=0
        )
        part = jnp.dot(cot3[...], right, preferred_element_type=F32).astype(BF)
        out[ab * 576 : (ab + 1) * 576, :] = part[:, :COLS]
        rest = part[:, COLS:192]
        if ab == 8:
            out[MAIN + 4 * 576 : MAIN + 4 * 576 + 288, :] = jnp.concatenate([rest[:288], rest[288:]], axis=1)
        elif ab % 2:
            at = MAIN + (ab // 2) * 576
            out[at : at + 576, :] = jnp.concatenate([held, rest], axis=1)
        else:
            held = rest
    done = MAIN + MAIN // 2
    out[done:, :] = jnp.zeros((out.shape[0] - done, COLS), BF)


def input_kernel(own, gain, cot3, by_tm, top, bot, dtop, dbot, weights, out, gain_out, ext, rhs):
    for fe in range(5):
        lo = fe * 768
        if fe < 3:
            ext[:, lo : lo + COLS] = top[:, fe * COLS : (fe + 1) * COLS]
            ext[:, lo + COLS : lo + 5 * COLS] = cot3[192:384, fe * 512 : (fe + 1) * 512]
            ext[:, lo + 5 * COLS : lo + 6 * COLS] = bot[:, fe * COLS : (fe + 1) * COLS]
        else:
            f = fe - 3
            ext[:, lo : lo + COLS] = dtop[:, f * COLS : (f + 1) * COLS]
            ext[:, lo + COLS : lo + 5 * COLS] = by_tm[:, f * 512 : (f + 1) * 512]
            ext[:, lo + 5 * COLS : lo + 6 * COLS] = dbot[:, f * COLS : (f + 1) * COLS]
    gain_sum = jnp.zeros((192, COLS), F32)
    rhs[1728:, :] = jnp.zeros((64, 512), BF)
    for f in range(3):
        for ab in range(9):
            a, b = divmod(ab, 3)
            lo = ((f + a) * 6 + b) * COLS
            rhs[ab * 192 : (ab + 1) * 192, :] = ext[:, lo : lo + 512]
        spread = jnp.dot(weights[...], rhs[...], preferred_element_type=F32)
        grad = sideways(spread[0:192], 1) + spread[192:384] + sideways(spread[384:576], -1)
        x = own[:, f * 512 : (f + 1) * 512].astype(F32)
        inverse = lax.rsqrt(jnp.mean(x * x, axis=0, keepdims=True) + EPSILON)
        normed = x * inverse
        preact = normed * gain[...]
        s = jax.nn.sigmoid(preact)
        preact_grad = grad * s * (1.0 + preact * (1.0 - s))
        term = preact_grad * normed
        for lo in range(0, 512, COLS):
            gain_sum += term[:, lo : lo + COLS]
        projection = jnp.mean(term * gain[...], axis=0, keepdims=True)
        cot = cot3[192:384, f * 512 : (f + 1) * 512].astype(F32)
        result = inverse * (preact_grad * gain[...] - normed * projection) + cot
        out[:, f * 512 : (f + 1) * 512] = result.astype(BF)
    totals = jnp.broadcast_to(jnp.sum(gain_sum, axis=1, keepdims=True), (192, COLS))
    line = jnp.concatenate([totals, jnp.zeros((64, COLS), F32)], axis=0).T[0:1, :]
    high = line.astype(BF).astype(F32)
    low = line - high
    at = lax.broadcasted_iota(jnp.int32, (16, COLS), 0)
    block = jnp.zeros((16, COLS), F32)
    for i, piece in enumerate((high[:, :COLS], high[:, COLS:], low[:, :COLS], low[:, COLS:])):
        block = jnp.where(at == i, piece, block)
    gain_out[...] = block.astype(BF)


def final_kernel(scale, clip, mine, other, out, gain_out, buf):
    n, share = mine.shape[0], mine.shape[1] - 16
    at = clip[0]
    gains = jnp.zeros((2, COLS), F32)
    for held, half in ((mine, at), (other, 1 - at)):
        for i in range(n):
            rows = pl.ds(pl.multiple_of(half * (n * share) + i * share, share), share)
            buf[rows, :] = held[i, :share, :]
            gains += gain_of(held[i, share:, :].astype(F32))
    gain_out[...] = gains * scale
    for tap in range(27):
        ab, q = divmod(tap, 3)
        main = buf[tap * 192 : (tap + 1) * 192, :].astype(F32)
        if ab < 8:
            row = MAIN + (ab // 2) * 576 + q * 192
            side = buf[row : row + 192, :].astype(F32)
            side = side[:, 64 * (ab % 2) : 64 * (ab % 2) + 64]
        else:
            row = MAIN + 4 * 576
            first, second = buf[row : row + 288, 0:64].astype(F32), buf[row : row + 288, 64:128].astype(F32)
            if q == 0:
                side = first[0:192]
            elif q == 1:
                side = jnp.concatenate([first[192:288], second[0:96]], axis=0)
            else:
                side = second[96:288]
        out[tap, :, :] = jnp.concatenate([main, side], axis=1) * scale


def shifted(shard, tm_by, rows_by):
    n_tm, n_rows = lax.axis_size("tm"), lax.axis_size("rows")
    if rows_by == 0:
        return lax.ppermute(shard, "tm", [(i, i + tm_by) for i in range(n_tm) if 0 <= i + tm_by < n_tm])
    if tm_by == 0:
        return lax.ppermute(shard, "rows", [(j, j + rows_by) for j in range(n_rows) if 0 <= j + rows_by < n_rows])
    pairs = [
        (i * n_rows + j, (i + tm_by) * n_rows + j + rows_by)
        for i in range(n_tm)
        for j in range(n_rows)
        if 0 <= i + tm_by < n_tm and 0 <= j + rows_by < n_rows
    ]
    return lax.ppermute(shard, ("tm", "rows"), pairs)


def exchange(x, axis):
    return lax.all_to_all(x, axis, split_axis=0, concat_axis=0, tiled=True)


def shards(activations, norm_gain, conv_weights, packed_grads, piece_lengths):
    n_tm, n_rows, n_clip = lax.axis_size("tm"), lax.axis_size("rows"), lax.axis_size("clip")
    channels, frames, row_count, col_count = activations.shape[1:]
    voxels = frames * row_count * col_count
    owners = piece_lengths.shape[2]
    width = packed_grads.shape[3]
    capacity = width // channels
    grad_scale = 1.0 / math.sqrt(voxels * n_tm * n_rows * n_clip)
    gain_col = norm_gain[:, None]

    packed = packed_grads.reshape(owners, width)
    own = activations.reshape(channels, voxels)
    edge = [(channels, 1024), (channels, 384), (channels, 384), (channels, 256), (channels, 256)]
    a_tm, a_top, a_bot, a_dtop, a_dbot = call(edges_kernel, [(s, BF) for s in edge], own)
    act_tm = shifted(a_tm, 1, 0)
    act_bot = shifted(a_top, 0, -1)
    act_top = shifted(a_bot, 0, 1)
    act_dbot = shifted(a_dtop, 1, -1)
    act_dtop = shifted(a_dbot, 1, 1)

    first = exchange(packed.reshape(n_tm, n_rows, width), "tm").reshape(owners, width)
    first, act_tm, act_top, act_bot, act_dtop, act_dbot = lax.optimization_barrier(
        (first, act_tm, act_top, act_bot, act_dtop, act_dbot)
    )
    arrived = exchange(swap_rows(first, n_tm, n_rows).reshape(n_rows, n_tm, width), "rows").reshape(owners, width)

    hid = call(
        hidden_kernel, [((30 * COLS, channels), BF)], own, act_tm, act_top, act_bot, act_dtop, act_dbot, gain_col
    )[0]
    weights = call(turn_weights_kernel, [((576, 1792), BF)], conv_weights.transpose(1, 0, 2))[0]
    arrived, hid, weights = lax.optimization_barrier((arrived, hid, weights))

    cot3, s_tm, s_top, s_bot, s_dtop, s_dbot = unpack(
        arrived, piece_lengths.reshape(1, owners), n_tm, n_rows, capacity
    )
    cot_tm = shifted(s_tm, -1, 0)
    cot_bot = shifted(s_top, 0, -1)
    cot_top = shifted(s_bot, 0, 1)
    cot_dbot = shifted(s_dtop, -1, -1)
    cot_dtop = shifted(s_dbot, -1, 1)

    buf = call(weight_kernel, [((8192, COLS), BF)], cot3, hid)[0]
    got = exchange(buf.reshape(n_clip, 8192 // n_clip, COLS), "clip")
    part = call(add_kernel, [((8192 // n_clip, COLS), BF)], got)[0]
    share = part.shape[0] // n_tm
    got = exchange(part.reshape(n_tm, share, COLS), "tm")

    input_grad, gain_part = call(
        input_kernel,
        [((channels, voxels), BF), ((16, COLS), BF)],
        own,
        gain_col,
        cot3,
        cot_tm,
        cot_top,
        cot_bot,
        cot_dtop,
        cot_dbot,
        weights,
        scratch=[pltpu.VMEM((channels, 30 * COLS), BF), pltpu.VMEM((1792, 512), BF)],
    )

    sent = call(share_kernel, [((n_rows, share + 16, COLS), BF)], got, gain_part)[0]
    sent = call(gather_kernel, [((n_tm, share + 16, COLS), BF)], exchange(sent, "rows"))[0]
    mine = exchange(sent, "tm")
    other = lax.ppermute(mine, "clip", [(0, 1), (1, 0)])

    def finish(*refs):
        final_kernel(grad_scale, *refs)

    vmem = pl.BlockSpec(memory_space=pltpu.VMEM)
    weight_grad, gain_grad = pl.pallas_call(
        finish,
        out_shape=[
            jax.ShapeDtypeStruct((27, channels, channels), F32),
            jax.ShapeDtypeStruct((2, COLS), F32),
        ],
        in_specs=[pl.BlockSpec(memory_space=pltpu.SMEM), vmem, vmem],
        out_specs=[vmem, vmem],
        scratch_shapes=[pltpu.VMEM((8192, COLS), BF)],
        compiler_params=pltpu.CompilerParams(vmem_limit_bytes=16 << 20),
    )(lax.axis_index("clip").astype(jnp.int32).reshape(1), mine, other)
    gain_grad = gain_grad.reshape(2 * COLS)[:channels]
    return (input_grad.reshape(activations.shape), weight_grad.transpose(1, 0, 2), gain_grad)


def solution(mesh):
    return jax.shard_map(
        shards,
        mesh=mesh,
        in_specs=(
            P("clip", None, "tm", "rows", None),
            P(),
            P(),
            P("clip", ("tm", "rows"), None, None),
            P("clip", ("tm", "rows"), None),
        ),
        out_specs=(P("clip", None, "tm", "rows", None), P(), P()),
        check_vma=False,
    )
```

```python
import math

import jax
import jax.numpy as jnp
from jax import lax
from jax.experimental import pallas as pl
from jax.experimental.pallas import tpu as pltpu
from jax.sharding import PartitionSpec as P

EPSILON = 1e-06
BF = jnp.bfloat16
F32 = jnp.float32
COLS = 128
MAIN = 5184


def call(body, outs, *args, scratch=(), after=()):
    outs = [jax.ShapeDtypeStruct(s, d) for s, d in outs]
    spec = pl.BlockSpec(memory_space=pltpu.VMEM)

    def after_them(*refs):
        body(*refs[len(after) :])

    return pl.pallas_call(
        after_them,
        out_shape=outs,
        in_specs=[pl.BlockSpec(memory_space=pl.ANY)] * len(after)
        + [pl.BlockSpec(memory_space=pltpu.SMEM) if a.ndim == 1 else spec for a in args],
        out_specs=[spec] * len(outs),
        scratch_shapes=list(scratch),
        compiler_params=pltpu.CompilerParams(vmem_limit_bytes=16 << 20),
    )(*after, *args)


def swap_kernel(major, minor, src, out):
    n = major * minor
    to = lax.broadcasted_iota(jnp.int32, (n, n), 0)
    at = lax.broadcasted_iota(jnp.int32, (n, n), 1)
    pick = (at == (to % major) * minor + to // major).astype(F32).astype(BF)
    width = src.shape[1]
    for lo in range(0, width, 512):
        part = jnp.dot(pick, src[:, lo : lo + 512], preferred_element_type=F32)
        out[:, lo : lo + 512] = part.astype(BF)


def swap_rows(x, major, minor, after):
    def body(src, out):
        swap_kernel(major, minor, src, out)

    return call(body, [(x.shape, BF)], x, after=after)[0]


def sideways(x, by):
    lanes = lax.broadcasted_iota(jnp.int32, (x.shape[0], COLS), 1)
    edge = 0 if by == 1 else COLS - 1
    parts = []
    for lo in range(0, x.shape[1], COLS):
        turned = pltpu.roll(x[:, lo : lo + COLS], by % COLS, 1)
        parts.append(jnp.where(lanes == edge, 0.0, turned))
    return jnp.concatenate(parts, axis=1)


def place(lengths, owner):
    owners = owner.shape[0]
    other = lax.broadcasted_iota(jnp.int32, (owners, owners), 1)
    held = jnp.broadcast_to(lengths[...], (owners, owners)).astype(F32)
    begins = jnp.sum(jnp.where(other < owner, held, 0.0), axis=1, keepdims=True)
    count = jnp.sum(jnp.where(other == owner, held, 0.0), axis=1, keepdims=True)
    return begins, count


def unpack_body(n_tm, n_rows, capacity, one, lengths, cot3, to_tm, turned):
    owners = n_tm * n_rows
    width = one.shape[1]
    channels = width // capacity
    row = lax.broadcasted_iota(jnp.int32, (owners, owners), 0)
    begins, count = place(lengths, (row % n_tm) * n_rows + row // n_tm)
    for lo in range(0, width, COLS):
        turned[lo : lo + COLS, :] = one[:, lo : lo + COLS].astype(F32).T.astype(BF)
    group = capacity // 3
    for f in range(3):
        voxel = lax.broadcasted_iota(jnp.int32, (owners, 512), 1).astype(F32) + float(f * 512)
        slot = voxel - begins
        slot = jnp.where((slot >= 0.0) & (slot < count), slot, -1.0).astype(BF)
        total = jnp.zeros((channels, 512), F32)
        for k in range(0, capacity, group):
            left = jnp.concatenate(
                [turned[(k + i) * channels : (k + i + 1) * channels, :] for i in range(group)], axis=1
            )
            right = jnp.concatenate(
                [jnp.where(slot == jnp.asarray(k + i, BF), jnp.asarray(1, BF), jnp.asarray(0, BF)) for i in range(group)],
                axis=0,
            )
            total += jnp.dot(left, right, preferred_element_type=F32)
        lo = f * 512
        cot = total.astype(BF)
        cot3[0:channels, lo : lo + 512] = sideways(total, -1).astype(BF)
        cot3[channels : 2 * channels, lo : lo + 512] = cot
        cot3[2 * channels : 3 * channels, lo : lo + 512] = sideways(total, 1).astype(BF)
        if f < 2:
            to_tm[:, lo : lo + 512] = cot


def unpack(one, lengths, n_tm, n_rows, capacity, after):
    channels = one.shape[1] // capacity

    def body(*refs):
        unpack_body(n_tm, n_rows, capacity, *refs)

    return call(
        body,
        [((3 * channels, 1536), BF), ((channels, 1024), BF)],
        one,
        lengths,
        scratch=[pltpu.VMEM((one.shape[1], one.shape[0]), BF)],
        after=after,
    )


def edges_kernel(own, top, bot):
    for f in range(3):
        top[:, f * COLS : (f + 1) * COLS] = own[:, f * 512 : f * 512 + COLS]
        bot[:, f * COLS : (f + 1) * COLS] = own[:, f * 512 + 3 * COLS : (f + 1) * 512]


def frames_kernel(own, top, bot, to_tm):
    for f in range(2):
        lo = f * 768
        to_tm[:, lo : lo + COLS] = top[:, (f + 1) * COLS : (f + 2) * COLS]
        to_tm[:, lo + COLS : lo + 5 * COLS] = own[:, (f + 1) * 512 : (f + 2) * 512]
        to_tm[:, lo + 5 * COLS : lo + 6 * COLS] = bot[:, (f + 1) * COLS : (f + 2) * COLS]


def rims_kernel(cot3, by_tm, top, bot):
    for f in range(5):
        if f < 3:
            frame = cot3[192:384, f * 512 : (f + 1) * 512]
        else:
            frame = by_tm[:, (f - 3) * 512 : (f - 2) * 512]
        top[:, f * COLS : (f + 1) * COLS] = frame[:, :COLS]
        bot[:, f * COLS : (f + 1) * COLS] = frame[:, 3 * COLS :]


def turn_weights_kernel(src, out, done):
    done[...] = jnp.zeros(done.shape, F32)

    def turned(tap):
        wide = jnp.concatenate([src[26 - tap].astype(F32), jnp.zeros((64, 192), F32)], axis=0)
        wide = jnp.concatenate([wide, jnp.zeros((256, 64), F32)], axis=1).T
        return wide[:192, :192].astype(BF)

    for q in range(3):
        for ab in range(0, 9, 2):
            left = turned(ab * 3 + q)
            right = turned((ab + 1) * 3 + q) if ab < 8 else jnp.zeros((192, 64), BF)
            pair = jnp.concatenate([left, right], axis=1)
            out[q * 192 : (q + 1) * 192, ab * 192 : ab * 192 + pair.shape[1]] = pair


def add_kernel(kept, got, out):
    out[...] = (kept[...].astype(F32) + got[...].astype(F32)).astype(BF)


def share_kernel(got, out):
    total = got[0].astype(F32)
    for i in range(1, got.shape[0]):
        total += got[i].astype(F32)
    total = total.astype(BF)
    for i in range(out.shape[0]):
        out[i] = total


def gain_of(total):
    return total[0:2] + total[2:4]


def gather_kernel(got, line, out):
    share = got.shape[1]
    total = got[0].astype(F32)
    for i in range(1, got.shape[0]):
        total += got[i].astype(F32)
    total = total.astype(BF)
    high = line[...].astype(BF).astype(F32)
    block = jnp.concatenate([high, line[...] - high, jnp.zeros((12, COLS), F32)], axis=0).astype(BF)
    for i in range(out.shape[0]):
        out[i, :share, :] = total
        out[i, share:, :] = block


def hidden_kernel(own, by_tm, top, bot, gain, out, done):
    done[...] = jnp.zeros(done.shape, F32)
    for fe in range(5):
        if fe < 2:
            x = by_tm[:, fe * 768 : (fe + 1) * 768].astype(F32)
        else:
            f = fe - 2
            mid = own[:, f * 512 : (f + 1) * 512]
            above = top[:, f * COLS : (f + 1) * COLS]
            below = bot[:, f * COLS : (f + 1) * COLS]
            x = jnp.concatenate([above, mid, below], axis=1).astype(F32)
        inverse = lax.rsqrt(jnp.mean(x * x, axis=0, keepdims=True) + EPSILON)
        preact = x * inverse * gain[...]
        hidden = preact * jax.nn.sigmoid(preact)
        wide = jnp.concatenate([hidden, jnp.zeros((64, 768), F32)], axis=0)
        out[fe * 768 : (fe + 1) * 768, :] = wide.T[:, :192].astype(BF)


def weight_kernel(clip, cot3, hid, keep, give, out):
    held = None
    for ab in range(9):
        a, b = divmod(ab, 3)
        right = jnp.concatenate(
            [hid[((f + a) * 6 + b) * COLS : ((f + a) * 6 + b + 4) * COLS, :] for f in range(3)], axis=0
        )
        part = jnp.dot(cot3[...], right, preferred_element_type=F32).astype(BF)
        out[ab * 576 : (ab + 1) * 576, :] = part[:, :COLS]
        rest = part[:, COLS:192]
        if ab == 8:
            out[MAIN + 4 * 576 : MAIN + 4 * 576 + 288, :] = jnp.concatenate([rest[:288], rest[288:]], axis=1)
        elif ab % 2:
            at = MAIN + (ab // 2) * 576
            out[at : at + 576, :] = jnp.concatenate([held, rest], axis=1)
        else:
            held = rest
    done = MAIN + MAIN // 2
    out[done:, :] = jnp.zeros((out.shape[0] - done, COLS), BF)
    half = out.shape[0] // 2
    keep[...] = out[pl.ds(pl.multiple_of(clip[0] * half, half), half), :]
    give[...] = out[pl.ds(pl.multiple_of((1 - clip[0]) * half, half), half), :]


def input_kernel(own, gain, cot3, by_tm, top, bot, weights, out, gain_out, ext, rhs):
    for fe in range(5):
        lo = fe * 768
        ext[:, lo : lo + COLS] = top[:, fe * COLS : (fe + 1) * COLS]
        if fe < 3:
            ext[:, lo + COLS : lo + 5 * COLS] = cot3[192:384, fe * 512 : (fe + 1) * 512]
        else:
            ext[:, lo + COLS : lo + 5 * COLS] = by_tm[:, (fe - 3) * 512 : (fe - 2) * 512]
        ext[:, lo + 5 * COLS : lo + 6 * COLS] = bot[:, fe * COLS : (fe + 1) * COLS]
    gain_sum = jnp.zeros((192, COLS), F32)
    rhs[1728:, :] = jnp.zeros((64, 512), BF)
    for f in range(3):
        for ab in range(9):
            a, b = divmod(ab, 3)
            lo = ((f + a) * 6 + b) * COLS
            rhs[ab * 192 : (ab + 1) * 192, :] = ext[:, lo : lo + 512]
        spread = jnp.dot(weights[...], rhs[...], preferred_element_type=F32)
        grad = sideways(spread[0:192], 1) + spread[192:384] + sideways(spread[384:576], -1)
        x = own[:, f * 512 : (f + 1) * 512].astype(F32)
        inverse = lax.rsqrt(jnp.mean(x * x, axis=0, keepdims=True) + EPSILON)
        normed = x * inverse
        preact = normed * gain[...]
        s = jax.nn.sigmoid(preact)
        preact_grad = grad * s * (1.0 + preact * (1.0 - s))
        term = preact_grad * normed
        for lo in range(0, 512, COLS):
            gain_sum += term[:, lo : lo + COLS]
        projection = jnp.mean(term * gain[...], axis=0, keepdims=True)
        cot = cot3[192:384, f * 512 : (f + 1) * 512].astype(F32)
        result = inverse * (preact_grad * gain[...] - normed * projection) + cot
        out[:, f * 512 : (f + 1) * 512] = result.astype(BF)
    totals = jnp.broadcast_to(jnp.sum(gain_sum, axis=1, keepdims=True), (192, COLS))
    line = jnp.concatenate([totals, jnp.zeros((64, COLS), F32)], axis=0).T[0:1, :]
    gain_out[0:1, :] = line[:, :COLS]
    gain_out[1:2, :] = line[:, COLS:]


def final_kernel(scale, clip, mine, other, out, gain_out, buf):
    n, share = mine.shape[0], mine.shape[1] - 16
    at = clip[0]
    gains = jnp.zeros((2, COLS), F32)
    for held, half in ((mine, at), (other, 1 - at)):
        for i in range(n):
            rows = pl.ds(pl.multiple_of(half * (n * share) + i * share, share), share)
            buf[rows, :] = held[i, :share, :]
            gains += gain_of(held[i, share:, :].astype(F32))
    gain_out[...] = gains * scale
    for tap in range(27):
        ab, q = divmod(tap, 3)
        main = buf[tap * 192 : (tap + 1) * 192, :].astype(F32)
        if ab < 8:
            row = MAIN + (ab // 2) * 576 + q * 192
            side = buf[row : row + 192, :].astype(F32)
            side = side[:, 64 * (ab % 2) : 64 * (ab % 2) + 64]
        else:
            row = MAIN + 4 * 576
            first, second = buf[row : row + 288, 0:64].astype(F32), buf[row : row + 288, 64:128].astype(F32)
            if q == 0:
                side = first[0:192]
            elif q == 1:
                side = jnp.concatenate([first[192:288], second[0:96]], axis=0)
            else:
                side = second[96:288]
        out[tap, :, :] = jnp.concatenate([main, side], axis=1) * scale


def shifted(shard, axis, by):
    count = lax.axis_size(axis)
    return lax.ppermute(shard, axis, [(i, i + by) for i in range(count) if 0 <= i + by < count])


def exchange(x, axis):
    return lax.all_to_all(x, axis, split_axis=0, concat_axis=0, tiled=True)


def shards(activations, norm_gain, conv_weights, packed_grads, piece_lengths):
    n_tm, n_rows, n_clip = lax.axis_size("tm"), lax.axis_size("rows"), lax.axis_size("clip")
    channels, frames, row_count, col_count = activations.shape[1:]
    voxels = frames * row_count * col_count
    owners = piece_lengths.shape[2]
    width = packed_grads.shape[3]
    capacity = width // channels
    grad_scale = 1.0 / math.sqrt(voxels * n_tm * n_rows * n_clip)
    gain_col = norm_gain[:, None]

    packed = packed_grads.reshape(owners, width)
    own = activations.reshape(channels, voxels)
    a_top, a_bot = call(edges_kernel, [((channels, 384), BF)] * 2, own)
    act_bot = shifted(a_top, "rows", -1)
    act_top = shifted(a_bot, "rows", 1)
    first = exchange(packed.reshape(n_tm, n_rows, width), "tm").reshape(owners, width)
    first = swap_rows(first, n_tm, n_rows, (act_top, act_bot))
    arrived = exchange(first.reshape(n_rows, n_tm, width), "rows").reshape(owners, width)
    a_frames = call(frames_kernel, [((channels, 1536), BF)], own, act_top, act_bot)[0]
    act_tm = shifted(a_frames, "tm", 1)
    flag = ((8, COLS), F32)
    hid, had_hid = call(hidden_kernel, [((30 * COLS, channels), BF), flag], own, act_tm, act_top, act_bot, gain_col)
    weights, had_weights = call(turn_weights_kernel, [((576, 1792), BF), flag], conv_weights.transpose(1, 0, 2))

    cot3, c_frames = unpack(arrived, piece_lengths.reshape(1, owners), n_tm, n_rows, capacity, (had_hid, had_weights))
    cot_tm = shifted(c_frames, "tm", -1)

    clip = lax.axis_index("clip").astype(jnp.int32).reshape(1)
    swap_clip = [(0, 1), (1, 0)]
    keep, give = call(
        weight_kernel, [((4096, COLS), BF)] * 2, clip, cot3, hid, scratch=[pltpu.VMEM((8192, COLS), BF)]
    )
    part = call(
        add_kernel, [((4096, COLS), BF)], keep, lax.ppermute(give, "clip", swap_clip), after=(cot_tm,)
    )[0]
    share = part.shape[0] // n_tm
    got = exchange(part.reshape(n_tm, share, COLS), "tm")

    c_top, c_bot = call(rims_kernel, [((channels, 640), BF)] * 2, cot3, cot_tm)
    cot_bot = shifted(c_top, "rows", -1)
    cot_top = shifted(c_bot, "rows", 1)
    input_grad, gain_sum = call(
        input_kernel,
        [((channels, voxels), BF), ((2, COLS), F32)],
        own,
        gain_col,
        cot3,
        cot_tm,
        cot_top,
        cot_bot,
        weights,
        scratch=[pltpu.VMEM((channels, 30 * COLS), BF), pltpu.VMEM((1792, 512), BF)],
    )
    by = 1
    while by < n_rows:
        gain_sum = gain_sum + lax.ppermute(gain_sum, "rows", [(j, j ^ by) for j in range(n_rows)])
        by *= 2

    had_rims = cot_top[:8, :COLS] + cot_bot[:8, :COLS]

    sent = call(share_kernel, [((n_rows, share, COLS), BF)], got, after=(had_rims,))[0]
    got = exchange(sent, "rows")
    sent = call(gather_kernel, [((n_tm, share + 16, COLS), BF)], got, gain_sum)[0]
    mine = exchange(sent, "tm")
    other = lax.ppermute(mine, "clip", swap_clip)

    def finish(*refs):
        final_kernel(grad_scale, *refs)

    weight_grad, gain_grad = call(
        finish,
        [((27, channels, channels), F32), ((2, COLS), F32)],
        clip,
        mine,
        other,
        scratch=[pltpu.VMEM((8192, COLS), BF)],
    )
    gain_grad = gain_grad.reshape(2 * COLS)[:channels]
    return (input_grad.reshape(activations.shape), weight_grad.transpose(1, 0, 2), gain_grad)


def solution(mesh):
    return jax.shard_map(
        shards,
        mesh=mesh,
        in_specs=(
            P("clip", None, "tm", "rows", None),
            P(),
            P(),
            P("clip", ("tm", "rows"), None, None),
            P("clip", ("tm", "rows"), None),
        ),
        out_specs=(P("clip", None, "tm", "rows", None), P(), P()),
        check_vma=False,
    )
```

```python
import math

import jax
import jax.numpy as jnp
from jax import lax
from jax.experimental import pallas as pl
from jax.experimental.pallas import tpu as pltpu
from jax.sharding import PartitionSpec as P

EPSILON = 1e-06
BF = jnp.bfloat16
F32 = jnp.float32
COLS = 128
MAIN = 5184
GIVEN = 4


def call(body, outs, *args, scratch=(), after=()):
    outs = [jax.ShapeDtypeStruct(s, d) for s, d in outs]
    spec = pl.BlockSpec(memory_space=pltpu.VMEM)

    def after_them(*refs):
        body(*refs[len(after) :])

    return pl.pallas_call(
        after_them,
        out_shape=outs,
        in_specs=[pl.BlockSpec(memory_space=pl.ANY)] * len(after)
        + [pl.BlockSpec(memory_space=pltpu.SMEM) if a.ndim == 1 else spec for a in args],
        out_specs=[spec] * len(outs),
        scratch_shapes=list(scratch),
        compiler_params=pltpu.CompilerParams(vmem_limit_bytes=16 << 20),
    )(*after, *args)


def swap_kernel(major, minor, src, out):
    n = major * minor
    to = lax.broadcasted_iota(jnp.int32, (n, n), 0)
    at = lax.broadcasted_iota(jnp.int32, (n, n), 1)
    pick = (at == (to % major) * minor + to // major).astype(F32).astype(BF)
    width = src.shape[1]
    for lo in range(0, width, 512):
        part = jnp.dot(pick, src[:, lo : lo + 512], preferred_element_type=F32)
        out[:, lo : lo + 512] = part.astype(BF)


def swap_rows(x, major, minor, after):
    def body(src, out):
        swap_kernel(major, minor, src, out)

    return call(body, [(x.shape, BF)], x, after=after)[0]


def sideways(x, by):
    lanes = lax.broadcasted_iota(jnp.int32, (x.shape[0], COLS), 1)
    edge = 0 if by == 1 else COLS - 1
    parts = []
    for lo in range(0, x.shape[1], COLS):
        turned = pltpu.roll(x[:, lo : lo + COLS], by % COLS, 1)
        parts.append(jnp.where(lanes == edge, 0.0, turned))
    return jnp.concatenate(parts, axis=1)


def place(lengths, owner):
    owners = owner.shape[0]
    other = lax.broadcasted_iota(jnp.int32, (owners, owners), 1)
    held = jnp.broadcast_to(lengths[...], (owners, owners)).astype(F32)
    begins = jnp.sum(jnp.where(other < owner, held, 0.0), axis=1, keepdims=True)
    count = jnp.sum(jnp.where(other == owner, held, 0.0), axis=1, keepdims=True)
    return begins, count


def unpack_body(n_tm, n_rows, capacity, one, lengths, cot3, to_tm, turned):
    owners = n_tm * n_rows
    width = one.shape[1]
    channels = width // capacity
    row = lax.broadcasted_iota(jnp.int32, (owners, owners), 0)
    begins, count = place(lengths, (row % n_tm) * n_rows + row // n_tm)
    for lo in range(0, width, COLS):
        turned[lo : lo + COLS, :] = one[:, lo : lo + COLS].astype(F32).T.astype(BF)
    group = capacity // 3
    for f in range(3):
        voxel = lax.broadcasted_iota(jnp.int32, (owners, 512), 1).astype(F32) + float(f * 512)
        slot = voxel - begins
        slot = jnp.where((slot >= 0.0) & (slot < count), slot, -1.0).astype(BF)
        total = jnp.zeros((channels, 512), F32)
        for k in range(0, capacity, group):
            left = jnp.concatenate(
                [turned[(k + i) * channels : (k + i + 1) * channels, :] for i in range(group)], axis=1
            )
            right = jnp.concatenate(
                [jnp.where(slot == jnp.asarray(k + i, BF), jnp.asarray(1, BF), jnp.asarray(0, BF)) for i in range(group)],
                axis=0,
            )
            total += jnp.dot(left, right, preferred_element_type=F32)
        lo = f * 512
        cot = total.astype(BF)
        cot3[0:channels, lo : lo + 512] = sideways(total, -1).astype(BF)
        cot3[channels : 2 * channels, lo : lo + 512] = cot
        cot3[2 * channels : 3 * channels, lo : lo + 512] = sideways(total, 1).astype(BF)
        if f < 2:
            to_tm[:, lo : lo + 512] = cot


def unpack(one, lengths, n_tm, n_rows, capacity, after):
    channels = one.shape[1] // capacity

    def body(*refs):
        unpack_body(n_tm, n_rows, capacity, *refs)

    return call(
        body,
        [((3 * channels, 1536), BF), ((channels, 1024), BF)],
        one,
        lengths,
        scratch=[pltpu.VMEM((one.shape[1], one.shape[0]), BF)],
        after=after,
    )


def edges_kernel(own, top, bot):
    for f in range(3):
        top[:, f * COLS : (f + 1) * COLS] = own[:, f * 512 : f * 512 + COLS]
        bot[:, f * COLS : (f + 1) * COLS] = own[:, f * 512 + 3 * COLS : (f + 1) * 512]


def frames_kernel(own, top, bot, to_tm):
    for f in range(2):
        lo = f * 768
        to_tm[:, lo : lo + COLS] = top[:, (f + 1) * COLS : (f + 2) * COLS]
        to_tm[:, lo + COLS : lo + 5 * COLS] = own[:, (f + 1) * 512 : (f + 2) * 512]
        to_tm[:, lo + 5 * COLS : lo + 6 * COLS] = bot[:, (f + 1) * COLS : (f + 2) * COLS]


def rims_kernel(cot3, by_tm, top, bot):
    for f in range(5):
        if f < 3:
            frame = cot3[192:384, f * 512 : (f + 1) * 512]
        else:
            frame = by_tm[:, (f - 3) * 512 : (f - 2) * 512]
        top[:, f * COLS : (f + 1) * COLS] = frame[:, :COLS]
        bot[:, f * COLS : (f + 1) * COLS] = frame[:, 3 * COLS :]


def turn_weights_kernel(src, out, done):
    done[...] = jnp.zeros(done.shape, F32)

    def turned(tap):
        wide = jnp.concatenate([src[26 - tap].astype(F32), jnp.zeros((64, 192), F32)], axis=0)
        wide = jnp.concatenate([wide, jnp.zeros((256, 64), F32)], axis=1).T
        return wide[:192, :192].astype(BF)

    for q in range(3):
        for ab in range(0, 9, 2):
            left = turned(ab * 3 + q)
            right = turned((ab + 1) * 3 + q) if ab < 8 else jnp.zeros((192, 64), BF)
            pair = jnp.concatenate([left, right], axis=1)
            out[q * 192 : (q + 1) * 192, ab * 192 : ab * 192 + pair.shape[1]] = pair


def add_kernel(kept, *rest):
    got, out = rest[:-1], rest[-1]
    size = got[0].shape[0]
    for i, piece in enumerate(got):
        rows = slice(i * size, (i + 1) * size)
        out[rows, :] = (kept[rows, :].astype(F32) + piece[...].astype(F32)).astype(BF)


def gain_lines(total):
    return total[0:2] + total[2:4]


def gain_block(lines):
    high = lines.astype(BF).astype(F32)
    return jnp.concatenate([high, lines - high, jnp.zeros((12, COLS), F32)], axis=0).astype(BF)


def sum_of(got, rows):
    total = got[0, rows, :].astype(F32)
    for i in range(1, got.shape[0]):
        total += got[i, rows, :].astype(F32)
    return total


def share_kernel(got, lines, out):
    share = got.shape[1]
    total = sum_of(got, slice(0, share)).astype(BF)
    block = gain_block(lines[...])
    for i in range(out.shape[0]):
        out[i, :share, :] = total
        out[i, share:, :] = block


def gather_kernel(got, out):
    share = got.shape[1] - 16
    total = sum_of(got, slice(0, share)).astype(BF)
    block = gain_block(gain_lines(sum_of(got, slice(share, share + 16))))
    for i in range(out.shape[0]):
        out[i, :share, :] = total
        out[i, share:, :] = block


def hidden_kernel(own, by_tm, top, bot, gain, out, factor, done):
    done[...] = jnp.zeros(done.shape, F32)
    for fe in range(5):
        if fe < 2:
            x = by_tm[:, fe * 768 : (fe + 1) * 768].astype(F32)
        else:
            f = fe - 2
            mid = own[:, f * 512 : (f + 1) * 512]
            above = top[:, f * COLS : (f + 1) * COLS]
            below = bot[:, f * COLS : (f + 1) * COLS]
            x = jnp.concatenate([above, mid, below], axis=1).astype(F32)
        normed = x * lax.rsqrt(jnp.mean(x * x, axis=0, keepdims=True) + EPSILON)
        preact = normed * gain[...]
        s = jax.nn.sigmoid(preact)
        for value, to in ((preact * s, out), (s * (1.0 + preact * (1.0 - s)) * normed, factor)):
            wide = jnp.concatenate([value, jnp.zeros((64, 768), F32)], axis=0)
            to[fe * 768 : (fe + 1) * 768, :] = wide.T[:, :192].astype(BF)


def window(ext, ab):
    a, b = divmod(ab, 3)
    parts = [ext[((f + a) * 6 + b) * COLS : ((f + a) * 6 + b + 4) * COLS, :] for f in range(3)]
    return jnp.concatenate(parts, axis=0)


def gain_kernel(cot3, factor, weights, out):
    total = jnp.zeros((1, 192), F32)
    for ab in range(9):
        part = jnp.dot(cot3[...], window(factor, ab), preferred_element_type=F32)
        for q in range(3):
            term = part[q * 192 : (q + 1) * 192] * weights[ab * 3 + q].astype(F32)
            total += jnp.sum(term, axis=0, keepdims=True)
    wide = jnp.concatenate([total, jnp.zeros((1, 64), F32)], axis=1)
    out[0:1, :] = wide[:, :COLS]
    out[1:2, :] = wide[:, COLS:]


def weight_kernel(clip, cot3, hid, keep, *rest):
    give, out = rest[:-1], rest[-1]
    held = None
    for ab in range(9):
        right = window(hid, ab)
        part = jnp.dot(cot3[...], right, preferred_element_type=F32).astype(BF)
        out[ab * 576 : (ab + 1) * 576, :] = part[:, :COLS]
        rest = part[:, COLS:192]
        if ab == 8:
            out[MAIN + 4 * 576 : MAIN + 4 * 576 + 288, :] = jnp.concatenate([rest[:288], rest[288:]], axis=1)
        elif ab % 2:
            at = MAIN + (ab // 2) * 576
            out[at : at + 576, :] = jnp.concatenate([held, rest], axis=1)
        else:
            held = rest
    done = MAIN + MAIN // 2
    out[done:, :] = jnp.zeros((out.shape[0] - done, COLS), BF)
    half = out.shape[0] // 2
    keep[...] = out[pl.ds(pl.multiple_of(clip[0] * half, half), half), :]
    size = half // len(give)
    for i, piece in enumerate(give):
        piece[...] = out[pl.ds(pl.multiple_of((1 - clip[0]) * half + i * size, size), size), :]


def input_kernel(own, gain, cot3, by_tm, top, bot, weights, out, ext, rhs):
    for fe in range(5):
        lo = fe * 768
        ext[:, lo : lo + COLS] = top[:, fe * COLS : (fe + 1) * COLS]
        if fe < 3:
            ext[:, lo + COLS : lo + 5 * COLS] = cot3[192:384, fe * 512 : (fe + 1) * 512]
        else:
            ext[:, lo + COLS : lo + 5 * COLS] = by_tm[:, (fe - 3) * 512 : (fe - 2) * 512]
        ext[:, lo + 5 * COLS : lo + 6 * COLS] = bot[:, fe * COLS : (fe + 1) * COLS]
    rhs[1728:, :] = jnp.zeros((64, 512), BF)
    for f in range(3):
        for ab in range(9):
            a, b = divmod(ab, 3)
            lo = ((f + a) * 6 + b) * COLS
            rhs[ab * 192 : (ab + 1) * 192, :] = ext[:, lo : lo + 512]
        spread = jnp.dot(weights[...], rhs[...], preferred_element_type=F32)
        grad = sideways(spread[0:192], 1) + spread[192:384] + sideways(spread[384:576], -1)
        x = own[:, f * 512 : (f + 1) * 512].astype(F32)
        inverse = lax.rsqrt(jnp.mean(x * x, axis=0, keepdims=True) + EPSILON)
        normed = x * inverse
        preact = normed * gain[...]
        s = jax.nn.sigmoid(preact)
        preact_grad = grad * s * (1.0 + preact * (1.0 - s))
        projection = jnp.mean(preact_grad * normed * gain[...], axis=0, keepdims=True)
        cot = cot3[192:384, f * 512 : (f + 1) * 512].astype(F32)
        result = inverse * (preact_grad * gain[...] - normed * projection) + cot
        out[:, f * 512 : (f + 1) * 512] = result.astype(BF)


def final_kernel(scale, clip, mine, other, out, gain_out, buf):
    n, share = mine.shape[0], mine.shape[1] - 16
    at = clip[0]
    gains = jnp.zeros((2, COLS), F32)
    for held, half in ((mine, at), (other, 1 - at)):
        for i in range(n):
            rows = pl.ds(pl.multiple_of(half * (n * share) + i * share, share), share)
            buf[rows, :] = held[i, :share, :]
            gains += gain_lines(held[i, share:, :].astype(F32))
    gain_out[...] = gains * scale
    for tap in range(27):
        ab, q = divmod(tap, 3)
        main = buf[tap * 192 : (tap + 1) * 192, :].astype(F32)
        if ab < 8:
            row = MAIN + (ab // 2) * 576 + q * 192
            side = buf[row : row + 192, :].astype(F32)
            side = side[:, 64 * (ab % 2) : 64 * (ab % 2) + 64]
        else:
            row = MAIN + 4 * 576
            first, second = buf[row : row + 288, 0:64].astype(F32), buf[row : row + 288, 64:128].astype(F32)
            if q == 0:
                side = first[0:192]
            elif q == 1:
                side = jnp.concatenate([first[192:288], second[0:96]], axis=0)
            else:
                side = second[96:288]
        out[tap, :, :] = jnp.concatenate([main, side], axis=1) * scale


def shifted(shard, axis, by):
    count = lax.axis_size(axis)
    return lax.ppermute(shard, axis, [(i, i + by) for i in range(count) if 0 <= i + by < count])


def exchange(x, axis):
    return lax.all_to_all(x, axis, split_axis=0, concat_axis=0, tiled=True)


def shards(activations, norm_gain, conv_weights, packed_grads, piece_lengths):
    n_tm, n_rows, n_clip = lax.axis_size("tm"), lax.axis_size("rows"), lax.axis_size("clip")
    channels, frames, row_count, col_count = activations.shape[1:]
    voxels = frames * row_count * col_count
    owners = piece_lengths.shape[2]
    width = packed_grads.shape[3]
    capacity = width // channels
    grad_scale = 1.0 / math.sqrt(voxels * n_tm * n_rows * n_clip)
    gain_col = norm_gain[:, None]

    packed = packed_grads.reshape(owners, width)
    own = activations.reshape(channels, voxels)
    a_top, a_bot = call(edges_kernel, [((channels, 384), BF)] * 2, own)
    act_bot = shifted(a_top, "rows", -1)
    act_top = shifted(a_bot, "rows", 1)
    first = exchange(packed.reshape(n_tm, n_rows, width), "tm").reshape(owners, width)
    first = swap_rows(first, n_tm, n_rows, (act_top, act_bot))
    arrived = exchange(first.reshape(n_rows, n_tm, width), "rows").reshape(owners, width)
    a_frames = call(frames_kernel, [((channels, 1536), BF)], own, act_top, act_bot)[0]
    act_tm = shifted(a_frames, "tm", 1)
    flag = ((8, COLS), F32)
    extended = ((30 * COLS, channels), BF)
    hid, factor, had_hid = call(
        hidden_kernel, [extended, extended, flag], own, act_tm, act_top, act_bot, gain_col
    )
    taps = conv_weights.transpose(1, 0, 2)
    weights, had_weights = call(turn_weights_kernel, [((576, 1792), BF), flag], taps)

    cot3, c_frames = unpack(arrived, piece_lengths.reshape(1, owners), n_tm, n_rows, capacity, (had_hid, had_weights))
    cot_tm = shifted(c_frames, "tm", -1)

    clip = lax.axis_index("clip").astype(jnp.int32).reshape(1)
    swap_clip = [(0, 1), (1, 0)]
    outs = [((4096, COLS), BF)] + [((4096 // GIVEN, COLS), BF)] * GIVEN
    keep, *give = call(weight_kernel, outs, clip, cot3, hid, scratch=[pltpu.VMEM((8192, COLS), BF)])
    given = [lax.ppermute(piece, "clip", swap_clip) for piece in give]
    part = call(add_kernel, [((4096, COLS), BF)], keep, *given, after=(cot_tm,))[0]
    share = part.shape[0] // n_tm
    got = exchange(part.reshape(n_tm, share, COLS), "tm")

    gain_sum = call(gain_kernel, [((2, COLS), F32)], cot3, factor, taps)[0]

    c_top, c_bot = call(rims_kernel, [((channels, 640), BF)] * 2, cot3, cot_tm)
    cot_bot = shifted(c_top, "rows", -1)
    cot_top = shifted(c_bot, "rows", 1)
    input_grad = call(
        input_kernel,
        [((channels, voxels), BF)],
        own,
        gain_col,
        cot3,
        cot_tm,
        cot_top,
        cot_bot,
        weights,
        scratch=[pltpu.VMEM((channels, 30 * COLS), BF), pltpu.VMEM((1792, 512), BF)],
    )[0]

    had_rims = cot_top[:8, :COLS] + cot_bot[:8, :COLS]

    sent = call(share_kernel, [((n_rows, share + 16, COLS), BF)], got, gain_sum, after=(had_rims,))[0]
    got = exchange(sent, "rows")
    had_grad = input_grad[:8, :COLS]
    sent = call(gather_kernel, [((n_tm, share + 16, COLS), BF)], got, after=(had_grad,))[0]
    mine = exchange(sent, "tm")
    other = lax.ppermute(mine, "clip", swap_clip)

    def finish(*refs):
        final_kernel(grad_scale, *refs)

    weight_grad, gain_grad = call(
        finish,
        [((27, channels, channels), F32), ((2, COLS), F32)],
        clip,
        mine,
        other,
        scratch=[pltpu.VMEM((8192, COLS), BF)],
    )
    gain_grad = gain_grad.reshape(2 * COLS)[:channels]
    return (input_grad.reshape(activations.shape), weight_grad.transpose(1, 0, 2), gain_grad)


def solution(mesh):
    return jax.shard_map(
        shards,
        mesh=mesh,
        in_specs=(
            P("clip", None, "tm", "rows", None),
            P(),
            P(),
            P("clip", ("tm", "rows"), None, None),
            P("clip", ("tm", "rows"), None),
        ),
        out_specs=(P("clip", None, "tm", "rows", None), P(), P()),
        check_vma=False,
    )
```

```python
import math

import jax
import jax.numpy as jnp
from jax import lax
from jax.experimental import pallas as pl
from jax.experimental.pallas import tpu as pltpu
from jax.sharding import PartitionSpec as P

EPSILON = 1e-06
BF = jnp.bfloat16
F32 = jnp.float32
COLS = 128
MAIN = 5184
GIVEN = 4


def call(body, outs, *args, scratch=(), after=()):
    outs = [jax.ShapeDtypeStruct(s, d) for s, d in outs]
    spec = pl.BlockSpec(memory_space=pltpu.VMEM)

    def after_them(*refs):
        body(*refs[len(after) :])

    return pl.pallas_call(
        after_them,
        out_shape=outs,
        in_specs=[pl.BlockSpec(memory_space=pl.ANY)] * len(after)
        + [pl.BlockSpec(memory_space=pltpu.SMEM) if a.ndim == 1 else spec for a in args],
        out_specs=[spec] * len(outs),
        scratch_shapes=list(scratch),
        compiler_params=pltpu.CompilerParams(vmem_limit_bytes=16 << 20),
    )(*after, *args)


def chunk_rows(packed):
    rows, width = packed.shape
    parts = width // COLS

    def body(src, out, wide):
        for j in range(parts):
            wide[pl.ds(j, rows, stride=parts), :] = src[:, j * COLS : (j + 1) * COLS].astype(F32)
        out[...] = wide[...].astype(BF)

    return call(body, [((rows * parts, COLS), BF)], packed, scratch=[pltpu.VMEM((rows * parts, COLS), F32)])[0]


def sideways(x, by):
    lanes = lax.broadcasted_iota(jnp.int32, (x.shape[0], COLS), 1)
    edge = 0 if by == 1 else COLS - 1
    parts = []
    for lo in range(0, x.shape[1], COLS):
        turned = pltpu.roll(x[:, lo : lo + COLS], by % COLS, 1)
        parts.append(jnp.where(lanes == edge, 0.0, turned))
    return jnp.concatenate(parts, axis=1)


def place(lengths, owner):
    owners = owner.shape[0]
    other = lax.broadcasted_iota(jnp.int32, (owners, owners), 1)
    held = jnp.broadcast_to(lengths[...], (owners, owners)).astype(F32)
    begins = jnp.sum(jnp.where(other < owner, held, 0.0), axis=1, keepdims=True)
    count = jnp.sum(jnp.where(other == owner, held, 0.0), axis=1, keepdims=True)
    return begins, count


def unpack_body(capacity, arrived, lengths, cot3, to_tm, wide, turned):
    owners = lengths.shape[1]
    parts = arrived.shape[0] // owners
    channels = parts * COLS // capacity
    begins, count = place(lengths, lax.broadcasted_iota(jnp.int32, (owners, owners), 0))
    wide[...] = arrived[...].astype(F32)
    for j in range(parts):
        turned[j * COLS : (j + 1) * COLS, :] = wide[pl.ds(j, owners, stride=parts), :].T.astype(BF)
    group = capacity // 3
    for f in range(3):
        voxel = lax.broadcasted_iota(jnp.int32, (owners, 512), 1).astype(F32) + float(f * 512)
        slot = voxel - begins
        slot = jnp.where((slot >= 0.0) & (slot < count), slot, -1.0).astype(BF)
        total = jnp.zeros((channels, 512), F32)
        for k in range(0, capacity, group):
            left = jnp.concatenate(
                [turned[(k + i) * channels : (k + i + 1) * channels, :] for i in range(group)], axis=1
            )
            right = jnp.concatenate(
                [jnp.where(slot == jnp.asarray(k + i, BF), jnp.asarray(1, BF), jnp.asarray(0, BF)) for i in range(group)],
                axis=0,
            )
            total += jnp.dot(left, right, preferred_element_type=F32)
        lo = f * 512
        cot = total.astype(BF)
        cot3[0:channels, lo : lo + 512] = sideways(total, -1).astype(BF)
        cot3[channels : 2 * channels, lo : lo + 512] = cot
        cot3[2 * channels : 3 * channels, lo : lo + 512] = sideways(total, 1).astype(BF)
        if f < 2:
            to_tm[:, lo : lo + 512] = cot


def unpack(arrived, lengths, capacity, after):
    owners = lengths.shape[1]
    size = arrived.shape[0] * COLS // owners
    channels = size // capacity

    def body(*refs):
        unpack_body(capacity, *refs)

    return call(
        body,
        [((3 * channels, 1536), BF), ((channels, 1024), BF)],
        arrived,
        lengths,
        scratch=[pltpu.VMEM(arrived.shape, F32), pltpu.VMEM((size, owners), BF)],
        after=after,
    )


def edges_kernel(own, top, bot):
    for f in range(3):
        top[:, f * COLS : (f + 1) * COLS] = own[:, f * 512 : f * 512 + COLS]
        bot[:, f * COLS : (f + 1) * COLS] = own[:, f * 512 + 3 * COLS : (f + 1) * 512]


def frames_kernel(own, top, bot, to_tm):
    for f in range(2):
        lo = f * 768
        to_tm[:, lo : lo + COLS] = top[:, (f + 1) * COLS : (f + 2) * COLS]
        to_tm[:, lo + COLS : lo + 5 * COLS] = own[:, (f + 1) * 512 : (f + 2) * 512]
        to_tm[:, lo + 5 * COLS : lo + 6 * COLS] = bot[:, (f + 1) * COLS : (f + 2) * COLS]


def rims_kernel(cot3, by_tm, top, bot):
    for f in range(5):
        if f < 3:
            frame = cot3[192:384, f * 512 : (f + 1) * 512]
        else:
            frame = by_tm[:, (f - 3) * 512 : (f - 2) * 512]
        top[:, f * COLS : (f + 1) * COLS] = frame[:, :COLS]
        bot[:, f * COLS : (f + 1) * COLS] = frame[:, 3 * COLS :]


def turn_weights_kernel(src, out, done):
    done[...] = jnp.zeros(done.shape, F32)

    def turned(tap):
        wide = jnp.concatenate([src[26 - tap].astype(F32), jnp.zeros((64, 192), F32)], axis=0)
        wide = jnp.concatenate([wide, jnp.zeros((256, 64), F32)], axis=1).T
        return wide[:192, :192].astype(BF)

    for q in range(3):
        for ab in range(0, 9, 2):
            left = turned(ab * 3 + q)
            right = turned((ab + 1) * 3 + q) if ab < 8 else jnp.zeros((192, 64), BF)
            pair = jnp.concatenate([left, right], axis=1)
            out[q * 192 : (q + 1) * 192, ab * 192 : ab * 192 + pair.shape[1]] = pair


def add_kernel(kept, *rest):
    got, out = rest[:-1], rest[-1]
    size = got[0].shape[0]
    for i, piece in enumerate(got):
        rows = slice(i * size, (i + 1) * size)
        out[rows, :] = (kept[rows, :].astype(F32) + piece[...].astype(F32)).astype(BF)


def gain_lines(total):
    return total[0:2] + total[2:4]


def gain_block(lines):
    high = lines.astype(BF).astype(F32)
    return jnp.concatenate([high, lines - high, jnp.zeros((12, COLS), F32)], axis=0).astype(BF)


def sum_of(got, rows):
    total = got[0, rows, :].astype(F32)
    for i in range(1, got.shape[0]):
        total += got[i, rows, :].astype(F32)
    return total


def share_kernel(got, lines, out):
    share = got.shape[1]
    total = sum_of(got, slice(0, share)).astype(BF)
    block = gain_block(lines[...])
    for i in range(out.shape[0]):
        out[i, :share, :] = total
        out[i, share:, :] = block


def gather_kernel(got, out):
    share = got.shape[1] - 16
    total = sum_of(got, slice(0, share)).astype(BF)
    block = gain_block(gain_lines(sum_of(got, slice(share, share + 16))))
    for i in range(out.shape[0]):
        out[i, :share, :] = total
        out[i, share:, :] = block


def hidden_kernel(own, by_tm, top, bot, gain, out, factor, done):
    done[...] = jnp.zeros(done.shape, F32)
    for fe in range(5):
        if fe < 2:
            x = by_tm[:, fe * 768 : (fe + 1) * 768].astype(F32)
        else:
            f = fe - 2
            mid = own[:, f * 512 : (f + 1) * 512]
            above = top[:, f * COLS : (f + 1) * COLS]
            below = bot[:, f * COLS : (f + 1) * COLS]
            x = jnp.concatenate([above, mid, below], axis=1).astype(F32)
        normed = x * lax.rsqrt(jnp.mean(x * x, axis=0, keepdims=True) + EPSILON)
        preact = normed * gain[...]
        s = jax.nn.sigmoid(preact)
        for value, to in ((preact * s, out), (s * (1.0 + preact * (1.0 - s)) * normed, factor)):
            wide = jnp.concatenate([value, jnp.zeros((64, 768), F32)], axis=0)
            to[fe * 768 : (fe + 1) * 768, :] = wide.T[:, :192].astype(BF)


def window(ext, ab):
    a, b = divmod(ab, 3)
    parts = [ext[((f + a) * 6 + b) * COLS : ((f + a) * 6 + b + 4) * COLS, :] for f in range(3)]
    return jnp.concatenate(parts, axis=0)


def gain_kernel(cot3, factor, weights, out):
    total = jnp.zeros((1, 192), F32)
    for ab in range(9):
        part = jnp.dot(cot3[...], window(factor, ab), preferred_element_type=F32)
        for q in range(3):
            term = part[q * 192 : (q + 1) * 192] * weights[ab * 3 + q].astype(F32)
            total += jnp.sum(term, axis=0, keepdims=True)
    wide = jnp.concatenate([total, jnp.zeros((1, 64), F32)], axis=1)
    out[0:1, :] = wide[:, :COLS]
    out[1:2, :] = wide[:, COLS:]


def weight_kernel(clip, cot3, hid, keep, *rest):
    give, out = rest[:-1], rest[-1]
    held = None
    for ab in range(9):
        right = window(hid, ab)
        part = jnp.dot(cot3[...], right, preferred_element_type=F32).astype(BF)
        out[ab * 576 : (ab + 1) * 576, :] = part[:, :COLS]
        rest = part[:, COLS:192]
        if ab == 8:
            out[MAIN + 4 * 576 : MAIN + 4 * 576 + 288, :] = jnp.concatenate([rest[:288], rest[288:]], axis=1)
        elif ab % 2:
            at = MAIN + (ab // 2) * 576
            out[at : at + 576, :] = jnp.concatenate([held, rest], axis=1)
        else:
            held = rest
    done = MAIN + MAIN // 2
    out[done:, :] = jnp.zeros((out.shape[0] - done, COLS), BF)
    half = out.shape[0] // 2
    keep[...] = out[pl.ds(pl.multiple_of(clip[0] * half, half), half), :]
    size = half // len(give)
    for i, piece in enumerate(give):
        piece[...] = out[pl.ds(pl.multiple_of((1 - clip[0]) * half + i * size, size), size), :]


def input_kernel(own, gain, cot3, by_tm, top, bot, weights, out, ext, rhs):
    for fe in range(5):
        lo = fe * 768
        ext[:, lo : lo + COLS] = top[:, fe * COLS : (fe + 1) * COLS]
        if fe < 3:
            ext[:, lo + COLS : lo + 5 * COLS] = cot3[192:384, fe * 512 : (fe + 1) * 512]
        else:
            ext[:, lo + COLS : lo + 5 * COLS] = by_tm[:, (fe - 3) * 512 : (fe - 2) * 512]
        ext[:, lo + 5 * COLS : lo + 6 * COLS] = bot[:, fe * COLS : (fe + 1) * COLS]
    rhs[1728:, :] = jnp.zeros((64, 512), BF)
    for f in range(3):
        for ab in range(9):
            a, b = divmod(ab, 3)
            lo = ((f + a) * 6 + b) * COLS
            rhs[ab * 192 : (ab + 1) * 192, :] = ext[:, lo : lo + 512]
        spread = jnp.dot(weights[...], rhs[...], preferred_element_type=F32)
        grad = sideways(spread[0:192], 1) + spread[192:384] + sideways(spread[384:576], -1)
        x = own[:, f * 512 : (f + 1) * 512].astype(F32)
        inverse = lax.rsqrt(jnp.mean(x * x, axis=0, keepdims=True) + EPSILON)
        normed = x * inverse
        preact = normed * gain[...]
        s = jax.nn.sigmoid(preact)
        preact_grad = grad * s * (1.0 + preact * (1.0 - s))
        projection = jnp.mean(preact_grad * normed * gain[...], axis=0, keepdims=True)
        cot = cot3[192:384, f * 512 : (f + 1) * 512].astype(F32)
        result = inverse * (preact_grad * gain[...] - normed * projection) + cot
        out[:, f * 512 : (f + 1) * 512] = result.astype(BF)


def final_kernel(scale, clip, mine, other, out, gain_out, buf):
    n, share = mine.shape[0], mine.shape[1] - 16
    at = clip[0]
    gains = jnp.zeros((2, COLS), F32)
    for held, half in ((mine, at), (other, 1 - at)):
        for i in range(n):
            rows = pl.ds(pl.multiple_of(half * (n * share) + i * share, share), share)
            buf[rows, :] = held[i, :share, :]
            gains += gain_lines(held[i, share:, :].astype(F32))
    gain_out[...] = gains * scale
    for tap in range(27):
        ab, q = divmod(tap, 3)
        main = buf[tap * 192 : (tap + 1) * 192, :].astype(F32)
        if ab < 8:
            row = MAIN + (ab // 2) * 576 + q * 192
            side = buf[row : row + 192, :].astype(F32)
            side = side[:, 64 * (ab % 2) : 64 * (ab % 2) + 64]
        else:
            row = MAIN + 4 * 576
            first, second = buf[row : row + 288, 0:64].astype(F32), buf[row : row + 288, 64:128].astype(F32)
            if q == 0:
                side = first[0:192]
            elif q == 1:
                side = jnp.concatenate([first[192:288], second[0:96]], axis=0)
            else:
                side = second[96:288]
        out[tap, :, :] = jnp.concatenate([main, side], axis=1) * scale


def shifted(shard, axis, by):
    count = lax.axis_size(axis)
    return lax.ppermute(shard, axis, [(i, i + by) for i in range(count) if 0 <= i + by < count])


def exchange(x, axis):
    return lax.all_to_all(x, axis, split_axis=0, concat_axis=0, tiled=True)


def shards(activations, norm_gain, conv_weights, packed_grads, piece_lengths):
    n_tm, n_rows, n_clip = lax.axis_size("tm"), lax.axis_size("rows"), lax.axis_size("clip")
    channels, frames, row_count, col_count = activations.shape[1:]
    voxels = frames * row_count * col_count
    owners = piece_lengths.shape[2]
    width = packed_grads.shape[3]
    capacity = width // channels
    grad_scale = 1.0 / math.sqrt(voxels * n_tm * n_rows * n_clip)
    gain_col = norm_gain[:, None]

    packed = packed_grads.reshape(owners, width)
    own = activations.reshape(channels, voxels)
    a_top, a_bot = call(edges_kernel, [((channels, 384), BF)] * 2, own)
    act_bot = shifted(a_top, "rows", -1)
    act_top = shifted(a_bot, "rows", 1)
    sent = chunk_rows(packed).reshape(owners, width // 512, 4, COLS)
    arrived = exchange(sent, ("tm", "rows")).reshape(owners * width // COLS, COLS)
    a_frames = call(frames_kernel, [((channels, 1536), BF)], own, act_top, act_bot)[0]
    act_tm = shifted(a_frames, "tm", 1)
    flag = ((8, COLS), F32)
    extended = ((30 * COLS, channels), BF)
    hid, factor, had_hid = call(
        hidden_kernel, [extended, extended, flag], own, act_tm, act_top, act_bot, gain_col
    )
    taps = conv_weights.transpose(1, 0, 2)
    weights, had_weights = call(turn_weights_kernel, [((576, 1792), BF), flag], taps)

    cot3, c_frames = unpack(arrived, piece_lengths.reshape(1, owners), capacity, (had_hid, had_weights))
    cot_tm = shifted(c_frames, "tm", -1)

    clip = lax.axis_index("clip").astype(jnp.int32).reshape(1)
    swap_clip = [(0, 1), (1, 0)]
    outs = [((4096, COLS), BF)] + [((4096 // GIVEN, COLS), BF)] * GIVEN
    keep, *give = call(weight_kernel, outs, clip, cot3, hid, scratch=[pltpu.VMEM((8192, COLS), BF)])
    given = [lax.ppermute(piece, "clip", swap_clip) for piece in give]
    part = call(add_kernel, [((4096, COLS), BF)], keep, *given, after=(cot_tm,))[0]
    share = part.shape[0] // n_tm
    got = exchange(part.reshape(n_tm, share, COLS), "tm")

    gain_sum = call(gain_kernel, [((2, COLS), F32)], cot3, factor, taps)[0]

    c_top, c_bot = call(rims_kernel, [((channels, 640), BF)] * 2, cot3, cot_tm)
    cot_bot = shifted(c_top, "rows", -1)
    cot_top = shifted(c_bot, "rows", 1)
    input_grad = call(
        input_kernel,
        [((channels, voxels), BF)],
        own,
        gain_col,
        cot3,
        cot_tm,
        cot_top,
        cot_bot,
        weights,
        scratch=[pltpu.VMEM((channels, 30 * COLS), BF), pltpu.VMEM((1792, 512), BF)],
    )[0]

    had_rims = cot_top[:8, :COLS] + cot_bot[:8, :COLS]

    sent = call(share_kernel, [((n_rows, share + 16, COLS), BF)], got, gain_sum, after=(had_rims,))[0]
    got = exchange(sent, "rows")
    had_grad = input_grad[:8, :COLS]
    sent = call(gather_kernel, [((n_tm, share + 16, COLS), BF)], got, after=(had_grad,))[0]
    mine = exchange(sent, "tm")
    other = lax.ppermute(mine, "clip", swap_clip)

    def finish(*refs):
        final_kernel(grad_scale, *refs)

    weight_grad, gain_grad = call(
        finish,
        [((27, channels, channels), F32), ((2, COLS), F32)],
        clip,
        mine,
        other,
        scratch=[pltpu.VMEM((8192, COLS), BF)],
    )
    gain_grad = gain_grad.reshape(2 * COLS)[:channels]
    return (input_grad.reshape(activations.shape), weight_grad.transpose(1, 0, 2), gain_grad)


def solution(mesh):
    return jax.shard_map(
        shards,
        mesh=mesh,
        in_specs=(
            P("clip", None, "tm", "rows", None),
            P(),
            P(),
            P("clip", ("tm", "rows"), None, None),
            P("clip", ("tm", "rows"), None),
        ),
        out_specs=(P("clip", None, "tm", "rows", None), P(), P()),
        check_vma=False,
    )
```

```python
import math

import jax
import jax.numpy as jnp
from jax import lax
from jax.experimental import pallas as pl
from jax.experimental.pallas import tpu as pltpu
from jax.sharding import PartitionSpec as P

EPSILON = 1e-06
BF = jnp.bfloat16
F32 = jnp.float32
COLS = 128
MAIN = 5184
GIVEN = 4


def call(body, outs, *args, scratch=(), after=()):
    outs = [jax.ShapeDtypeStruct(s, d) for s, d in outs]
    spec = pl.BlockSpec(memory_space=pltpu.VMEM)

    def after_them(*refs):
        body(*refs[len(after) :])

    return pl.pallas_call(
        after_them,
        out_shape=outs,
        in_specs=[pl.BlockSpec(memory_space=pl.ANY)] * len(after)
        + [pl.BlockSpec(memory_space=pltpu.SMEM) if a.ndim == 1 else spec for a in args],
        out_specs=[spec] * len(outs),
        scratch_shapes=list(scratch),
        compiler_params=pltpu.CompilerParams(vmem_limit_bytes=16 << 20),
    )(*after, *args)


def chunk_rows(packed):
    rows, width = packed.shape
    parts = width // COLS

    def body(src, out, wide):
        for j in range(parts):
            wide[pl.ds(j, rows, stride=parts), :] = src[:, j * COLS : (j + 1) * COLS].astype(F32)
        out[...] = wide[...].astype(BF)

    return call(body, [((rows * parts, COLS), BF)], packed, scratch=[pltpu.VMEM((rows * parts, COLS), F32)])[0]


def sideways(x, by):
    lanes = lax.broadcasted_iota(jnp.int32, (x.shape[0], COLS), 1)
    edge = 0 if by == 1 else COLS - 1
    parts = []
    for lo in range(0, x.shape[1], COLS):
        turned = pltpu.roll(x[:, lo : lo + COLS], by % COLS, 1)
        parts.append(jnp.where(lanes == edge, 0.0, turned))
    return jnp.concatenate(parts, axis=1)


def place(lengths, owner):
    owners = owner.shape[0]
    other = lax.broadcasted_iota(jnp.int32, (owners, owners), 1)
    held = jnp.broadcast_to(lengths[...], (owners, owners)).astype(F32)
    begins = jnp.sum(jnp.where(other < owner, held, 0.0), axis=1, keepdims=True)
    count = jnp.sum(jnp.where(other == owner, held, 0.0), axis=1, keepdims=True)
    return begins, count


def unpack_body(capacity, arrived, lengths, cot3, to_tm, top, bot, wide, turned):
    owners = lengths.shape[1]
    parts = arrived.shape[0] // owners
    channels = parts * COLS // capacity
    begins, count = place(lengths, lax.broadcasted_iota(jnp.int32, (owners, owners), 0))
    wide[...] = arrived[...].astype(F32)
    for j in range(parts):
        turned[j * COLS : (j + 1) * COLS, :] = wide[pl.ds(j, owners, stride=parts), :].T.astype(BF)
    group = capacity // 3
    for f in range(3):
        voxel = lax.broadcasted_iota(jnp.int32, (owners, 512), 1).astype(F32) + float(f * 512)
        slot = voxel - begins
        slot = jnp.where((slot >= 0.0) & (slot < count), slot, -1.0).astype(BF)
        total = jnp.zeros((channels, 512), F32)
        for k in range(0, capacity, group):
            left = jnp.concatenate(
                [turned[(k + i) * channels : (k + i + 1) * channels, :] for i in range(group)], axis=1
            )
            right = jnp.concatenate(
                [jnp.where(slot == jnp.asarray(k + i, BF), jnp.asarray(1, BF), jnp.asarray(0, BF)) for i in range(group)],
                axis=0,
            )
            total += jnp.dot(left, right, preferred_element_type=F32)
        lo = f * 512
        cot = total.astype(BF)
        cot3[0:channels, lo : lo + 512] = sideways(total, -1).astype(BF)
        cot3[channels : 2 * channels, lo : lo + 512] = cot
        cot3[2 * channels : 3 * channels, lo : lo + 512] = sideways(total, 1).astype(BF)
        top[:, f * COLS : (f + 1) * COLS] = cot[:, :COLS]
        bot[:, f * COLS : (f + 1) * COLS] = cot[:, 3 * COLS :]
        if f < 2:
            to_tm[:, lo : lo + 512] = cot


def unpack(arrived, lengths, capacity, after):
    owners = lengths.shape[1]
    size = arrived.shape[0] * COLS // owners
    channels = size // capacity

    def body(*refs):
        unpack_body(capacity, *refs)

    return call(
        body,
        [((3 * channels, 1536), BF), ((channels, 1024), BF), ((channels, 384), BF), ((channels, 384), BF)],
        arrived,
        lengths,
        scratch=[pltpu.VMEM(arrived.shape, F32), pltpu.VMEM((size, owners), BF)],
        after=after,
    )


def corners_kernel(by_tm, top, bot):
    for f in range(2):
        top[:, f * COLS : (f + 1) * COLS] = by_tm[:, f * 512 : f * 512 + COLS]
        bot[:, f * COLS : (f + 1) * COLS] = by_tm[:, f * 512 + 3 * COLS : (f + 1) * 512]


def turn_weights_kernel(src, out, done):
    done[...] = jnp.zeros(done.shape, F32)

    def turned(tap):
        wide = jnp.concatenate([src[26 - tap].astype(F32), jnp.zeros((64, 192), F32)], axis=0)
        wide = jnp.concatenate([wide, jnp.zeros((256, 64), F32)], axis=1).T
        return wide[:192, :192].astype(BF)

    for q in range(3):
        for ab in range(0, 9, 2):
            left = turned(ab * 3 + q)
            right = turned((ab + 1) * 3 + q) if ab < 8 else jnp.zeros((192, 64), BF)
            pair = jnp.concatenate([left, right], axis=1)
            out[q * 192 : (q + 1) * 192, ab * 192 : ab * 192 + pair.shape[1]] = pair


def add_kernel(kept, *rest):
    got, out = rest[:-1], rest[-1]
    size = got[0].shape[0]
    for i, piece in enumerate(got):
        rows = slice(i * size, (i + 1) * size)
        out[rows, :] = (kept[rows, :].astype(F32) + piece[...].astype(F32)).astype(BF)


def gain_lines(total):
    return total[0:2] + total[2:4]


def gain_block(lines):
    high = lines.astype(BF).astype(F32)
    return jnp.concatenate([high, lines - high, jnp.zeros((12, COLS), F32)], axis=0).astype(BF)


def sum_of(got, rows):
    total = got[0, rows, :].astype(F32)
    for i in range(1, got.shape[0]):
        total += got[i, rows, :].astype(F32)
    return total


def share_kernel(got, lines, out):
    share = got.shape[1]
    total = sum_of(got, slice(0, share)).astype(BF)
    block = gain_block(lines[...])
    for i in range(out.shape[0]):
        out[i, :share, :] = total
        out[i, share:, :] = block


def gather_kernel(got, out):
    share = got.shape[1] - 16
    total = sum_of(got, slice(0, share)).astype(BF)
    block = gain_block(gain_lines(sum_of(got, slice(share, share + 16))))
    for i in range(out.shape[0]):
        out[i, :share, :] = total
        out[i, share:, :] = block


def hidden_kernel(first, acts, gain, out, factor, done):
    done[...] = jnp.zeros(done.shape, F32)
    for f in range(first, 3):
        lo = (f - first) * 512
        x = acts[:, f * 512 : (f + 1) * 512].astype(F32)
        normed = x * lax.rsqrt(jnp.mean(x * x, axis=0, keepdims=True) + EPSILON)
        preact = normed * gain[...]
        s = jax.nn.sigmoid(preact)
        for value, to in ((preact * s, out), (s * (1.0 + preact * (1.0 - s)) * normed, factor)):
            wide = jnp.concatenate([value, jnp.zeros((64, 512), F32)], axis=0)
            to[lo : lo + 512, :] = wide.T[:, :192].astype(BF)


def span(before, own, a):
    if a == 2:
        return own[...]
    return jnp.concatenate([before[a * 512 :, :], own[: (a + 1) * 512, :]], axis=0)


def rows_beside(cot3, top, bot, b):
    if b == 1:
        return cot3[...]
    rim = (bot if b == 0 else top)[...]
    wide = rim.astype(F32)
    rim3 = jnp.concatenate([sideways(wide, -1).astype(BF), rim, sideways(wide, 1).astype(BF)], axis=0)
    parts = []
    for f in range(3):
        edge = rim3[:, f * COLS : (f + 1) * COLS]
        if b == 0:
            parts += [cot3[:, f * 512 + COLS : (f + 1) * 512], edge]
        else:
            parts += [edge, cot3[:, f * 512 : f * 512 + 3 * COLS]]
    return jnp.concatenate(parts, axis=1)


def gain_kernel(cot3, top, bot, before, own, weights, out):
    total = jnp.zeros((1, 192), F32)
    for b in range(3):
        left = rows_beside(cot3, top, bot, b)
        for a in range(3):
            part = jnp.dot(left, span(before, own, a), preferred_element_type=F32)
            for q in range(3):
                term = part[q * 192 : (q + 1) * 192] * weights[9 * a + 3 * b + q].astype(F32)
                total += jnp.sum(term, axis=0, keepdims=True)
    wide = jnp.concatenate([total, jnp.zeros((1, 64), F32)], axis=1)
    out[0:1, :] = wide[:, :COLS]
    out[1:2, :] = wide[:, COLS:]


def middle_kernel(cot3, before, own, out):
    for a in range(3):
        part = jnp.dot(cot3[...], span(before, own, a), preferred_element_type=F32)
        out[a * 576 : (a + 1) * 576, :] = part.astype(BF)


def weight_kernel(clip, cot3, top, bot, before, own, middle, keep, *rest):
    give, out, sides = rest[:-2], rest[-2], rest[-1]
    for b in range(3):
        if b != 1:
            left = rows_beside(cot3, top, bot, b)
        for a in range(3):
            ab = 3 * a + b
            if b == 1:
                part = middle[a * 576 : (a + 1) * 576, :]
            else:
                part = jnp.dot(left, span(before, own, a), preferred_element_type=F32).astype(BF)
            out[ab * 576 : (ab + 1) * 576, :] = part[:, :COLS]
            sides[ab * 576 : (ab + 1) * 576, :] = part[:, COLS:192]
    for ab in range(0, 8, 2):
        at = MAIN + (ab // 2) * 576
        pair = [sides[(ab + i) * 576 : (ab + i + 1) * 576, :] for i in range(2)]
        out[at : at + 576, :] = jnp.concatenate(pair, axis=1)
    pair = [sides[8 * 576 + i * 288 : 8 * 576 + (i + 1) * 288, :] for i in range(2)]
    out[MAIN + 4 * 576 : MAIN + 4 * 576 + 288, :] = jnp.concatenate(pair, axis=1)
    done = MAIN + MAIN // 2
    out[done:, :] = jnp.zeros((out.shape[0] - done, COLS), BF)
    half = out.shape[0] // 2
    keep[...] = out[pl.ds(pl.multiple_of(clip[0] * half, half), half), :]
    size = half // len(give)
    for i, piece in enumerate(give):
        piece[...] = out[pl.ds(pl.multiple_of((1 - clip[0]) * half + i * size, size), size), :]


def input_kernel(own, gain, cot3, by_tm, top, bot, tops, bots, weights, out, ext, rhs):
    for fe in range(5):
        lo = fe * 768
        if fe < 3:
            f, above, below = fe, top, bot
            ext[:, lo + COLS : lo + 5 * COLS] = cot3[192:384, f * 512 : (f + 1) * 512]
        else:
            f, above, below = fe - 3, tops, bots
            ext[:, lo + COLS : lo + 5 * COLS] = by_tm[:, f * 512 : (f + 1) * 512]
        ext[:, lo : lo + COLS] = above[:, f * COLS : (f + 1) * COLS]
        ext[:, lo + 5 * COLS : lo + 6 * COLS] = below[:, f * COLS : (f + 1) * COLS]
    rhs[1728:, :] = jnp.zeros((64, 512), BF)
    for f in range(3):
        for ab in range(9):
            a, b = divmod(ab, 3)
            lo = ((f + a) * 6 + b) * COLS
            rhs[ab * 192 : (ab + 1) * 192, :] = ext[:, lo : lo + 512]
        spread = jnp.dot(weights[...], rhs[...], preferred_element_type=F32)
        grad = sideways(spread[0:192], 1) + spread[192:384] + sideways(spread[384:576], -1)
        x = own[:, f * 512 : (f + 1) * 512].astype(F32)
        inverse = lax.rsqrt(jnp.mean(x * x, axis=0, keepdims=True) + EPSILON)
        normed = x * inverse
        preact = normed * gain[...]
        s = jax.nn.sigmoid(preact)
        preact_grad = grad * s * (1.0 + preact * (1.0 - s))
        projection = jnp.mean(preact_grad * normed * gain[...], axis=0, keepdims=True)
        cot = cot3[192:384, f * 512 : (f + 1) * 512].astype(F32)
        result = inverse * (preact_grad * gain[...] - normed * projection) + cot
        out[:, f * 512 : (f + 1) * 512] = result.astype(BF)


def final_kernel(scale, clip, mine, other, out, gain_out, buf):
    n, share = mine.shape[0], mine.shape[1] - 16
    at = clip[0]
    gains = jnp.zeros((2, COLS), F32)
    for held, half in ((mine, at), (other, 1 - at)):
        for i in range(n):
            rows = pl.ds(pl.multiple_of(half * (n * share) + i * share, share), share)
            buf[rows, :] = held[i, :share, :]
            gains += gain_lines(held[i, share:, :].astype(F32))
    gain_out[...] = gains * scale
    for tap in range(27):
        ab, q = divmod(tap, 3)
        main = buf[tap * 192 : (tap + 1) * 192, :].astype(F32)
        if ab < 8:
            row = MAIN + (ab // 2) * 576 + q * 192
            side = buf[row : row + 192, :].astype(F32)
            side = side[:, 64 * (ab % 2) : 64 * (ab % 2) + 64]
        else:
            row = MAIN + 4 * 576
            first, second = buf[row : row + 288, 0:64].astype(F32), buf[row : row + 288, 64:128].astype(F32)
            if q == 0:
                side = first[0:192]
            elif q == 1:
                side = jnp.concatenate([first[192:288], second[0:96]], axis=0)
            else:
                side = second[96:288]
        out[tap, :, :] = jnp.concatenate([main, side], axis=1) * scale


def shifted(shard, axis, by):
    count = lax.axis_size(axis)
    return lax.ppermute(shard, axis, [(i, i + by) for i in range(count) if 0 <= i + by < count])


def exchange(x, axis):
    return lax.all_to_all(x, axis, split_axis=0, concat_axis=0, tiled=True)


def shards(activations, norm_gain, conv_weights, packed_grads, piece_lengths):
    n_tm, n_rows, n_clip = lax.axis_size("tm"), lax.axis_size("rows"), lax.axis_size("clip")
    channels, frames, row_count, col_count = activations.shape[1:]
    voxels = frames * row_count * col_count
    owners = piece_lengths.shape[2]
    width = packed_grads.shape[3]
    capacity = width // channels
    grad_scale = 1.0 / math.sqrt(voxels * n_tm * n_rows * n_clip)
    gain_col = norm_gain[:, None]

    packed = packed_grads.reshape(owners, width)
    sent = chunk_rows(packed).reshape(owners, width // 512, 4, COLS)
    arrived = exchange(sent, ("tm", "rows")).reshape(owners * width // COLS, COLS)

    own = activations.reshape(channels, voxels)
    acts_before = shifted(own, "tm", 1)
    flag = ((8, COLS), F32)

    def hidden_of(acts, first):
        def body(*refs):
            hidden_kernel(first, *refs)

        shape = (((3 - first) * 512, channels), BF)
        return call(body, [shape, shape, flag], acts, gain_col)

    hid, factor, had_hid = hidden_of(own, 0)
    hid_before, factor_before, _ = hidden_of(acts_before, 1)
    taps = conv_weights.transpose(1, 0, 2)
    weights, had_weights = call(turn_weights_kernel, [((576, 1792), BF), flag], taps)

    cot3, c_frames, c_top, c_bot = unpack(
        arrived, piece_lengths.reshape(1, owners), capacity, (had_hid, had_weights)
    )
    cot_tm = shifted(c_frames, "tm", -1)
    rim_bot = shifted(c_top, "rows", -1)
    rim_top = shifted(c_bot, "rows", 1)

    clip = lax.axis_index("clip").astype(jnp.int32).reshape(1)
    swap_clip = [(0, 1), (1, 0)]
    outs = [((4096, COLS), BF)] + [((4096 // GIVEN, COLS), BF)] * GIVEN
    middle = call(middle_kernel, [((1728, channels), BF)], cot3, hid_before, hid)[0]
    scratch = [pltpu.VMEM((8192, COLS), BF), pltpu.VMEM((MAIN, 64), BF)]
    keep, *give = call(
        weight_kernel, outs, clip, cot3, rim_top, rim_bot, hid_before, hid, middle, scratch=scratch
    )
    given = [lax.ppermute(piece, "clip", swap_clip) for piece in give]
    part = call(add_kernel, [((4096, COLS), BF)], keep, *given, after=(cot_tm,))[0]
    share = part.shape[0] // n_tm
    got = exchange(part.reshape(n_tm, share, COLS), "tm")

    gain_sum = call(
        gain_kernel, [((2, COLS), F32)], cot3, rim_top, rim_bot, factor_before, factor, taps
    )[0]

    t_top, t_bot = call(corners_kernel, [((channels, 256), BF)] * 2, cot_tm)
    tops = shifted(t_bot, "rows", 1)
    bots = shifted(t_top, "rows", -1)
    input_grad = call(
        input_kernel,
        [((channels, voxels), BF)],
        own,
        gain_col,
        cot3,
        cot_tm,
        rim_top,
        rim_bot,
        tops,
        bots,
        weights,
        scratch=[pltpu.VMEM((channels, 30 * COLS), BF), pltpu.VMEM((1792, 512), BF)],
    )[0]

    had_rims = tops[:8, :COLS] + bots[:8, :COLS]

    sent = call(share_kernel, [((n_rows, share + 16, COLS), BF)], got, gain_sum, after=(had_rims,))[0]
    got = exchange(sent, "rows")
    had_grad = input_grad[:8, :COLS]
    sent = call(gather_kernel, [((n_tm, share + 16, COLS), BF)], got, after=(had_grad,))[0]
    mine = exchange(sent, "tm")
    other = lax.ppermute(mine, "clip", swap_clip)

    def finish(*refs):
        final_kernel(grad_scale, *refs)

    weight_grad, gain_grad = call(
        finish,
        [((27, channels, channels), F32), ((2, COLS), F32)],
        clip,
        mine,
        other,
        scratch=[pltpu.VMEM((8192, COLS), BF)],
    )
    gain_grad = gain_grad.reshape(2 * COLS)[:channels]
    return (input_grad.reshape(activations.shape), weight_grad.transpose(1, 0, 2), gain_grad)


def solution(mesh):
    return jax.shard_map(
        shards,
        mesh=mesh,
        in_specs=(
            P("clip", None, "tm", "rows", None),
            P(),
            P(),
            P("clip", ("tm", "rows"), None, None),
            P("clip", ("tm", "rows"), None),
        ),
        out_specs=(P("clip", None, "tm", "rows", None), P(), P()),
        check_vma=False,
    )
```

```python
import math

import jax
import jax.numpy as jnp
from jax import lax
from jax.experimental import pallas as pl
from jax.experimental.pallas import tpu as pltpu
from jax.sharding import PartitionSpec as P

EPSILON = 1e-06
BF = jnp.bfloat16
F32 = jnp.float32
COLS = 128
MAIN = 5184
GIVEN = 3
DATA = 243
SHARE = 256


def call(body, outs, *args, scratch=(), after=(), far=(), far_out=False, limit=24):
    outs = [jax.ShapeDtypeStruct(s, d) for s, d in outs]
    spec = pl.BlockSpec(memory_space=pltpu.VMEM)
    anywhere = pl.BlockSpec(memory_space=pl.ANY)
    hbm = pl.BlockSpec(memory_space=pltpu.HBM)

    def after_them(*refs):
        body(*refs[len(after) :])

    return pl.pallas_call(
        after_them,
        out_shape=outs,
        in_specs=[anywhere] * len(after)
        + [hbm] * len(far)
        + [pl.BlockSpec(memory_space=pltpu.SMEM) if a.ndim == 1 else spec for a in args],
        out_specs=[hbm if far_out and i == 0 else spec for i in range(len(outs))],
        scratch_shapes=list(scratch),
        compiler_params=pltpu.CompilerParams(vmem_limit_bytes=limit << 20),
    )(*after, *far, *args)


def chunk_rows(packed):
    rows, width = packed.shape
    parts = width // COLS

    def body(src, out, wide):
        for j in range(parts):
            wide[pl.ds(j, rows, stride=parts), :] = src[:, j * COLS : (j + 1) * COLS].astype(F32)
        out[...] = wide[...].astype(BF)

    return call(body, [((rows * parts, COLS), BF)], packed, scratch=[pltpu.VMEM((rows * parts, COLS), F32)])[0]


def sideways(x, by):
    lanes = lax.broadcasted_iota(jnp.int32, (x.shape[0], COLS), 1)
    edge = 0 if by == 1 else COLS - 1
    parts = []
    for lo in range(0, x.shape[1], COLS):
        turned = pltpu.roll(x[:, lo : lo + COLS], by % COLS, 1)
        parts.append(jnp.where(lanes == edge, 0.0, turned))
    return jnp.concatenate(parts, axis=1)


def place(lengths, owner):
    owners = owner.shape[0]
    other = lax.broadcasted_iota(jnp.int32, (owners, owners), 1)
    held = jnp.broadcast_to(lengths[...], (owners, owners)).astype(F32)
    begins = jnp.sum(jnp.where(other < owner, held, 0.0), axis=1, keepdims=True)
    count = jnp.sum(jnp.where(other == owner, held, 0.0), axis=1, keepdims=True)
    return begins, count


def unpack_body(capacity, arrived, lengths, cot3, to_tm, top, bot, wide, turned):
    owners = lengths.shape[1]
    parts = arrived.shape[0] // owners
    channels = parts * COLS // capacity
    begins, count = place(lengths, lax.broadcasted_iota(jnp.int32, (owners, owners), 0))
    wide[...] = arrived[...].astype(F32)
    for j in range(parts):
        turned[j * COLS : (j + 1) * COLS, :] = wide[pl.ds(j, owners, stride=parts), :].T.astype(BF)
    group = capacity // 3
    for f in range(3):
        voxel = lax.broadcasted_iota(jnp.int32, (owners, 512), 1).astype(F32) + float(f * 512)
        slot = voxel - begins
        slot = jnp.where((slot >= 0.0) & (slot < count), slot, -1.0).astype(BF)
        total = jnp.zeros((channels, 512), F32)
        for k in range(0, capacity, group):
            left = jnp.concatenate(
                [turned[(k + i) * channels : (k + i + 1) * channels, :] for i in range(group)], axis=1
            )
            right = jnp.concatenate(
                [jnp.where(slot == jnp.asarray(k + i, BF), jnp.asarray(1, BF), jnp.asarray(0, BF)) for i in range(group)],
                axis=0,
            )
            total += jnp.dot(left, right, preferred_element_type=F32)
        lo = f * 512
        cot = total.astype(BF)
        cot3[0:channels, lo : lo + 512] = sideways(total, -1).astype(BF)
        cot3[channels : 2 * channels, lo : lo + 512] = cot
        cot3[2 * channels : 3 * channels, lo : lo + 512] = sideways(total, 1).astype(BF)
        top[:, f * COLS : (f + 1) * COLS] = cot[:, :COLS]
        bot[:, f * COLS : (f + 1) * COLS] = cot[:, 3 * COLS :]
        if f < 2:
            to_tm[:, lo : lo + 512] = cot


def unpack(arrived, lengths, capacity, after):
    owners = lengths.shape[1]
    size = arrived.shape[0] * COLS // owners
    channels = size // capacity

    def body(*refs):
        unpack_body(capacity, *refs)

    return call(
        body,
        [((3 * channels, 1536), BF), ((channels, 1024), BF), ((channels, 384), BF), ((channels, 384), BF)],
        arrived,
        lengths,
        scratch=[pltpu.VMEM(arrived.shape, F32), pltpu.VMEM((size, owners), BF)],
        after=after,
    )


def corners_kernel(by_tm, top, bot):
    for f in range(2):
        top[:, f * COLS : (f + 1) * COLS] = by_tm[:, f * 512 : f * 512 + COLS]
        bot[:, f * COLS : (f + 1) * COLS] = by_tm[:, f * 512 + 3 * COLS : (f + 1) * 512]


def turn_weights_kernel(src, out, done):
    done[...] = jnp.zeros(done.shape, F32)

    def turned(tap):
        wide = jnp.concatenate([src[26 - tap].astype(F32), jnp.zeros((64, 192), F32)], axis=0)
        wide = jnp.concatenate([wide, jnp.zeros((256, 64), F32)], axis=1).T
        return wide[:192, :192].astype(BF)

    for q in range(3):
        for ab in range(0, 9, 2):
            left = turned(ab * 3 + q)
            right = turned((ab + 1) * 3 + q) if ab < 8 else jnp.zeros((192, 64), BF)
            pair = jnp.concatenate([left, right], axis=1)
            out[q * 192 : (q + 1) * 192, ab * 192 : ab * 192 + pair.shape[1]] = pair


def add_kernel(kept, *rest):
    got, out, total = rest[:-2], rest[-2], rest[-1]
    size = got[0].shape[0]
    for i, piece in enumerate(got):
        rows = slice(i * size, (i + 1) * size)
        total[rows, :] = kept[rows, :].astype(F32) + piece[...].astype(F32)
    at = lax.broadcasted_iota(jnp.int32, (SHARE, COLS), 0)
    for i in range(out.shape[0] // SHARE):
        block = jnp.where(at < DATA, total[i * DATA : i * DATA + SHARE, :], 0.0)
        out[i * SHARE : (i + 1) * SHARE, :] = block.astype(BF)


def gain_lines(tail):
    at = DATA - SHARE + 16
    return tail[at : at + 2] + tail[at + 2 : at + 4]


def with_gain(total, lines):
    high = lines.astype(BF).astype(F32)
    low = lines - high
    at = lax.broadcasted_iota(jnp.int32, (SHARE, COLS), 0)
    for i, line in enumerate((high[0:1], high[1:2], low[0:1], low[1:2])):
        total = jnp.where(at == DATA + i, line, total)
    return total.astype(BF)


def sum_of(got):
    total = got[0].astype(F32)
    for i in range(1, got.shape[0]):
        total += got[i].astype(F32)
    return total


def share_kernel(got, lines, out):
    block = with_gain(sum_of(got), lines[...])
    for i in range(out.shape[0]):
        out[i] = block


def gather_kernel(got, out):
    total = sum_of(got)
    block = with_gain(total, gain_lines(total[SHARE - 16 :]))
    for i in range(out.shape[0]):
        out[i] = block


def hidden_kernel(acts, gain, out, factor, last, done):
    done[...] = jnp.zeros(done.shape, F32)
    for f in range(3):
        x = acts[:, f * 512 : (f + 1) * 512].astype(F32)
        normed = x * lax.rsqrt(jnp.mean(x * x, axis=0, keepdims=True) + EPSILON)
        preact = normed * gain[...]
        s = jax.nn.sigmoid(preact)
        for value, to in ((preact * s, out), (s * (1.0 + preact * (1.0 - s)) * normed, factor)):
            wide = jnp.concatenate([value, jnp.zeros((64, 512), F32)], axis=0)
            to[f * 512 : (f + 1) * 512, :] = wide.T[:, :192].astype(BF)
    for i, whole in enumerate((out, factor)):
        last[i * 1536 : i * 1536 + 1024, :] = whole[512:, :COLS]
        last[i * 1536 + 1024 : (i + 1) * 1536, :] = jnp.concatenate([whole[512:1024, COLS:], whole[1024:, COLS:]], axis=1)


def widen(last, before):
    before[:512, :] = jnp.concatenate([last[:512, :], last[1024:1536, :64]], axis=1)
    before[512:, :] = jnp.concatenate([last[512:1024, :], last[1024:1536, 64:]], axis=1)


def span(before, own, a):
    if a == 2:
        return own[...]
    return jnp.concatenate([before[a * 512 :, :], own[: (a + 1) * 512, :]], axis=0)


def rows_beside(cot3, top, bot, b):
    if b == 1:
        return cot3[...]
    rim = (bot if b == 0 else top)[...]
    wide = rim.astype(F32)
    rim3 = jnp.concatenate([sideways(wide, -1).astype(BF), rim, sideways(wide, 1).astype(BF)], axis=0)
    parts = []
    for f in range(3):
        edge = rim3[:, f * COLS : (f + 1) * COLS]
        if b == 0:
            parts += [cot3[:, f * 512 + COLS : (f + 1) * 512], edge]
        else:
            parts += [edge, cot3[:, f * 512 : f * 512 + 3 * COLS]]
    return jnp.concatenate(parts, axis=1)


def gain_kernel(far_own, far_last, far_weights, cot3, top, bot, out, own, last, weights, before, sems):
    pairs = ((far_own, own), (far_last.at[pl.ds(1536, 1536)], last), (far_weights, weights))
    copies = [pltpu.make_async_copy(src, to, sems.at[i]) for i, (src, to) in enumerate(pairs)]
    for copy in copies:
        copy.start()
    copies[0].wait()
    total = jnp.zeros((1, 192), F32)
    for step, b in enumerate((1, 0, 2)):
        left = rows_beside(cot3, top, bot, b)
        for a in (2, 1, 0):
            if step == 0 and a == 1:
                widen(last, before)
            part = jnp.dot(left, span(before, own, a), preferred_element_type=F32)
            if step == 0 and a == 2:
                copies[1].wait()
                copies[2].wait()
            for q in range(3):
                term = part[q * 192 : (q + 1) * 192] * weights[9 * a + 3 * b + q].astype(F32)
                total += jnp.sum(term, axis=0, keepdims=True)
    wide = jnp.concatenate([total, jnp.zeros((1, 64), F32)], axis=1)
    out[0:1, :] = wide[:, :COLS]
    out[1:2, :] = wide[:, COLS:]


def weight_kernel(far_own, clip, cot3, top, bot, last, keep, *rest):
    give, (out, sides, own, before, sem) = rest[:-5], rest[-5:]
    copy = pltpu.make_async_copy(far_own, own, sem)
    copy.start()
    widen(last, before)
    copy.wait()
    for b in (1, 0, 2):
        left = rows_beside(cot3, top, bot, b)
        for a in range(3):
            ab = 3 * a + b
            part = jnp.dot(left, span(before, own, a), preferred_element_type=F32).astype(BF)
            out[ab * 576 : (ab + 1) * 576, :] = part[:, :COLS]
            sides[ab * 576 : (ab + 1) * 576, :] = part[:, COLS:192]
    for ab in range(0, 8, 2):
        at = MAIN + (ab // 2) * 576
        pair = [sides[(ab + i) * 576 : (ab + i + 1) * 576, :] for i in range(2)]
        out[at : at + 576, :] = jnp.concatenate(pair, axis=1)
    pair = [sides[8 * 576 + i * 288 : 8 * 576 + (i + 1) * 288, :] for i in range(2)]
    out[MAIN + 4 * 576 : MAIN + 4 * 576 + 288, :] = jnp.concatenate(pair, axis=1)
    half = out.shape[0] // 2
    keep[...] = out[pl.ds(pl.multiple_of(clip[0] * half, 16), half), :]
    size = half // len(give)
    for i, piece in enumerate(give):
        piece[...] = out[pl.ds(pl.multiple_of((1 - clip[0]) * half + i * size, 16), size), :]


def input_kernel(own, gain, cot3, by_tm, top, bot, tops, bots, weights, out, ext, rhs):
    for fe in range(5):
        lo = fe * 768
        if fe < 3:
            f, above, below = fe, top, bot
            ext[:, lo + COLS : lo + 5 * COLS] = cot3[192:384, f * 512 : (f + 1) * 512]
        else:
            f, above, below = fe - 3, tops, bots
            ext[:, lo + COLS : lo + 5 * COLS] = by_tm[:, f * 512 : (f + 1) * 512]
        ext[:, lo : lo + COLS] = above[:, f * COLS : (f + 1) * COLS]
        ext[:, lo + 5 * COLS : lo + 6 * COLS] = below[:, f * COLS : (f + 1) * COLS]
    rhs[1728:, :] = jnp.zeros((64, 512), BF)
    for f in range(3):
        for ab in range(9):
            a, b = divmod(ab, 3)
            lo = ((f + a) * 6 + b) * COLS
            rhs[ab * 192 : (ab + 1) * 192, :] = ext[:, lo : lo + 512]
        spread = jnp.dot(weights[...], rhs[...], preferred_element_type=F32)
        grad = sideways(spread[0:192], 1) + spread[192:384] + sideways(spread[384:576], -1)
        x = own[:, f * 512 : (f + 1) * 512].astype(F32)
        inverse = lax.rsqrt(jnp.mean(x * x, axis=0, keepdims=True) + EPSILON)
        normed = x * inverse
        preact = normed * gain[...]
        s = jax.nn.sigmoid(preact)
        preact_grad = grad * s * (1.0 + preact * (1.0 - s))
        projection = jnp.mean(preact_grad * normed * gain[...], axis=0, keepdims=True)
        cot = cot3[192:384, f * 512 : (f + 1) * 512].astype(F32)
        result = inverse * (preact_grad * gain[...] - normed * projection) + cot
        out[:, f * 512 : (f + 1) * 512] = result.astype(BF)


def final_kernel(scale, clip, mine, other, far_out, gain_out, buf, out, sems):
    n = mine.shape[0]
    first = clip[0] == 0
    gains = jnp.zeros((2, COLS), F32)
    for half in range(2):
        for i in range(n):
            one, two = (mine, other) if half == 0 else (other, mine)
            block = jnp.where(first, one[i].astype(F32), two[i].astype(F32))
            at = (half * n + i) * DATA
            buf[at : at + SHARE, :] = block
            gains += gain_lines(block[SHARE - 16 :])
    gain_out[...] = gains * scale
    copies = []
    for tap in range(27):
        ab, q = divmod(tap, 3)
        main = buf[tap * 192 : (tap + 1) * 192, :]
        if ab < 8:
            row = MAIN + (ab // 2) * 576 + q * 192
            side = buf[row : row + 192, 64 * (ab % 2) : 64 * (ab % 2) + 64]
        else:
            row = MAIN + 4 * 576
            first, second = buf[row : row + 288, 0:64], buf[row : row + 288, 64:128]
            if q == 0:
                side = first[0:192]
            elif q == 1:
                side = jnp.concatenate([first[192:288], second[0:96]], axis=0)
            else:
                side = second[96:288]
        out[tap, :, :] = jnp.concatenate([main, side], axis=1) * scale
        if q == 2:
            taps = pl.ds(ab * 3, 3)
            copies.append(pltpu.make_async_copy(out.at[taps], far_out.at[taps], sems.at[ab]))
            copies[-1].start()
    for copy in copies:
        copy.wait()


def shifted(shard, axis, by):
    count = lax.axis_size(axis)
    return lax.ppermute(shard, axis, [(i, i + by) for i in range(count) if 0 <= i + by < count])


def exchange(x, axis):
    return lax.all_to_all(x, axis, split_axis=0, concat_axis=0, tiled=True)


def shards(activations, norm_gain, conv_weights, packed_grads, piece_lengths):
    n_tm, n_rows, n_clip = lax.axis_size("tm"), lax.axis_size("rows"), lax.axis_size("clip")
    channels, frames, row_count, col_count = activations.shape[1:]
    voxels = frames * row_count * col_count
    owners = piece_lengths.shape[2]
    width = packed_grads.shape[3]
    capacity = width // channels
    grad_scale = 1.0 / math.sqrt(voxels * n_tm * n_rows * n_clip)
    gain_col = norm_gain[:, None]

    packed = packed_grads.reshape(owners, width)
    sent = chunk_rows(packed).reshape(owners, width // 512, 4, COLS)
    arrived = exchange(sent, ("tm", "rows")).reshape(owners * width // COLS, COLS)

    own = activations.reshape(channels, voxels)
    flag = ((8, COLS), F32)
    whole = ((voxels, channels), BF)
    hid, factor, last, had_hid = call(
        hidden_kernel, [whole, whole, ((2 * voxels, COLS), BF), flag], own, gain_col
    )
    before = shifted(last, "tm", 1)
    taps = conv_weights.transpose(1, 0, 2)
    weights, had_weights = call(turn_weights_kernel, [((576, 1792), BF), flag], taps)

    cot3, c_frames, c_top, c_bot = unpack(
        arrived, piece_lengths.reshape(1, owners), capacity, (had_hid, had_weights)
    )
    cot_tm = shifted(c_frames, "tm", -1)
    rim_bot = shifted(c_top, "rows", -1)
    rim_top = shifted(c_bot, "rows", 1)

    clip = lax.axis_index("clip").astype(jnp.int32).reshape(1)
    swap_clip = [(0, 1), (1, 0)]
    half = (MAIN + MAIN // 2) // n_clip
    outs = [((half, COLS), BF)] + [((half // GIVEN, COLS), BF)] * GIVEN
    scratch = [pltpu.VMEM((n_clip * half, COLS), BF), pltpu.VMEM((MAIN, 64), BF)]
    two_frames = pltpu.VMEM((1024, channels), BF)
    scratch += [pltpu.VMEM((voxels, channels), BF), two_frames, pltpu.SemaphoreType.DMA(())]
    keep, *give = call(
        weight_kernel, outs, clip, cot3, rim_top, rim_bot, before, far=(hid,), scratch=scratch, limit=24
    )
    given = [lax.ppermute(piece, "clip", swap_clip) for piece in give]
    scratch = [pltpu.VMEM((half + 16, COLS), F32)]
    part = call(
        add_kernel, [((n_tm * SHARE, COLS), BF)], keep, *given, scratch=scratch, after=(cot_tm,)
    )[0]
    got = exchange(part.reshape(n_tm, SHARE, COLS), "tm")

    scratch = [pltpu.VMEM((voxels, channels), BF), pltpu.VMEM((voxels, COLS), BF)]
    scratch += [pltpu.VMEM(taps.shape, BF), two_frames, pltpu.SemaphoreType.DMA((3,))]
    gain_sum = call(
        gain_kernel,
        [((2, COLS), F32)],
        cot3,
        rim_top,
        rim_bot,
        far=(factor, before, taps),
        limit=58,
        scratch=scratch,
    )[0]

    t_top, t_bot = call(corners_kernel, [((channels, 256), BF)] * 2, cot_tm)
    tops = shifted(t_bot, "rows", 1)
    bots = shifted(t_top, "rows", -1)
    input_grad = call(
        input_kernel,
        [((channels, voxels), BF)],
        own,
        gain_col,
        cot3,
        cot_tm,
        rim_top,
        rim_bot,
        tops,
        bots,
        weights,
        scratch=[pltpu.VMEM((channels, 30 * COLS), BF), pltpu.VMEM((1792, 512), BF)],
    )[0]

    had_rims = tops[:8, :COLS] + bots[:8, :COLS]

    sent = call(share_kernel, [((n_rows, SHARE, COLS), BF)], got, gain_sum, after=(had_rims,))[0]
    got = exchange(sent, "rows")
    had_grad = input_grad[:8, :COLS]
    sent = call(gather_kernel, [((n_tm, SHARE, COLS), BF)], got, after=(had_grad,))[0]
    mine = exchange(sent, "tm")
    other = lax.ppermute(mine, "clip", swap_clip)

    def finish(*refs):
        final_kernel(grad_scale, *refs)

    shape = (27, channels, channels)
    scratch = [pltpu.VMEM((n_clip * half + 16, COLS), F32), pltpu.VMEM(shape, F32), pltpu.SemaphoreType.DMA((9,))]
    weight_grad, gain_grad = call(
        finish, [(shape, F32), ((2, COLS), F32)], clip, mine, other, scratch=scratch, far_out=True
    )
    gain_grad = gain_grad.reshape(2 * COLS)[:channels]
    return (input_grad.reshape(activations.shape), weight_grad.transpose(1, 0, 2), gain_grad)


def solution(mesh):
    return jax.shard_map(
        shards,
        mesh=mesh,
        in_specs=(
            P("clip", None, "tm", "rows", None),
            P(),
            P(),
            P("clip", ("tm", "rows"), None, None),
            P("clip", ("tm", "rows"), None),
        ),
        out_specs=(P("clip", None, "tm", "rows", None), P(), P()),
        check_vma=False,
    )
```

```python
import math

import jax
import jax.numpy as jnp
from jax import lax
from jax.experimental import pallas as pl
from jax.experimental.pallas import tpu as pltpu
from jax.sharding import PartitionSpec as P

EPSILON = 1e-06
BF = jnp.bfloat16
F32 = jnp.float32
COLS = 128
MAIN = 5184
GIVEN = 3
DATA = 243
STEPS = 8
SHARE = 256


def call(body, outs, *args, scratch=(), after=(), far=(), far_out=False, limit=24):
    outs = [jax.ShapeDtypeStruct(s, d) for s, d in outs]
    spec = pl.BlockSpec(memory_space=pltpu.VMEM)
    anywhere = pl.BlockSpec(memory_space=pl.ANY)
    hbm = pl.BlockSpec(memory_space=pltpu.HBM)

    def after_them(*refs):
        body(*refs[len(after) :])

    return pl.pallas_call(
        after_them,
        out_shape=outs,
        in_specs=[anywhere] * len(after)
        + [hbm] * len(far)
        + [pl.BlockSpec(memory_space=pltpu.SMEM) if a.ndim == 1 else spec for a in args],
        out_specs=[hbm if far_out and i == 0 else spec for i in range(len(outs))],
        scratch_shapes=list(scratch),
        compiler_params=pltpu.CompilerParams(vmem_limit_bytes=limit << 20),
    )(*after, *far, *args)


def chunk_rows(packed):
    rows, width = packed.shape
    parts = width // COLS
    size = rows // STEPS

    def body(src, out, came, wide, goes, in_sems, out_sems):
        ins = [
            pltpu.make_async_copy(src.at[pl.ds(g * size, size)], came.at[pl.ds(g * size, size)], in_sems.at[g])
            for g in range(STEPS)
        ]
        for copy in ins:
            copy.start()
        outs = []
        for g in range(STEPS):
            ins[g].wait()
            at = g * size * parts
            for j in range(parts):
                block = came[g * size : (g + 1) * size, j * COLS : (j + 1) * COLS]
                wide[pl.ds(at + j, size, stride=parts), :] = block.astype(F32)
            goes[at : at + size * parts, :] = wide[at : at + size * parts, :].astype(BF)
            to = pl.ds(at, size * parts)
            outs.append(pltpu.make_async_copy(goes.at[to], out.at[to], out_sems.at[g]))
            outs[-1].start()
        for copy in outs:
            copy.wait()

    long = (rows * parts, COLS)
    sems = pltpu.SemaphoreType.DMA((STEPS,))
    scratch = [pltpu.VMEM(packed.shape, BF), pltpu.VMEM(long, F32), pltpu.VMEM(long, BF), sems, sems]
    return call(body, [(long, BF)], far=(packed,), far_out=True, scratch=scratch, limit=60)[0]


def sideways(x, by):
    lanes = lax.broadcasted_iota(jnp.int32, (x.shape[0], COLS), 1)
    edge = 0 if by == 1 else COLS - 1
    parts = []
    for lo in range(0, x.shape[1], COLS):
        turned = pltpu.roll(x[:, lo : lo + COLS], by % COLS, 1)
        parts.append(jnp.where(lanes == edge, 0.0, turned))
    return jnp.concatenate(parts, axis=1)


def place(lengths, owner):
    owners = owner.shape[0]
    other = lax.broadcasted_iota(jnp.int32, (owners, owners), 1)
    held = jnp.broadcast_to(lengths[...], (owners, owners)).astype(F32)
    begins = jnp.sum(jnp.where(other < owner, held, 0.0), axis=1, keepdims=True)
    count = jnp.sum(jnp.where(other == owner, held, 0.0), axis=1, keepdims=True)
    return begins, count


def unpack_body(capacity, arrived, lengths, cot3, to_tm, top, bot, wide, turned):
    owners = lengths.shape[1]
    parts = arrived.shape[0] // owners
    channels = parts * COLS // capacity
    begins, count = place(lengths, lax.broadcasted_iota(jnp.int32, (owners, owners), 0))
    wide[...] = arrived[...].astype(F32)
    for j in range(parts):
        turned[j * COLS : (j + 1) * COLS, :] = wide[pl.ds(j, owners, stride=parts), :].T.astype(BF)
    group = capacity // 3
    for f in range(3):
        voxel = lax.broadcasted_iota(jnp.int32, (owners, 512), 1).astype(F32) + float(f * 512)
        slot = voxel - begins
        slot = jnp.where((slot >= 0.0) & (slot < count), slot, -1.0).astype(BF)
        total = jnp.zeros((channels, 512), F32)
        for k in range(0, capacity, group):
            left = jnp.concatenate(
                [turned[(k + i) * channels : (k + i + 1) * channels, :] for i in range(group)], axis=1
            )
            right = jnp.concatenate(
                [jnp.where(slot == jnp.asarray(k + i, BF), jnp.asarray(1, BF), jnp.asarray(0, BF)) for i in range(group)],
                axis=0,
            )
            total += jnp.dot(left, right, preferred_element_type=F32)
        lo = f * 512
        cot = total.astype(BF)
        cot3[0:channels, lo : lo + 512] = sideways(total, -1).astype(BF)
        cot3[channels : 2 * channels, lo : lo + 512] = cot
        cot3[2 * channels : 3 * channels, lo : lo + 512] = sideways(total, 1).astype(BF)
        top[:, f * COLS : (f + 1) * COLS] = cot[:, :COLS]
        bot[:, f * COLS : (f + 1) * COLS] = cot[:, 3 * COLS :]
        if f < 2:
            to_tm[:, lo : lo + 512] = cot


def unpack(arrived, lengths, capacity, after):
    owners = lengths.shape[1]
    size = arrived.shape[0] * COLS // owners
    channels = size // capacity

    def body(*refs):
        unpack_body(capacity, *refs)

    return call(
        body,
        [((3 * channels, 1536), BF), ((channels, 1024), BF), ((channels, 384), BF), ((channels, 384), BF)],
        arrived,
        lengths,
        scratch=[pltpu.VMEM(arrived.shape, F32), pltpu.VMEM((size, owners), BF)],
        after=after,
    )


def corners_kernel(by_tm, top, bot):
    for f in range(2):
        top[:, f * COLS : (f + 1) * COLS] = by_tm[:, f * 512 : f * 512 + COLS]
        bot[:, f * COLS : (f + 1) * COLS] = by_tm[:, f * 512 + 3 * COLS : (f + 1) * 512]


def turn_weights_kernel(src, out, done):
    done[...] = jnp.zeros(done.shape, F32)

    def turned(tap):
        wide = jnp.concatenate([src[26 - tap].astype(F32), jnp.zeros((64, 192), F32)], axis=0)
        wide = jnp.concatenate([wide, jnp.zeros((256, 64), F32)], axis=1).T
        return wide[:192, :192].astype(BF)

    for q in range(3):
        for ab in range(0, 9, 2):
            left = turned(ab * 3 + q)
            right = turned((ab + 1) * 3 + q) if ab < 8 else jnp.zeros((192, 64), BF)
            pair = jnp.concatenate([left, right], axis=1)
            out[q * 192 : (q + 1) * 192, ab * 192 : ab * 192 + pair.shape[1]] = pair


def add_kernel(kept, *rest):
    got, out, total = rest[:-2], rest[-2], rest[-1]
    size = got[0].shape[0]
    for i, piece in enumerate(got):
        rows = slice(i * size, (i + 1) * size)
        total[rows, :] = kept[rows, :].astype(F32) + piece[...].astype(F32)
    at = lax.broadcasted_iota(jnp.int32, (SHARE, COLS), 0)
    for i in range(out.shape[0] // SHARE):
        block = jnp.where(at < DATA, total[i * DATA : i * DATA + SHARE, :], 0.0)
        out[i * SHARE : (i + 1) * SHARE, :] = block.astype(BF)


def gain_lines(tail):
    at = DATA - SHARE + 16
    return tail[at : at + 2] + tail[at + 2 : at + 4]


def with_gain(total, lines):
    high = lines.astype(BF).astype(F32)
    low = lines - high
    at = lax.broadcasted_iota(jnp.int32, (SHARE, COLS), 0)
    for i, line in enumerate((high[0:1], high[1:2], low[0:1], low[1:2])):
        total = jnp.where(at == DATA + i, line, total)
    return total.astype(BF)


def sum_of(got):
    total = got[0].astype(F32)
    for i in range(1, got.shape[0]):
        total += got[i].astype(F32)
    return total


def share_kernel(got, lines, out):
    block = with_gain(sum_of(got), lines[...])
    for i in range(out.shape[0]):
        out[i] = block


def gather_kernel(got, out):
    total = sum_of(got)
    block = with_gain(total, gain_lines(total[SHARE - 16 :]))
    for i in range(out.shape[0]):
        out[i] = block


def hidden_kernel(acts, gain, out, factor, last, done):
    done[...] = jnp.zeros(done.shape, F32)
    for f in range(3):
        x = acts[:, f * 512 : (f + 1) * 512].astype(F32)
        normed = x * lax.rsqrt(jnp.mean(x * x, axis=0, keepdims=True) + EPSILON)
        preact = normed * gain[...]
        s = jax.nn.sigmoid(preact)
        for value, to in ((preact * s, out), (s * (1.0 + preact * (1.0 - s)) * normed, factor)):
            wide = jnp.concatenate([value, jnp.zeros((64, 512), F32)], axis=0)
            to[f * 512 : (f + 1) * 512, :] = wide.T[:, :192].astype(BF)
    for i, whole in enumerate((out, factor)):
        last[i * 1536 : i * 1536 + 1024, :] = whole[512:, :COLS]
        last[i * 1536 + 1024 : (i + 1) * 1536, :] = jnp.concatenate([whole[512:1024, COLS:], whole[1024:, COLS:]], axis=1)


def widen(last, before):
    before[:512, :] = jnp.concatenate([last[:512, :], last[1024:1536, :64]], axis=1)
    before[512:, :] = jnp.concatenate([last[512:1024, :], last[1024:1536, 64:]], axis=1)


def span(before, own, a):
    if a == 2:
        return own[...]
    return jnp.concatenate([before[a * 512 :, :], own[: (a + 1) * 512, :]], axis=0)


def rows_beside(cot3, top, bot, b):
    if b == 1:
        return cot3[...]
    rim = (bot if b == 0 else top)[...]
    wide = rim.astype(F32)
    rim3 = jnp.concatenate([sideways(wide, -1).astype(BF), rim, sideways(wide, 1).astype(BF)], axis=0)
    parts = []
    for f in range(3):
        edge = rim3[:, f * COLS : (f + 1) * COLS]
        if b == 0:
            parts += [cot3[:, f * 512 + COLS : (f + 1) * 512], edge]
        else:
            parts += [edge, cot3[:, f * 512 : f * 512 + 3 * COLS]]
    return jnp.concatenate(parts, axis=1)


def gain_kernel(own, last, weights, cot3, top, bot, out, before):
    widen(last[1536:, :], before)
    total = jnp.zeros((1, 192), F32)
    for b in range(3):
        left = rows_beside(cot3, top, bot, b)
        for a in range(3):
            part = jnp.dot(left, span(before, own, a), preferred_element_type=F32)
            for q in range(3):
                term = part[q * 192 : (q + 1) * 192] * weights[9 * a + 3 * b + q].astype(F32)
                total += jnp.sum(term, axis=0, keepdims=True)
    wide = jnp.concatenate([total, jnp.zeros((1, 64), F32)], axis=1)
    out[0:1, :] = wide[:, :COLS]
    out[1:2, :] = wide[:, COLS:]


def weight_kernel(clip, own, cot3, top, bot, last, keep, *rest):
    give, (out, sides, before) = rest[:-3], rest[-3:]
    widen(last[:1536, :], before)
    for b in (1, 0, 2):
        left = rows_beside(cot3, top, bot, b)
        for a in range(3):
            ab = 3 * a + b
            part = jnp.dot(left, span(before, own, a), preferred_element_type=F32).astype(BF)
            out[ab * 576 : (ab + 1) * 576, :] = part[:, :COLS]
            sides[ab * 576 : (ab + 1) * 576, :] = part[:, COLS:192]
    for ab in range(0, 8, 2):
        at = MAIN + (ab // 2) * 576
        pair = [sides[(ab + i) * 576 : (ab + i + 1) * 576, :] for i in range(2)]
        out[at : at + 576, :] = jnp.concatenate(pair, axis=1)
    pair = [sides[8 * 576 + i * 288 : 8 * 576 + (i + 1) * 288, :] for i in range(2)]
    out[MAIN + 4 * 576 : MAIN + 4 * 576 + 288, :] = jnp.concatenate(pair, axis=1)
    half = out.shape[0] // 2
    keep[...] = out[pl.ds(pl.multiple_of(clip[0] * half, 16), half), :]
    size = half // len(give)
    for i, piece in enumerate(give):
        piece[...] = out[pl.ds(pl.multiple_of((1 - clip[0]) * half + i * size, 16), size), :]


def input_kernel(own, gain, cot3, by_tm, top, bot, tops, bots, weights, out, ext, rhs):
    for fe in range(5):
        lo = fe * 768
        if fe < 3:
            f, above, below = fe, top, bot
            ext[:, lo + COLS : lo + 5 * COLS] = cot3[192:384, f * 512 : (f + 1) * 512]
        else:
            f, above, below = fe - 3, tops, bots
            ext[:, lo + COLS : lo + 5 * COLS] = by_tm[:, f * 512 : (f + 1) * 512]
        ext[:, lo : lo + COLS] = above[:, f * COLS : (f + 1) * COLS]
        ext[:, lo + 5 * COLS : lo + 6 * COLS] = below[:, f * COLS : (f + 1) * COLS]
    rhs[1728:, :] = jnp.zeros((64, 512), BF)
    for f in range(3):
        for ab in range(9):
            a, b = divmod(ab, 3)
            lo = ((f + a) * 6 + b) * COLS
            rhs[ab * 192 : (ab + 1) * 192, :] = ext[:, lo : lo + 512]
        spread = jnp.dot(weights[...], rhs[...], preferred_element_type=F32)
        grad = sideways(spread[0:192], 1) + spread[192:384] + sideways(spread[384:576], -1)
        x = own[:, f * 512 : (f + 1) * 512].astype(F32)
        inverse = lax.rsqrt(jnp.mean(x * x, axis=0, keepdims=True) + EPSILON)
        normed = x * inverse
        preact = normed * gain[...]
        s = jax.nn.sigmoid(preact)
        preact_grad = grad * s * (1.0 + preact * (1.0 - s))
        projection = jnp.mean(preact_grad * normed * gain[...], axis=0, keepdims=True)
        cot = cot3[192:384, f * 512 : (f + 1) * 512].astype(F32)
        result = inverse * (preact_grad * gain[...] - normed * projection) + cot
        out[:, f * 512 : (f + 1) * 512] = result.astype(BF)


def pack_kernel(got, out, wide):
    n = got.shape[0]
    gains = jnp.zeros((2, COLS), F32)
    for i in range(n):
        block = got[i].astype(F32)
        wide[i * DATA : i * DATA + SHARE, :] = block
        gains += gain_lines(block[SHARE - 16 :])
    high = gains.astype(BF).astype(F32)
    out[: n * DATA, :] = wide[: n * DATA, :].astype(BF)
    out[n * DATA :, :] = jnp.concatenate([high, gains - high, jnp.zeros((12, COLS), F32)], axis=0).astype(BF)


def final_kernel(scale, clip, mine, other, far_out, gain_out, buf, out, sems):
    half = mine.shape[0] - 16
    buf[pl.ds(pl.multiple_of(clip[0] * half, 16), half), :] = mine[:half, :]
    buf[pl.ds(pl.multiple_of((1 - clip[0]) * half, 16), half), :] = other[:half, :]
    tails = mine[half:, :].astype(F32) + other[half:, :].astype(F32)
    gain_out[...] = (tails[0:2] + tails[2:4]) * scale
    copies = []
    for tap in range(27):
        ab, q = divmod(tap, 3)
        main = buf[tap * 192 : (tap + 1) * 192, :].astype(F32)
        if ab < 8:
            row = MAIN + (ab // 2) * 576 + q * 192
            side = buf[row : row + 192, :].astype(F32)[:, 64 * (ab % 2) : 64 * (ab % 2) + 64]
        else:
            row = MAIN + 4 * 576
            rest = buf[row : row + 288, :].astype(F32)
            first, second = rest[:, 0:64], rest[:, 64:128]
            if q == 0:
                side = first[0:192]
            elif q == 1:
                side = jnp.concatenate([first[192:288], second[0:96]], axis=0)
            else:
                side = second[96:288]
        out[tap, :, :] = jnp.concatenate([main, side], axis=1) * scale
        if q == 2:
            taps = pl.ds(ab * 3, 3)
            copies.append(pltpu.make_async_copy(out.at[taps], far_out.at[taps], sems.at[ab]))
            copies[-1].start()
    for copy in copies:
        copy.wait()


def shifted(shard, axis, by):
    count = lax.axis_size(axis)
    return lax.ppermute(shard, axis, [(i, i + by) for i in range(count) if 0 <= i + by < count])


def exchange(x, axis):
    return lax.all_to_all(x, axis, split_axis=0, concat_axis=0, tiled=True)


def shards(activations, norm_gain, conv_weights, packed_grads, piece_lengths):
    n_tm, n_rows, n_clip = lax.axis_size("tm"), lax.axis_size("rows"), lax.axis_size("clip")
    channels, frames, row_count, col_count = activations.shape[1:]
    voxels = frames * row_count * col_count
    owners = piece_lengths.shape[2]
    width = packed_grads.shape[3]
    capacity = width // channels
    grad_scale = 1.0 / math.sqrt(voxels * n_tm * n_rows * n_clip)
    gain_col = norm_gain[:, None]

    packed = packed_grads.reshape(owners, width)
    sent = chunk_rows(packed).reshape(owners, width // 512, 4, COLS)
    arrived = exchange(sent, ("tm", "rows")).reshape(owners * width // COLS, COLS)

    own = activations.reshape(channels, voxels)
    flag = ((8, COLS), F32)
    whole = ((voxels, channels), BF)
    hid, factor, last, had_hid = call(
        hidden_kernel, [whole, whole, ((2 * voxels, COLS), BF), flag], own, gain_col
    )
    before = shifted(last, "tm", 1)
    taps = conv_weights.transpose(1, 0, 2)
    weights, had_weights = call(turn_weights_kernel, [((576, 1792), BF), flag], taps)

    cot3, c_frames, c_top, c_bot = unpack(
        arrived, piece_lengths.reshape(1, owners), capacity, (had_hid, had_weights)
    )
    cot_tm = shifted(c_frames, "tm", -1)
    rim_bot = shifted(c_top, "rows", -1)
    rim_top = shifted(c_bot, "rows", 1)

    clip = lax.axis_index("clip").astype(jnp.int32).reshape(1)
    swap_clip = [(0, 1), (1, 0)]
    half = (MAIN + MAIN // 2) // n_clip
    outs = [((half, COLS), BF)] + [((half // GIVEN, COLS), BF)] * GIVEN
    scratch = [pltpu.VMEM((n_clip * half, COLS), BF), pltpu.VMEM((MAIN, 64), BF)]
    two_frames = pltpu.VMEM((1024, channels), BF)
    scratch += [two_frames]
    keep, *give = call(
        weight_kernel, outs, clip, hid, cot3, rim_top, rim_bot, before, scratch=scratch
    )
    given = [lax.ppermute(piece, "clip", swap_clip) for piece in give]
    scratch = [pltpu.VMEM((half + 16, COLS), F32)]
    part = call(
        add_kernel, [((n_tm * SHARE, COLS), BF)], keep, *given, scratch=scratch, after=(cot_tm,)
    )[0]
    got = exchange(part.reshape(n_tm, SHARE, COLS), "tm")

    gain_sum = call(
        gain_kernel,
        [((2, COLS), F32)],
        factor,
        before,
        taps,
        cot3,
        rim_top,
        rim_bot,
        scratch=[two_frames],
    )[0]

    t_top, t_bot = call(corners_kernel, [((channels, 256), BF)] * 2, cot_tm)
    tops = shifted(t_bot, "rows", 1)
    bots = shifted(t_top, "rows", -1)
    input_grad = call(
        input_kernel,
        [((channels, voxels), BF)],
        own,
        gain_col,
        cot3,
        cot_tm,
        rim_top,
        rim_bot,
        tops,
        bots,
        weights,
        scratch=[pltpu.VMEM((channels, 30 * COLS), BF), pltpu.VMEM((1792, 512), BF)],
    )[0]

    had_rims = tops[:8, :COLS] + bots[:8, :COLS]

    sent = call(share_kernel, [((n_rows, SHARE, COLS), BF)], got, gain_sum)[0]
    got = exchange(sent, "rows")
    sent = call(gather_kernel, [((n_tm, SHARE, COLS), BF)], got, after=(had_rims,))[0]
    had_grad = input_grad[:8, :COLS]
    scratch = [pltpu.VMEM((half + 16, COLS), F32)]
    mine = call(pack_kernel, [((half + 16, COLS), BF)], exchange(sent, "tm"), scratch=scratch, after=(had_grad,))[0]
    other = lax.ppermute(mine, "clip", swap_clip)

    def finish(*refs):
        final_kernel(grad_scale, *refs)

    shape = (27, channels, channels)
    scratch = [pltpu.VMEM((n_clip * half, COLS), BF), pltpu.VMEM(shape, F32), pltpu.SemaphoreType.DMA((9,))]
    weight_grad, gain_grad = call(
        finish, [(shape, F32), ((2, COLS), F32)], clip, mine, other, scratch=scratch, far_out=True
    )
    gain_grad = gain_grad.reshape(2 * COLS)[:channels]
    return (input_grad.reshape(activations.shape), weight_grad.transpose(1, 0, 2), gain_grad)


def solution(mesh):
    return jax.shard_map(
        shards,
        mesh=mesh,
        in_specs=(
            P("clip", None, "tm", "rows", None),
            P(),
            P(),
            P("clip", ("tm", "rows"), None, None),
            P("clip", ("tm", "rows"), None),
        ),
        out_specs=(P("clip", None, "tm", "rows", None), P(), P()),
        check_vma=False,
    )
```

```python
import math

import jax
import jax.numpy as jnp
from jax import lax
from jax.experimental import pallas as pl
from jax.experimental.pallas import tpu as pltpu
from jax.sharding import PartitionSpec as P

EPSILON = 1e-06
BF = jnp.bfloat16
F32 = jnp.float32
COLS = 128
MAIN = 5184
GIVEN = 3
DATA = 243
STEPS = 8
SHARE = 256


def call(body, outs, *args, scratch=(), after=(), far=(), far_out=False, limit=24):
    outs = [jax.ShapeDtypeStruct(s, d) for s, d in outs]
    spec = pl.BlockSpec(memory_space=pltpu.VMEM)
    anywhere = pl.BlockSpec(memory_space=pl.ANY)
    hbm = pl.BlockSpec(memory_space=pltpu.HBM)

    def after_them(*refs):
        body(*refs[len(after) :])

    return pl.pallas_call(
        after_them,
        out_shape=outs,
        in_specs=[anywhere] * len(after)
        + [hbm] * len(far)
        + [pl.BlockSpec(memory_space=pltpu.SMEM) if a.ndim == 1 else spec for a in args],
        out_specs=[hbm if far_out and i == 0 else spec for i in range(len(outs))],
        scratch_shapes=list(scratch),
        compiler_params=pltpu.CompilerParams(vmem_limit_bytes=limit << 20),
    )(*after, *far, *args)


def chunk_rows(packed):
    rows, width = packed.shape
    parts = width // COLS
    size = rows // STEPS

    def body(src, out, came, wide, goes, in_sems, out_sems):
        ins = [
            pltpu.make_async_copy(src.at[pl.ds(g * size, size)], came.at[pl.ds(g * size, size)], in_sems.at[g])
            for g in range(STEPS)
        ]
        for copy in ins:
            copy.start()
        outs = []
        for g in range(STEPS):
            ins[g].wait()
            at = g * size * parts
            for j in range(parts):
                block = came[g * size : (g + 1) * size, j * COLS : (j + 1) * COLS]
                wide[pl.ds(at + j, size, stride=parts), :] = block.astype(F32)
            goes[at : at + size * parts, :] = wide[at : at + size * parts, :].astype(BF)
            to = pl.ds(at, size * parts)
            outs.append(pltpu.make_async_copy(goes.at[to], out.at[to], out_sems.at[g]))
            outs[-1].start()
        for copy in outs:
            copy.wait()

    long = (rows * parts, COLS)
    sems = pltpu.SemaphoreType.DMA((STEPS,))
    scratch = [pltpu.VMEM(packed.shape, BF), pltpu.VMEM(long, F32), pltpu.VMEM(long, BF), sems, sems]
    return call(body, [(long, BF)], far=(packed,), far_out=True, scratch=scratch, limit=60)[0]


def sideways(x, by):
    lanes = lax.broadcasted_iota(jnp.int32, (x.shape[0], COLS), 1)
    edge = 0 if by == 1 else COLS - 1
    parts = []
    for lo in range(0, x.shape[1], COLS):
        turned = pltpu.roll(x[:, lo : lo + COLS], by % COLS, 1)
        parts.append(jnp.where(lanes == edge, 0.0, turned))
    return jnp.concatenate(parts, axis=1)


def place(lengths, owner):
    owners = owner.shape[0]
    other = lax.broadcasted_iota(jnp.int32, (owners, owners), 1)
    held = jnp.broadcast_to(lengths[...], (owners, owners)).astype(F32)
    begins = jnp.sum(jnp.where(other < owner, held, 0.0), axis=1, keepdims=True)
    count = jnp.sum(jnp.where(other == owner, held, 0.0), axis=1, keepdims=True)
    return begins, count


def unpack_body(capacity, arrived, lengths, cot3, to_tm, wide, turned):
    owners = lengths.shape[1]
    parts = arrived.shape[0] // owners
    channels = parts * COLS // capacity
    begins, count = place(lengths, lax.broadcasted_iota(jnp.int32, (owners, owners), 0))
    wide[...] = arrived[...].astype(F32)
    for j in range(parts):
        turned[j * COLS : (j + 1) * COLS, :] = wide[pl.ds(j, owners, stride=parts), :].T.astype(BF)
    group = capacity // 3
    for f in range(3):
        voxel = lax.broadcasted_iota(jnp.int32, (owners, 512), 1).astype(F32) + float(f * 512)
        slot = voxel - begins
        slot = jnp.where((slot >= 0.0) & (slot < count), slot, -1.0).astype(BF)
        total = jnp.zeros((channels, 512), F32)
        for k in range(0, capacity, group):
            left = jnp.concatenate(
                [turned[(k + i) * channels : (k + i + 1) * channels, :] for i in range(group)], axis=1
            )
            right = jnp.concatenate(
                [jnp.where(slot == jnp.asarray(k + i, BF), jnp.asarray(1, BF), jnp.asarray(0, BF)) for i in range(group)],
                axis=0,
            )
            total += jnp.dot(left, right, preferred_element_type=F32)
        lo = f * 512
        cot = total.astype(BF)
        cot3[0:channels, lo : lo + 512] = sideways(total, -1).astype(BF)
        cot3[channels : 2 * channels, lo : lo + 512] = cot
        cot3[2 * channels : 3 * channels, lo : lo + 512] = sideways(total, 1).astype(BF)
        if f < 2:
            to_tm[:, lo : lo + 512] = cot


def unpack(arrived, lengths, capacity, after):
    owners = lengths.shape[1]
    size = arrived.shape[0] * COLS // owners
    channels = size // capacity

    def body(*refs):
        unpack_body(capacity, *refs)

    return call(
        body,
        [((3 * channels, 1536), BF), ((channels, 1024), BF)],
        arrived,
        lengths,
        scratch=[pltpu.VMEM(arrived.shape, F32), pltpu.VMEM((size, owners), BF)],
        after=after,
    )


def edges_kernel(own, to_tm, top, bot, dtop, dbot):
    to_tm[...] = own[:, 512:]
    for f in range(3):
        first = own[:, f * 512 : f * 512 + COLS]
        last = own[:, f * 512 + 3 * COLS : (f + 1) * 512]
        top[:, f * COLS : (f + 1) * COLS] = first
        bot[:, f * COLS : (f + 1) * COLS] = last
        if f:
            dtop[:, (f - 1) * COLS : f * COLS] = first
            dbot[:, (f - 1) * COLS : f * COLS] = last


def rims_kernel(cot3, by_tm, top, bot):
    for f in range(5):
        if f < 3:
            frame = cot3[192:384, f * 512 : (f + 1) * 512]
        else:
            frame = by_tm[:, (f - 3) * 512 : (f - 2) * 512]
        top[:, f * COLS : (f + 1) * COLS] = frame[:, :COLS]
        bot[:, f * COLS : (f + 1) * COLS] = frame[:, 3 * COLS :]


def turn_weights_kernel(src, out, done):
    done[...] = jnp.zeros(done.shape, F32)

    def turned(tap):
        wide = jnp.concatenate([src[26 - tap].astype(F32), jnp.zeros((64, 192), F32)], axis=0)
        wide = jnp.concatenate([wide, jnp.zeros((256, 64), F32)], axis=1).T
        return wide[:192, :192].astype(BF)

    for q in range(3):
        for ab in range(0, 9, 2):
            left = turned(ab * 3 + q)
            right = turned((ab + 1) * 3 + q) if ab < 8 else jnp.zeros((192, 64), BF)
            pair = jnp.concatenate([left, right], axis=1)
            out[q * 192 : (q + 1) * 192, ab * 192 : ab * 192 + pair.shape[1]] = pair


def add_kernel(kept, *rest):
    got, out, total = rest[:-2], rest[-2], rest[-1]
    size = got[0].shape[0]
    for i, piece in enumerate(got):
        rows = slice(i * size, (i + 1) * size)
        total[rows, :] = kept[rows, :].astype(F32) + piece[...].astype(F32)
    at = lax.broadcasted_iota(jnp.int32, (SHARE, COLS), 0)
    for i in range(out.shape[0] // SHARE):
        block = jnp.where(at < DATA, total[i * DATA : i * DATA + SHARE, :], 0.0)
        out[i * SHARE : (i + 1) * SHARE, :] = block.astype(BF)


def gain_lines(tail):
    at = DATA - SHARE + 16
    return tail[at : at + 2] + tail[at + 2 : at + 4]


def with_gain(total, lines):
    high = lines.astype(BF).astype(F32)
    low = lines - high
    at = lax.broadcasted_iota(jnp.int32, (SHARE, COLS), 0)
    for i, line in enumerate((high[0:1], high[1:2], low[0:1], low[1:2])):
        total = jnp.where(at == DATA + i, line, total)
    return total.astype(BF)


def sum_of(got):
    total = got[0].astype(F32)
    for i in range(1, got.shape[0]):
        total += got[i].astype(F32)
    return total


def share_kernel(got, lines, out):
    block = with_gain(sum_of(got), lines[...])
    for i in range(out.shape[0]):
        out[i] = block


def gather_kernel(got, out):
    total = sum_of(got)
    block = with_gain(total, gain_lines(total[SHARE - 16 :]))
    for i in range(out.shape[0]):
        out[i] = block


def spread_out(around, gain, out, wanted):
    own, by_tm, top, bot, dtop, dbot = around
    for fe in range(5):
        mid, above, below, f = (by_tm, dtop, dbot, fe) if fe < 2 else (own, top, bot, fe - 2)
        row = slice(f * COLS, (f + 1) * COLS)
        x = jnp.concatenate([above[:, row], mid[:, f * 512 : (f + 1) * 512], below[:, row]], axis=1).astype(F32)
        normed = x * lax.rsqrt(jnp.mean(x * x, axis=0, keepdims=True) + EPSILON)
        preact = normed * gain[...]
        value = wanted(normed, preact, jax.nn.sigmoid(preact))
        wide = jnp.concatenate([value, jnp.zeros((64, 768), F32)], axis=0)
        out[fe * 768 : (fe + 1) * 768, :] = wide.T[:, :192].astype(BF)


def window(ext, ab):
    a, b = divmod(ab, 3)
    parts = [ext[((f + a) * 6 + b) * COLS : ((f + a) * 6 + b + 4) * COLS, :] for f in range(3)]
    return jnp.concatenate(parts, axis=0)


def gain_kernel(weights, gain, cot3, *rest):
    out, factor = rest[-2:]
    spread_out(rest[:-2], gain, factor, lambda normed, preact, s: s * (1.0 + preact * (1.0 - s)) * normed)
    total = jnp.zeros((1, 192), F32)
    for ab in range(9):
        part = jnp.dot(cot3[...], window(factor, ab), preferred_element_type=F32)
        for q in range(3):
            term = part[q * 192 : (q + 1) * 192] * weights[ab * 3 + q].astype(F32)
            total += jnp.sum(term, axis=0, keepdims=True)
    wide = jnp.concatenate([total, jnp.zeros((1, 64), F32)], axis=1)
    out[0:1, :] = wide[:, :COLS]
    out[1:2, :] = wide[:, COLS:]


def weight_kernel(clip, gain, cot3, *rest):
    around, keep, give, (out, hid) = rest[:6], rest[6], rest[7:-2], rest[-2:]
    spread_out(around, gain, hid, lambda normed, preact, s: preact * s)
    held = None
    for ab in range(9):
        part = jnp.dot(cot3[...], window(hid, ab), preferred_element_type=F32).astype(BF)
        out[ab * 576 : (ab + 1) * 576, :] = part[:, :COLS]
        side = part[:, COLS:192]
        if ab == 8:
            out[MAIN + 4 * 576 : MAIN + 4 * 576 + 288, :] = jnp.concatenate([side[:288], side[288:]], axis=1)
        elif ab % 2:
            at = MAIN + (ab // 2) * 576
            out[at : at + 576, :] = jnp.concatenate([held, side], axis=1)
        else:
            held = side
    half = out.shape[0] // 2
    keep[...] = out[pl.ds(pl.multiple_of(clip[0] * half, 16), half), :]
    size = half // len(give)
    for i, piece in enumerate(give):
        piece[...] = out[pl.ds(pl.multiple_of((1 - clip[0]) * half + i * size, 16), size), :]


def input_kernel(own, gain, cot3, by_tm, top, bot, weights, out, ext, rhs):
    for fe in range(5):
        lo = fe * 768
        ext[:, lo : lo + COLS] = top[:, fe * COLS : (fe + 1) * COLS]
        if fe < 3:
            ext[:, lo + COLS : lo + 5 * COLS] = cot3[192:384, fe * 512 : (fe + 1) * 512]
        else:
            ext[:, lo + COLS : lo + 5 * COLS] = by_tm[:, (fe - 3) * 512 : (fe - 2) * 512]
        ext[:, lo + 5 * COLS : lo + 6 * COLS] = bot[:, fe * COLS : (fe + 1) * COLS]
    rhs[1728:, :] = jnp.zeros((64, 512), BF)
    for f in range(3):
        for ab in range(9):
            a, b = divmod(ab, 3)
            lo = ((f + a) * 6 + b) * COLS
            rhs[ab * 192 : (ab + 1) * 192, :] = ext[:, lo : lo + 512]
        spread = jnp.dot(weights[...], rhs[...], preferred_element_type=F32)
        grad = sideways(spread[0:192], 1) + spread[192:384] + sideways(spread[384:576], -1)
        x = own[:, f * 512 : (f + 1) * 512].astype(F32)
        inverse = lax.rsqrt(jnp.mean(x * x, axis=0, keepdims=True) + EPSILON)
        normed = x * inverse
        preact = normed * gain[...]
        s = jax.nn.sigmoid(preact)
        preact_grad = grad * s * (1.0 + preact * (1.0 - s))
        projection = jnp.mean(preact_grad * normed * gain[...], axis=0, keepdims=True)
        cot = cot3[192:384, f * 512 : (f + 1) * 512].astype(F32)
        result = inverse * (preact_grad * gain[...] - normed * projection) + cot
        out[:, f * 512 : (f + 1) * 512] = result.astype(BF)


def final_kernel(scale, clip, mine, other, far_out, gain_out, buf, out, sems):
    n = mine.shape[0]

    def build(halves):
        gains = jnp.zeros((2, COLS), F32)
        for h, half in enumerate(halves):
            for i in range(n):
                block = half[i].astype(F32)
                at = (h * n + i) * DATA
                buf[at : at + SHARE, :] = block
                gains += gain_lines(block[SHARE - 16 :])
        gain_out[...] = gains * scale

    @pl.when(clip[0] == 0)
    def _():
        build((mine, other))

    @pl.when(clip[0] != 0)
    def _():
        build((other, mine))

    copies = []
    for tap in range(27):
        ab, q = divmod(tap, 3)
        main = buf[tap * 192 : (tap + 1) * 192, :]
        if ab < 8:
            row = MAIN + (ab // 2) * 576 + q * 192
            side = buf[row : row + 192, 64 * (ab % 2) : 64 * (ab % 2) + 64]
        else:
            row = MAIN + 4 * 576
            first, second = buf[row : row + 288, 0:64], buf[row : row + 288, 64:128]
            if q == 0:
                side = first[0:192]
            elif q == 1:
                side = jnp.concatenate([first[192:288], second[0:96]], axis=0)
            else:
                side = second[96:288]
        out[tap, :, :] = jnp.concatenate([main, side], axis=1) * scale
        if q == 2:
            taps = pl.ds(ab * 3, 3)
            copies.append(pltpu.make_async_copy(out.at[taps], far_out.at[taps], sems.at[ab]))
            copies[-1].start()
    for copy in copies:
        copy.wait()


def shifted(shard, axis, by):
    count = lax.axis_size(axis)
    return lax.ppermute(shard, axis, [(i, i + by) for i in range(count) if 0 <= i + by < count])


def diagonal(shard, rows_by):
    n_tm, n_rows = lax.axis_size("tm"), lax.axis_size("rows")
    pairs = [
        (i * n_rows + j, (i + 1) * n_rows + j + rows_by)
        for i in range(n_tm - 1)
        for j in range(n_rows)
        if 0 <= j + rows_by < n_rows
    ]
    return lax.ppermute(shard, ("tm", "rows"), pairs)


def exchange(x, axis):
    return lax.all_to_all(x, axis, split_axis=0, concat_axis=0, tiled=True)


def shards(activations, norm_gain, conv_weights, packed_grads, piece_lengths):
    n_tm, n_rows, n_clip = lax.axis_size("tm"), lax.axis_size("rows"), lax.axis_size("clip")
    channels, frames, row_count, col_count = activations.shape[1:]
    voxels = frames * row_count * col_count
    owners = piece_lengths.shape[2]
    width = packed_grads.shape[3]
    capacity = width // channels
    grad_scale = 1.0 / math.sqrt(voxels * n_tm * n_rows * n_clip)
    gain_col = norm_gain[:, None]

    packed = packed_grads.reshape(owners, width)
    sent = chunk_rows(packed).reshape(owners, width // 512, 4, COLS)
    arrived = exchange(sent, ("tm", "rows")).reshape(owners * width // COLS, COLS)

    own = activations.reshape(channels, voxels)
    edge = [(channels, 1024), (channels, 384), (channels, 384), (channels, 256), (channels, 256)]
    a_tm, a_top, a_bot, a_dtop, a_dbot = call(edges_kernel, [(s, BF) for s in edge], own)
    around = (
        own,
        shifted(a_tm, "tm", 1),
        shifted(a_bot, "rows", 1),
        shifted(a_top, "rows", -1),
        diagonal(a_dbot, 1),
        diagonal(a_dtop, -1),
    )
    flag = ((8, COLS), F32)
    taps = conv_weights.transpose(1, 0, 2)
    weights, had_weights = call(turn_weights_kernel, [((576, 1792), BF), flag], taps)

    cot3, c_frames = unpack(arrived, piece_lengths.reshape(1, owners), capacity, (had_weights,))
    cot_tm = shifted(c_frames, "tm", -1)

    clip = lax.axis_index("clip").astype(jnp.int32).reshape(1)
    swap_clip = [(0, 1), (1, 0)]
    half = (MAIN + MAIN // 2) // n_clip
    outs = [((half, COLS), BF)] + [((half // GIVEN, COLS), BF)] * GIVEN
    ext = pltpu.VMEM((30 * COLS, channels), BF)
    scratch = [pltpu.VMEM((n_clip * half, COLS), BF), ext]
    keep, *give = call(weight_kernel, outs, clip, gain_col, cot3, *around, scratch=scratch)
    given = [lax.ppermute(piece, "clip", swap_clip) for piece in give]
    scratch = [pltpu.VMEM((half + 16, COLS), F32)]
    part = call(
        add_kernel, [((n_tm * SHARE, COLS), BF)], keep, *given, scratch=scratch, after=(cot_tm,)
    )[0]
    got = exchange(part.reshape(n_tm, SHARE, COLS), "tm")

    gain_sum = call(gain_kernel, [((2, COLS), F32)], taps, gain_col, cot3, *around, scratch=[ext])[0]

    c_top, c_bot = call(rims_kernel, [((channels, 640), BF)] * 2, cot3, cot_tm)
    cot_bot = shifted(c_top, "rows", -1)
    cot_top = shifted(c_bot, "rows", 1)
    input_grad = call(
        input_kernel,
        [((channels, voxels), BF)],
        own,
        gain_col,
        cot3,
        cot_tm,
        cot_top,
        cot_bot,
        weights,
        scratch=[pltpu.VMEM((channels, 30 * COLS), BF), pltpu.VMEM((1792, 512), BF)],
    )[0]

    had_rims = cot_top[:8, :COLS] + cot_bot[:8, :COLS]

    sent = call(share_kernel, [((n_rows, SHARE, COLS), BF)], got, gain_sum, after=(had_rims,))[0]
    got = exchange(sent, "rows")
    had_grad = input_grad[:8, :COLS]
    sent = call(gather_kernel, [((n_tm, SHARE, COLS), BF)], got, after=(had_grad,))[0]
    mine = exchange(sent, "tm")
    other = lax.ppermute(mine, "clip", swap_clip)

    def finish(*refs):
        final_kernel(grad_scale, *refs)

    shape = (27, channels, channels)
    scratch = [pltpu.VMEM((n_clip * half + 16, COLS), F32), pltpu.VMEM(shape, F32), pltpu.SemaphoreType.DMA((9,))]
    weight_grad, gain_grad = call(
        finish, [(shape, F32), ((2, COLS), F32)], clip, mine, other, scratch=scratch, far_out=True
    )
    gain_grad = gain_grad.reshape(2 * COLS)[:channels]
    return (input_grad.reshape(activations.shape), weight_grad.transpose(1, 0, 2), gain_grad)


def solution(mesh):
    return jax.shard_map(
        shards,
        mesh=mesh,
        in_specs=(
            P("clip", None, "tm", "rows", None),
            P(),
            P(),
            P("clip", ("tm", "rows"), None, None),
            P("clip", ("tm", "rows"), None),
        ),
        out_specs=(P("clip", None, "tm", "rows", None), P(), P()),
        check_vma=False,
    )
```

```python
import math

import jax
import jax.numpy as jnp
from jax import lax
from jax.experimental import pallas as pl
from jax.experimental.pallas import tpu as pltpu
from jax.sharding import PartitionSpec as P

EPSILON = 1e-06
BF = jnp.bfloat16
F32 = jnp.float32
COLS = 128
MAIN = 5184
GIVEN = (1328, 1328, 1312)
DATA = 248
STEPS = 8
SHARE = 256


def call(body, outs, *args, scratch=(), after=(), far=(), far_out=False, limit=24):
    outs = [jax.ShapeDtypeStruct(s, d) for s, d in outs]
    spec = pl.BlockSpec(memory_space=pltpu.VMEM)
    anywhere = pl.BlockSpec(memory_space=pl.ANY)
    hbm = pl.BlockSpec(memory_space=pltpu.HBM)

    def after_them(*refs):
        body(*refs[len(after) :])

    return pl.pallas_call(
        after_them,
        out_shape=outs,
        in_specs=[anywhere] * len(after)
        + [hbm] * len(far)
        + [pl.BlockSpec(memory_space=pltpu.SMEM) if a.ndim == 1 else spec for a in args],
        out_specs=[hbm if far_out and i == 0 else spec for i in range(len(outs))],
        scratch_shapes=list(scratch),
        compiler_params=pltpu.CompilerParams(vmem_limit_bytes=limit << 20),
    )(*after, *far, *args)


def chunk_rows(packed):
    rows, width = packed.shape
    parts = width // COLS
    size = rows // STEPS

    def body(src, out, came, wide, goes, in_sems, out_sems):
        ins = [
            pltpu.make_async_copy(src.at[pl.ds(g * size, size)], came.at[pl.ds(g * size, size)], in_sems.at[g])
            for g in range(STEPS)
        ]
        for copy in ins:
            copy.start()
        outs = []
        for g in range(STEPS):
            ins[g].wait()
            at = g * size * parts
            for j in range(parts):
                block = came[g * size : (g + 1) * size, j * COLS : (j + 1) * COLS]
                wide[pl.ds(at + j, size, stride=parts), :] = block.astype(F32)
            goes[at : at + size * parts, :] = wide[at : at + size * parts, :].astype(BF)
            to = pl.ds(at, size * parts)
            outs.append(pltpu.make_async_copy(goes.at[to], out.at[to], out_sems.at[g]))
            outs[-1].start()
        for copy in outs:
            copy.wait()

    long = (rows * parts, COLS)
    sems = pltpu.SemaphoreType.DMA((STEPS,))
    scratch = [pltpu.VMEM(packed.shape, BF), pltpu.VMEM(long, F32), pltpu.VMEM(long, BF), sems, sems]
    return call(body, [(long, BF)], far=(packed,), far_out=True, scratch=scratch, limit=60)[0]


def sideways(x, by):
    lanes = lax.broadcasted_iota(jnp.int32, (x.shape[0], COLS), 1)
    edge = 0 if by == 1 else COLS - 1
    parts = []
    for lo in range(0, x.shape[1], COLS):
        turned = pltpu.roll(x[:, lo : lo + COLS], by % COLS, 1)
        parts.append(jnp.where(lanes == edge, 0.0, turned))
    return jnp.concatenate(parts, axis=1)


def place(lengths, owner):
    owners = owner.shape[0]
    other = lax.broadcasted_iota(jnp.int32, (owners, owners), 1)
    held = jnp.broadcast_to(lengths[...], (owners, owners)).astype(F32)
    begins = jnp.sum(jnp.where(other < owner, held, 0.0), axis=1, keepdims=True)
    count = jnp.sum(jnp.where(other == owner, held, 0.0), axis=1, keepdims=True)
    return begins, count


def unpack_body(capacity, arrived, lengths, cot3, to_tm, wide, turned):
    owners = lengths.shape[1]
    parts = arrived.shape[0] // owners
    channels = parts * COLS // capacity
    begins, count = place(lengths, lax.broadcasted_iota(jnp.int32, (owners, owners), 0))
    wide[...] = arrived[...].astype(F32)
    for j in range(parts):
        turned[j * COLS : (j + 1) * COLS, :] = wide[pl.ds(j, owners, stride=parts), :].T.astype(BF)
    group = capacity // 3
    for f in range(3):
        voxel = lax.broadcasted_iota(jnp.int32, (owners, 512), 1).astype(F32) + float(f * 512)
        slot = voxel - begins
        slot = jnp.where((slot >= 0.0) & (slot < count), slot, -1.0).astype(BF)
        total = jnp.zeros((channels, 512), F32)
        for k in range(0, capacity, group):
            left = jnp.concatenate(
                [turned[(k + i) * channels : (k + i + 1) * channels, :] for i in range(group)], axis=1
            )
            right = jnp.concatenate(
                [jnp.where(slot == jnp.asarray(k + i, BF), jnp.asarray(1, BF), jnp.asarray(0, BF)) for i in range(group)],
                axis=0,
            )
            total += jnp.dot(left, right, preferred_element_type=F32)
        lo = f * 512
        cot = total.astype(BF)
        cot3[0:channels, lo : lo + 512] = sideways(total, -1).astype(BF)
        cot3[channels : 2 * channels, lo : lo + 512] = cot
        cot3[2 * channels : 3 * channels, lo : lo + 512] = sideways(total, 1).astype(BF)
        if f < 2:
            to_tm[:, lo : lo + 512] = cot


def unpack(arrived, lengths, capacity, after):
    owners = lengths.shape[1]
    size = arrived.shape[0] * COLS // owners
    channels = size // capacity

    def body(*refs):
        unpack_body(capacity, *refs)

    return call(
        body,
        [((3 * channels, 1536), BF), ((channels, 1024), BF)],
        arrived,
        lengths,
        scratch=[pltpu.VMEM(arrived.shape, F32), pltpu.VMEM((size, owners), BF)],
        after=after,
    )


def edges_kernel(own, to_tm, top, bot, dtop, dbot):
    to_tm[...] = own[:, 512:]
    for f in range(3):
        first = own[:, f * 512 : f * 512 + COLS]
        last = own[:, f * 512 + 3 * COLS : (f + 1) * 512]
        top[:, f * COLS : (f + 1) * COLS] = first
        bot[:, f * COLS : (f + 1) * COLS] = last
        if f:
            dtop[:, (f - 1) * COLS : f * COLS] = first
            dbot[:, (f - 1) * COLS : f * COLS] = last


def rims_kernel(cot3, by_tm, top, bot):
    for f in range(5):
        if f < 3:
            frame = cot3[192:384, f * 512 : (f + 1) * 512]
        else:
            frame = by_tm[:, (f - 3) * 512 : (f - 2) * 512]
        top[:, f * COLS : (f + 1) * COLS] = frame[:, :COLS]
        bot[:, f * COLS : (f + 1) * COLS] = frame[:, 3 * COLS :]


def turn_weights_kernel(src, out, done):
    done[...] = jnp.zeros(done.shape, F32)

    def turned(tap):
        wide = jnp.concatenate([src[26 - tap].astype(F32), jnp.zeros((64, 192), F32)], axis=0)
        wide = jnp.concatenate([wide, jnp.zeros((256, 64), F32)], axis=1).T
        return wide[:192, :192].astype(BF)

    for q in range(3):
        for ab in range(0, 9, 2):
            left = turned(ab * 3 + q)
            right = turned((ab + 1) * 3 + q) if ab < 8 else jnp.zeros((192, 64), BF)
            pair = jnp.concatenate([left, right], axis=1)
            out[q * 192 : (q + 1) * 192, ab * 192 : ab * 192 + pair.shape[1]] = pair


def add_kernel(kept, *rest):
    got, out, total = rest[:-2], rest[-2], rest[-1]
    at = 0
    for piece in got:
        rows = slice(at, at + piece.shape[0])
        at += piece.shape[0]
        total[rows, :] = kept[rows, :].astype(F32) + piece[...].astype(F32)
    spare = jnp.zeros((SHARE - DATA, COLS), F32)
    for i in range(out.shape[0] // SHARE):
        block = jnp.concatenate([total[i * DATA : (i + 1) * DATA, :], spare], axis=0)
        out[i * SHARE : (i + 1) * SHARE, :] = block.astype(BF)


def gain_lines(tail):
    at = DATA - SHARE + 16
    return tail[at : at + 2] + tail[at + 2 : at + 4]


def with_gain(total, lines):
    high = lines.astype(BF).astype(F32)
    low = lines - high
    at = lax.broadcasted_iota(jnp.int32, (SHARE, COLS), 0)
    for i, line in enumerate((high[0:1], high[1:2], low[0:1], low[1:2])):
        total = jnp.where(at == DATA + i, line, total)
    return total.astype(BF)


def sum_of(got):
    total = got[0].astype(F32)
    for i in range(1, got.shape[0]):
        total += got[i].astype(F32)
    return total


def share_kernel(got, lines, out):
    block = with_gain(sum_of(got), lines[...])
    for i in range(out.shape[0]):
        out[i] = block


def gather_kernel(got, out):
    total = sum_of(got)
    block = with_gain(total, gain_lines(total[SHARE - 16 :]))
    for i in range(out.shape[0]):
        out[i] = block


def spread_out(around, gain, out, wanted):
    own, by_tm, top, bot, dtop, dbot = around
    for fe in range(5):
        mid, above, below, f = (by_tm, dtop, dbot, fe) if fe < 2 else (own, top, bot, fe - 2)
        row = slice(f * COLS, (f + 1) * COLS)
        x = jnp.concatenate([above[:, row], mid[:, f * 512 : (f + 1) * 512], below[:, row]], axis=1).astype(F32)
        normed = x * lax.rsqrt(jnp.mean(x * x, axis=0, keepdims=True) + EPSILON)
        preact = normed * gain[...]
        value = wanted(normed, preact, jax.nn.sigmoid(preact))
        wide = jnp.concatenate([value, jnp.zeros((64, 768), F32)], axis=0)
        out[fe * 768 : (fe + 1) * 768, :] = wide.T[:, :192].astype(BF)


def window(ext, ab):
    a, b = divmod(ab, 3)
    parts = [ext[((f + a) * 6 + b) * COLS : ((f + a) * 6 + b + 4) * COLS, :] for f in range(3)]
    return jnp.concatenate(parts, axis=0)


def gain_kernel(weights, gain, cot3, *rest):
    out, factor = rest[-2:]
    spread_out(rest[:-2], gain, factor, lambda normed, preact, s: s * (1.0 + preact * (1.0 - s)) * normed)
    total = jnp.zeros((1, 192), F32)
    for ab in range(9):
        part = jnp.dot(cot3[...], window(factor, ab), preferred_element_type=F32)
        for q in range(3):
            term = part[q * 192 : (q + 1) * 192] * weights[ab * 3 + q].astype(F32)
            total += jnp.sum(term, axis=0, keepdims=True)
    wide = jnp.concatenate([total, jnp.zeros((1, 64), F32)], axis=1)
    out[0:1, :] = wide[:, :COLS]
    out[1:2, :] = wide[:, COLS:]


def weight_kernel(clip, gain, cot3, *rest):
    around, keep, give, (out, hid) = rest[:6], rest[6], rest[7:-2], rest[-2:]
    spread_out(around, gain, hid, lambda normed, preact, s: preact * s)
    held = None
    for ab in range(9):
        part = jnp.dot(cot3[...], window(hid, ab), preferred_element_type=F32).astype(BF)
        out[ab * 576 : (ab + 1) * 576, :] = part[:, :COLS]
        side = part[:, COLS:192]
        if ab == 8:
            out[MAIN + 4 * 576 : MAIN + 4 * 576 + 288, :] = jnp.concatenate([side[:288], side[288:]], axis=1)
        elif ab % 2:
            at = MAIN + (ab // 2) * 576
            out[at : at + 576, :] = jnp.concatenate([held, side], axis=1)
        else:
            held = side
    out[MAIN + MAIN // 2 :, :] = jnp.zeros((out.shape[0] - MAIN - MAIN // 2, COLS), BF)
    half = out.shape[0] // 2
    keep[...] = out[pl.ds(pl.multiple_of(clip[0] * half, 16), half), :]
    at = (1 - clip[0]) * half
    for piece in give:
        size = piece.shape[0]
        piece[...] = out[pl.ds(pl.multiple_of(at, 16), size), :]
        at += size


def input_kernel(own, gain, cot3, by_tm, top, bot, weights, out, ext, rhs):
    for fe in range(5):
        lo = fe * 768
        ext[:, lo : lo + COLS] = top[:, fe * COLS : (fe + 1) * COLS]
        if fe < 3:
            ext[:, lo + COLS : lo + 5 * COLS] = cot3[192:384, fe * 512 : (fe + 1) * 512]
        else:
            ext[:, lo + COLS : lo + 5 * COLS] = by_tm[:, (fe - 3) * 512 : (fe - 2) * 512]
        ext[:, lo + 5 * COLS : lo + 6 * COLS] = bot[:, fe * COLS : (fe + 1) * COLS]
    rhs[1728:, :] = jnp.zeros((64, 512), BF)
    for f in range(3):
        for ab in range(9):
            a, b = divmod(ab, 3)
            lo = ((f + a) * 6 + b) * COLS
            rhs[ab * 192 : (ab + 1) * 192, :] = ext[:, lo : lo + 512]
        spread = jnp.dot(weights[...], rhs[...], preferred_element_type=F32)
        grad = sideways(spread[0:192], 1) + spread[192:384] + sideways(spread[384:576], -1)
        x = own[:, f * 512 : (f + 1) * 512].astype(F32)
        inverse = lax.rsqrt(jnp.mean(x * x, axis=0, keepdims=True) + EPSILON)
        normed = x * inverse
        preact = normed * gain[...]
        s = jax.nn.sigmoid(preact)
        preact_grad = grad * s * (1.0 + preact * (1.0 - s))
        projection = jnp.mean(preact_grad * normed * gain[...], axis=0, keepdims=True)
        cot = cot3[192:384, f * 512 : (f + 1) * 512].astype(F32)
        result = inverse * (preact_grad * gain[...] - normed * projection) + cot
        out[:, f * 512 : (f + 1) * 512] = result.astype(BF)


def final_kernel(scale, clip, mine, other, out, gain_out, buf):
    n = mine.shape[0]

    def build(halves):
        gains = jnp.zeros((2, COLS), F32)
        for h, half in enumerate(halves):
            for i in range(n):
                block = half[i].astype(F32)
                at = (h * n + i) * DATA
                buf[at : at + DATA, :] = block[:DATA]
                gains += gain_lines(block[SHARE - 16 :])
        gain_out[...] = gains * scale

    @pl.when(clip[0] == 0)
    def _():
        build((mine, other))

    @pl.when(clip[0] != 0)
    def _():
        build((other, mine))

    for tap in range(27):
        ab, q = divmod(tap, 3)
        main = buf[tap * 192 : (tap + 1) * 192, :]
        if ab < 8:
            row = MAIN + (ab // 2) * 576 + q * 192
            side = buf[row : row + 192, 64 * (ab % 2) : 64 * (ab % 2) + 64]
        else:
            row = MAIN + 4 * 576
            first, second = buf[row : row + 288, 0:64], buf[row : row + 288, 64:128]
            if q == 0:
                side = first[0:192]
            elif q == 1:
                side = jnp.concatenate([first[192:288], second[0:96]], axis=0)
            else:
                side = second[96:288]
        out[tap, :, :] = jnp.concatenate([main, side], axis=1) * scale


def shifted(shard, axis, by):
    count = lax.axis_size(axis)
    return lax.ppermute(shard, axis, [(i, i + by) for i in range(count) if 0 <= i + by < count])


def diagonal(shard, rows_by):
    n_tm, n_rows = lax.axis_size("tm"), lax.axis_size("rows")
    pairs = [
        (i * n_rows + j, (i + 1) * n_rows + j + rows_by)
        for i in range(n_tm - 1)
        for j in range(n_rows)
        if 0 <= j + rows_by < n_rows
    ]
    return lax.ppermute(shard, ("tm", "rows"), pairs)


def exchange(x, axis):
    return lax.all_to_all(x, axis, split_axis=0, concat_axis=0, tiled=True)


def shards(activations, norm_gain, conv_weights, packed_grads, piece_lengths):
    n_tm, n_rows, n_clip = lax.axis_size("tm"), lax.axis_size("rows"), lax.axis_size("clip")
    channels, frames, row_count, col_count = activations.shape[1:]
    voxels = frames * row_count * col_count
    owners = piece_lengths.shape[2]
    width = packed_grads.shape[3]
    capacity = width // channels
    grad_scale = 1.0 / math.sqrt(voxels * n_tm * n_rows * n_clip)
    gain_col = norm_gain[:, None]

    packed = packed_grads.reshape(owners, width)
    sent = chunk_rows(packed).reshape(owners, width // 512, 4, COLS)
    arrived = exchange(sent, ("tm", "rows")).reshape(owners * width // COLS, COLS)

    own = activations.reshape(channels, voxels)
    edge = [(channels, 1024), (channels, 384), (channels, 384), (channels, 256), (channels, 256)]
    a_tm, a_top, a_bot, a_dtop, a_dbot = call(edges_kernel, [(s, BF) for s in edge], own)
    around = (
        own,
        shifted(a_tm, "tm", 1),
        shifted(a_bot, "rows", 1),
        shifted(a_top, "rows", -1),
        diagonal(a_dbot, 1),
        diagonal(a_dtop, -1),
    )
    flag = ((8, COLS), F32)
    taps = conv_weights.transpose(1, 0, 2)
    weights, had_weights = call(turn_weights_kernel, [((576, 1792), BF), flag], taps)

    cot3, c_frames = unpack(arrived, piece_lengths.reshape(1, owners), capacity, (had_weights,))
    cot_tm = shifted(c_frames, "tm", -1)

    clip = lax.axis_index("clip").astype(jnp.int32).reshape(1)
    swap_clip = [(0, 1), (1, 0)]
    half = n_tm * DATA
    outs = [((half, COLS), BF)] + [((size, COLS), BF) for size in GIVEN]
    ext = pltpu.VMEM((30 * COLS, channels), BF)
    scratch = [pltpu.VMEM((n_clip * half, COLS), BF), ext]
    keep, *give = call(weight_kernel, outs, clip, gain_col, cot3, *around, scratch=scratch)
    given = [lax.ppermute(piece, "clip", swap_clip) for piece in give]
    scratch = [pltpu.VMEM((half, COLS), F32)]
    part = call(add_kernel, [((n_tm * SHARE, COLS), BF)], keep, *given, scratch=scratch, after=(cot_tm,))[0]
    got = exchange(part.reshape(n_tm, SHARE, COLS), "tm")

    gain_sum = call(gain_kernel, [((2, COLS), F32)], taps, gain_col, cot3, *around, scratch=[ext])[0]

    c_top, c_bot = call(rims_kernel, [((channels, 640), BF)] * 2, cot3, cot_tm)
    cot_bot = shifted(c_top, "rows", -1)
    cot_top = shifted(c_bot, "rows", 1)
    input_grad = call(
        input_kernel,
        [((channels, voxels), BF)],
        own,
        gain_col,
        cot3,
        cot_tm,
        cot_top,
        cot_bot,
        weights,
        scratch=[pltpu.VMEM((channels, 30 * COLS), BF), pltpu.VMEM((1792, 512), BF)],
    )[0]

    had_rims = cot_top[:8, :COLS] + cot_bot[:8, :COLS]

    sent = call(share_kernel, [((n_rows, SHARE, COLS), BF)], got, gain_sum, after=(had_rims,))[0]
    got = exchange(sent, "rows")
    had_grad = input_grad[:8, :COLS]
    sent = call(gather_kernel, [((n_tm, SHARE, COLS), BF)], got, after=(had_grad,))[0]
    mine = exchange(sent, "tm")
    other = lax.ppermute(mine, "clip", swap_clip)

    def finish(*refs):
        final_kernel(grad_scale, *refs)

    shape = (27, channels, channels)
    scratch = [pltpu.VMEM((n_clip * half, COLS), F32)]
    weight_grad, gain_grad = call(
        finish, [(shape, F32), ((2, COLS), F32)], clip, mine, other, scratch=scratch
    )
    gain_grad = gain_grad.reshape(2 * COLS)[:channels]
    return (input_grad.reshape(activations.shape), weight_grad.transpose(1, 0, 2), gain_grad)


def solution(mesh):
    return jax.shard_map(
        shards,
        mesh=mesh,
        in_specs=(
            P("clip", None, "tm", "rows", None),
            P(),
            P(),
            P("clip", ("tm", "rows"), None, None),
            P("clip", ("tm", "rows"), None),
        ),
        out_specs=(P("clip", None, "tm", "rows", None), P(), P()),
        check_vma=False,
    )
```

```python
import math

import jax
import jax.numpy as jnp
from jax import lax
from jax.experimental import pallas as pl
from jax.experimental.pallas import tpu as pltpu
from jax.sharding import PartitionSpec as P

EPSILON = 1e-06
BF = jnp.bfloat16
F32 = jnp.float32
COLS = 128
MAIN = 5184
GIVEN = (1328, 1328, 1312)
DATA = 248
STEPS = 8
SHARE = 256


def call(body, outs, *args, scratch=(), after=(), far=(), far_out=False, limit=24):
    outs = [jax.ShapeDtypeStruct(s, d) for s, d in outs]
    spec = pl.BlockSpec(memory_space=pltpu.VMEM)
    anywhere = pl.BlockSpec(memory_space=pl.ANY)
    hbm = pl.BlockSpec(memory_space=pltpu.HBM)

    def after_them(*refs):
        body(*refs[len(after) :])

    return pl.pallas_call(
        after_them,
        out_shape=outs,
        in_specs=[anywhere] * len(after)
        + [hbm] * len(far)
        + [pl.BlockSpec(memory_space=pltpu.SMEM) if a.ndim == 1 else spec for a in args],
        out_specs=[hbm if far_out and i == 0 else spec for i in range(len(outs))],
        scratch_shapes=list(scratch),
        compiler_params=pltpu.CompilerParams(vmem_limit_bytes=limit << 20),
    )(*after, *far, *args)


def chunk_rows(packed):
    rows, width = packed.shape
    parts = width // COLS
    size = rows // STEPS

    def body(src, out, came, wide, goes, in_sems, out_sems):
        ins = [
            pltpu.make_async_copy(src.at[pl.ds(g * size, size)], came.at[pl.ds(g * size, size)], in_sems.at[g])
            for g in range(STEPS)
        ]
        for copy in ins:
            copy.start()
        outs = []
        for g in range(STEPS):
            ins[g].wait()
            at = g * size * parts
            for j in range(parts):
                block = came[g * size : (g + 1) * size, j * COLS : (j + 1) * COLS]
                wide[pl.ds(at + j, size, stride=parts), :] = block.astype(F32)
            goes[at : at + size * parts, :] = wide[at : at + size * parts, :].astype(BF)
            to = pl.ds(at, size * parts)
            outs.append(pltpu.make_async_copy(goes.at[to], out.at[to], out_sems.at[g]))
            outs[-1].start()
        for copy in outs:
            copy.wait()

    long = (rows * parts, COLS)
    sems = pltpu.SemaphoreType.DMA((STEPS,))
    scratch = [pltpu.VMEM(packed.shape, BF), pltpu.VMEM(long, F32), pltpu.VMEM(long, BF), sems, sems]
    return call(body, [(long, BF)], far=(packed,), far_out=True, scratch=scratch, limit=60)[0]


def sideways(x, by):
    lanes = lax.broadcasted_iota(jnp.int32, (x.shape[0], COLS), 1)
    edge = 0 if by == 1 else COLS - 1
    parts = []
    for lo in range(0, x.shape[1], COLS):
        turned = pltpu.roll(x[:, lo : lo + COLS], by % COLS, 1)
        parts.append(jnp.where(lanes == edge, 0.0, turned))
    return jnp.concatenate(parts, axis=1)


def place(lengths, owner):
    owners = owner.shape[0]
    other = lax.broadcasted_iota(jnp.int32, (owners, owners), 1)
    held = jnp.broadcast_to(lengths[...], (owners, owners)).astype(F32)
    begins = jnp.sum(jnp.where(other < owner, held, 0.0), axis=1, keepdims=True)
    count = jnp.sum(jnp.where(other == owner, held, 0.0), axis=1, keepdims=True)
    return begins, count


def unpack_body(capacity, arrived, lengths, cot3, to_tm, wide, turned):
    owners = lengths.shape[1]
    parts = arrived.shape[0] // owners
    channels = parts * COLS // capacity
    begins, count = place(lengths, lax.broadcasted_iota(jnp.int32, (owners, owners), 0))
    wide[...] = arrived[...].astype(F32)
    for j in range(parts):
        turned[j * COLS : (j + 1) * COLS, :] = wide[pl.ds(j, owners, stride=parts), :].T.astype(BF)
    group = capacity // 3
    for f in range(3):
        voxel = lax.broadcasted_iota(jnp.int32, (owners, 512), 1).astype(F32) + float(f * 512)
        slot = voxel - begins
        slot = jnp.where((slot >= 0.0) & (slot < count), slot, -1.0).astype(BF)
        total = jnp.zeros((channels, 512), F32)
        for k in range(0, capacity, group):
            left = jnp.concatenate(
                [turned[(k + i) * channels : (k + i + 1) * channels, :] for i in range(group)], axis=1
            )
            right = jnp.concatenate(
                [jnp.where(slot == jnp.asarray(k + i, BF), jnp.asarray(1, BF), jnp.asarray(0, BF)) for i in range(group)],
                axis=0,
            )
            total += jnp.dot(left, right, preferred_element_type=F32)
        lo = f * 512
        cot = total.astype(BF)
        cot3[0:channels, lo : lo + 512] = sideways(total, -1).astype(BF)
        cot3[channels : 2 * channels, lo : lo + 512] = cot
        cot3[2 * channels : 3 * channels, lo : lo + 512] = sideways(total, 1).astype(BF)
        if f < 2:
            to_tm[:, lo : lo + 512] = cot


def unpack(arrived, lengths, capacity, after):
    owners = lengths.shape[1]
    size = arrived.shape[0] * COLS // owners
    channels = size // capacity

    def body(*refs):
        unpack_body(capacity, *refs)

    return call(
        body,
        [((3 * channels, 1536), BF), ((channels, 1024), BF)],
        arrived,
        lengths,
        scratch=[pltpu.VMEM(arrived.shape, F32), pltpu.VMEM((size, owners), BF)],
        after=after,
    )


def edges_kernel(own, to_tm, top, bot, dtop, dbot):
    to_tm[...] = own[:, 512:]
    for f in range(3):
        first = own[:, f * 512 : f * 512 + COLS]
        last = own[:, f * 512 + 3 * COLS : (f + 1) * 512]
        top[:, f * COLS : (f + 1) * COLS] = first
        bot[:, f * COLS : (f + 1) * COLS] = last
        if f:
            dtop[:, (f - 1) * COLS : f * COLS] = first
            dbot[:, (f - 1) * COLS : f * COLS] = last


def rims_kernel(cot3, by_tm, top, bot):
    for f in range(5):
        if f < 3:
            frame = cot3[192:384, f * 512 : (f + 1) * 512]
        else:
            frame = by_tm[:, (f - 3) * 512 : (f - 2) * 512]
        top[:, f * COLS : (f + 1) * COLS] = frame[:, :COLS]
        bot[:, f * COLS : (f + 1) * COLS] = frame[:, 3 * COLS :]


def turn_weights_kernel(src, out, done):
    done[...] = jnp.zeros(done.shape, F32)

    def turned(tap):
        wide = jnp.concatenate([src[26 - tap].astype(F32), jnp.zeros((64, 192), F32)], axis=0)
        wide = jnp.concatenate([wide, jnp.zeros((256, 64), F32)], axis=1).T
        return wide[:192, :192].astype(BF)

    for q in range(3):
        for ab in range(0, 9, 2):
            left = turned(ab * 3 + q)
            right = turned((ab + 1) * 3 + q) if ab < 8 else jnp.zeros((192, 64), BF)
            pair = jnp.concatenate([left, right], axis=1)
            out[q * 192 : (q + 1) * 192, ab * 192 : ab * 192 + pair.shape[1]] = pair


def add_kernel(kept, *rest):
    got, out, total = rest[:-2], rest[-2], rest[-1]
    at = 0
    for piece in got:
        rows = slice(at, at + piece.shape[0])
        at += piece.shape[0]
        total[rows, :] = kept[rows, :].astype(F32) + piece[...].astype(F32)
    spare = jnp.zeros((SHARE - DATA, COLS), F32)
    for i in range(out.shape[0] // SHARE):
        block = jnp.concatenate([total[i * DATA : (i + 1) * DATA, :], spare], axis=0)
        out[i * SHARE : (i + 1) * SHARE, :] = block.astype(BF)


def gain_lines(tail):
    at = DATA - SHARE + 16
    return tail[at : at + 2] + tail[at + 2 : at + 4]


def with_gain(total, lines):
    high = lines.astype(BF).astype(F32)
    low = lines - high
    at = lax.broadcasted_iota(jnp.int32, (SHARE, COLS), 0)
    for i, line in enumerate((high[0:1], high[1:2], low[0:1], low[1:2])):
        total = jnp.where(at == DATA + i, line, total)
    return total.astype(BF)


def sum_of(got):
    total = got[0].astype(F32)
    for i in range(1, got.shape[0]):
        total += got[i].astype(F32)
    return total


def share_kernel(got, lines, out):
    block = with_gain(sum_of(got), lines[...])
    for i in range(out.shape[0]):
        out[i] = block


def gather_kernel(got, out):
    total = sum_of(got)
    block = with_gain(total, gain_lines(total[SHARE - 16 :]))
    for i in range(out.shape[0]):
        out[i] = block


def spread_out(around, gain, out, wanted):
    own, by_tm, top, bot, dtop, dbot = around
    for fe in range(5):
        mid, above, below, f = (by_tm, dtop, dbot, fe) if fe < 2 else (own, top, bot, fe - 2)
        row = slice(f * COLS, (f + 1) * COLS)
        x = jnp.concatenate([above[:, row], mid[:, f * 512 : (f + 1) * 512], below[:, row]], axis=1).astype(F32)
        normed = x * lax.rsqrt(jnp.mean(x * x, axis=0, keepdims=True) + EPSILON)
        preact = normed * gain[...]
        value = wanted(normed, preact, jax.nn.sigmoid(preact))
        wide = jnp.concatenate([value, jnp.zeros((64, 768), F32)], axis=0)
        out[fe * 768 : (fe + 1) * 768, :] = wide.T[:, :192].astype(BF)


def window(ext, ab):
    a, b = divmod(ab, 3)
    parts = [ext[((f + a) * 6 + b) * COLS : ((f + a) * 6 + b + 4) * COLS, :] for f in range(3)]
    return jnp.concatenate(parts, axis=0)


def gain_kernel(weights, gain, cot3, *rest):
    out, factor = rest[-2:]
    spread_out(rest[:-2], gain, factor, lambda normed, preact, s: s * (1.0 + preact * (1.0 - s)) * normed)
    total = jnp.zeros((1, 192), F32)
    for ab in range(9):
        part = jnp.dot(cot3[...], window(factor, ab), preferred_element_type=F32)
        for q in range(3):
            term = part[q * 192 : (q + 1) * 192] * weights[ab * 3 + q].astype(F32)
            total += jnp.sum(term, axis=0, keepdims=True)
    wide = jnp.concatenate([total, jnp.zeros((1, 64), F32)], axis=1)
    out[0:1, :] = wide[:, :COLS]
    out[1:2, :] = wide[:, COLS:]


def weight_kernel(clip, gain, cot3, *rest):
    around, keep, give, (out, hid) = rest[:6], rest[6], rest[7:-2], rest[-2:]
    spread_out(around, gain, hid, lambda normed, preact, s: preact * s)
    held = None
    for ab in range(9):
        part = jnp.dot(cot3[...], window(hid, ab), preferred_element_type=F32).astype(BF)
        out[ab * 576 : (ab + 1) * 576, :] = part[:, :COLS]
        side = part[:, COLS:192]
        if ab == 8:
            out[MAIN + 4 * 576 : MAIN + 4 * 576 + 288, :] = jnp.concatenate([side[:288], side[288:]], axis=1)
        elif ab % 2:
            at = MAIN + (ab // 2) * 576
            out[at : at + 576, :] = jnp.concatenate([held, side], axis=1)
        else:
            held = side
    out[MAIN + MAIN // 2 :, :] = jnp.zeros((out.shape[0] - MAIN - MAIN // 2, COLS), BF)
    half = out.shape[0] // 2
    keep[...] = out[pl.ds(pl.multiple_of(clip[0] * half, 16), half), :]
    at = (1 - clip[0]) * half
    for piece in give:
        size = piece.shape[0]
        piece[...] = out[pl.ds(pl.multiple_of(at, 16), size), :]
        at += size


def input_kernel(own, gain, cot3, by_tm, top, bot, weights, out, ext, rhs):
    for fe in range(5):
        lo = fe * 768
        ext[:, lo : lo + COLS] = top[:, fe * COLS : (fe + 1) * COLS]
        if fe < 3:
            ext[:, lo + COLS : lo + 5 * COLS] = cot3[192:384, fe * 512 : (fe + 1) * 512]
        else:
            ext[:, lo + COLS : lo + 5 * COLS] = by_tm[:, (fe - 3) * 512 : (fe - 2) * 512]
        ext[:, lo + 5 * COLS : lo + 6 * COLS] = bot[:, fe * COLS : (fe + 1) * COLS]
    rhs[1728:, :] = jnp.zeros((64, 512), BF)
    for f in range(3):
        for ab in range(9):
            a, b = divmod(ab, 3)
            lo = ((f + a) * 6 + b) * COLS
            rhs[ab * 192 : (ab + 1) * 192, :] = ext[:, lo : lo + 512]
        spread = jnp.dot(weights[...], rhs[...], preferred_element_type=F32)
        grad = sideways(spread[0:192], 1) + spread[192:384] + sideways(spread[384:576], -1)
        x = own[:, f * 512 : (f + 1) * 512].astype(F32)
        inverse = lax.rsqrt(jnp.mean(x * x, axis=0, keepdims=True) + EPSILON)
        normed = x * inverse
        preact = normed * gain[...]
        s = jax.nn.sigmoid(preact)
        preact_grad = grad * s * (1.0 + preact * (1.0 - s))
        projection = jnp.mean(preact_grad * normed * gain[...], axis=0, keepdims=True)
        cot = cot3[192:384, f * 512 : (f + 1) * 512].astype(F32)
        result = inverse * (preact_grad * gain[...] - normed * projection) + cot
        out[:, f * 512 : (f + 1) * 512] = result.astype(BF)


def final_kernel(scale, far_other, clip, mine, out, gain_out, buf, other, sems):
    n = mine.shape[0]
    size = n // 4
    groups = [pl.ds(g * size, size) for g in range(4)]
    copies = [pltpu.make_async_copy(far_other.at[to], other.at[to], sems.at[g]) for g, to in enumerate(groups)]
    for copy in copies:
        copy.start()

    def build(half, held):
        gains = jnp.zeros((2, COLS), F32)
        for i in range(n):
            if held is other and i % size == 0:
                copies[i // size].wait()
            block = held[i].astype(F32)
            at = half * n * DATA + i * DATA
            buf[pl.ds(pl.multiple_of(at, 8), DATA), :] = block[:DATA]
            gains += gain_lines(block[SHARE - 16 :])
        return gains

    gains = build(clip[0], mine)
    gain_out[...] = (gains + build(1 - clip[0], other)) * scale
    for tap in range(27):
        ab, q = divmod(tap, 3)
        main = buf[tap * 192 : (tap + 1) * 192, :]
        if ab < 8:
            row = MAIN + (ab // 2) * 576 + q * 192
            side = buf[row : row + 192, 64 * (ab % 2) : 64 * (ab % 2) + 64]
        else:
            row = MAIN + 4 * 576
            first, second = buf[row : row + 288, 0:64], buf[row : row + 288, 64:128]
            if q == 0:
                side = first[0:192]
            elif q == 1:
                side = jnp.concatenate([first[192:288], second[0:96]], axis=0)
            else:
                side = second[96:288]
        out[tap, :, :] = jnp.concatenate([main, side], axis=1) * scale


def shifted(shard, axis, by):
    count = lax.axis_size(axis)
    return lax.ppermute(shard, axis, [(i, i + by) for i in range(count) if 0 <= i + by < count])


def diagonal(shard, rows_by):
    n_tm, n_rows = lax.axis_size("tm"), lax.axis_size("rows")
    pairs = [
        (i * n_rows + j, (i + 1) * n_rows + j + rows_by)
        for i in range(n_tm - 1)
        for j in range(n_rows)
        if 0 <= j + rows_by < n_rows
    ]
    return lax.ppermute(shard, ("tm", "rows"), pairs)


def exchange(x, axis):
    return lax.all_to_all(x, axis, split_axis=0, concat_axis=0, tiled=True)


def shards(activations, norm_gain, conv_weights, packed_grads, piece_lengths):
    n_tm, n_rows, n_clip = lax.axis_size("tm"), lax.axis_size("rows"), lax.axis_size("clip")
    channels, frames, row_count, col_count = activations.shape[1:]
    voxels = frames * row_count * col_count
    owners = piece_lengths.shape[2]
    width = packed_grads.shape[3]
    capacity = width // channels
    grad_scale = 1.0 / math.sqrt(voxels * n_tm * n_rows * n_clip)
    gain_col = norm_gain[:, None]

    packed = packed_grads.reshape(owners, width)
    sent = chunk_rows(packed).reshape(owners, width // 512, 4, COLS)
    arrived = exchange(sent, ("tm", "rows")).reshape(owners * width // COLS, COLS)

    own = activations.reshape(channels, voxels)
    edge = [(channels, 1024), (channels, 384), (channels, 384), (channels, 256), (channels, 256)]
    a_tm, a_top, a_bot, a_dtop, a_dbot = call(edges_kernel, [(s, BF) for s in edge], own)
    around = (
        own,
        shifted(a_tm, "tm", 1),
        shifted(a_bot, "rows", 1),
        shifted(a_top, "rows", -1),
        diagonal(a_dbot, 1),
        diagonal(a_dtop, -1),
    )
    flag = ((8, COLS), F32)
    taps = conv_weights.transpose(1, 0, 2)
    weights, had_weights = call(turn_weights_kernel, [((576, 1792), BF), flag], taps)

    cot3, c_frames = unpack(arrived, piece_lengths.reshape(1, owners), capacity, (had_weights,))
    cot_tm = shifted(c_frames, "tm", -1)

    clip = lax.axis_index("clip").astype(jnp.int32).reshape(1)
    swap_clip = [(0, 1), (1, 0)]
    half = n_tm * DATA
    outs = [((half, COLS), BF)] + [((size, COLS), BF) for size in GIVEN]
    ext = pltpu.VMEM((30 * COLS, channels), BF)
    scratch = [pltpu.VMEM((n_clip * half, COLS), BF), ext]
    keep, *give = call(weight_kernel, outs, clip, gain_col, cot3, *around, scratch=scratch)
    given = [lax.ppermute(piece, "clip", swap_clip) for piece in give]
    scratch = [pltpu.VMEM((half, COLS), F32)]
    part = call(add_kernel, [((n_tm * SHARE, COLS), BF)], keep, *given, scratch=scratch, after=(cot_tm,))[0]
    got = exchange(part.reshape(n_tm, SHARE, COLS), "tm")

    gain_sum = call(gain_kernel, [((2, COLS), F32)], taps, gain_col, cot3, *around, scratch=[ext])[0]

    c_top, c_bot = call(rims_kernel, [((channels, 640), BF)] * 2, cot3, cot_tm)
    cot_bot = shifted(c_top, "rows", -1)
    cot_top = shifted(c_bot, "rows", 1)
    input_grad = call(
        input_kernel,
        [((channels, voxels), BF)],
        own,
        gain_col,
        cot3,
        cot_tm,
        cot_top,
        cot_bot,
        weights,
        scratch=[pltpu.VMEM((channels, 30 * COLS), BF), pltpu.VMEM((1792, 512), BF)],
    )[0]

    had_rims = cot_top[:8, :COLS] + cot_bot[:8, :COLS]

    sent = call(share_kernel, [((n_rows, SHARE, COLS), BF)], got, gain_sum, after=(had_rims,))[0]
    got = exchange(sent, "rows")
    had_grad = input_grad[:8, :COLS]
    sent = call(gather_kernel, [((n_tm, SHARE, COLS), BF)], got, after=(had_grad,))[0]
    mine = exchange(sent, "tm")
    other = lax.ppermute(mine, "clip", swap_clip)

    def finish(*refs):
        final_kernel(grad_scale, *refs)

    shape = (27, channels, channels)
    scratch = [pltpu.VMEM((n_clip * half, COLS), F32), pltpu.VMEM(mine.shape, BF), pltpu.SemaphoreType.DMA((4,))]
    weight_grad, gain_grad = call(
        finish, [(shape, F32), ((2, COLS), F32)], clip, mine, far=(other,), scratch=scratch
    )
    gain_grad = gain_grad.reshape(2 * COLS)[:channels]
    return (input_grad.reshape(activations.shape), weight_grad.transpose(1, 0, 2), gain_grad)


def solution(mesh):
    return jax.shard_map(
        shards,
        mesh=mesh,
        in_specs=(
            P("clip", None, "tm", "rows", None),
            P(),
            P(),
            P("clip", ("tm", "rows"), None, None),
            P("clip", ("tm", "rows"), None),
        ),
        out_specs=(P("clip", None, "tm", "rows", None), P(), P()),
        check_vma=False,
    )
```

```python
import math

import jax
import jax.numpy as jnp
from jax import lax
from jax.experimental import pallas as pl
from jax.experimental.pallas import tpu as pltpu
from jax.sharding import PartitionSpec as P

EPSILON = 1e-06
BF = jnp.bfloat16
F32 = jnp.float32
COLS = 128
MAIN = 5184
GIVEN = (1328, 1328, 1312)
DATA = 248
STEPS = 8
SHARE = 256


def call(body, outs, *args, scratch=(), after=(), far=(), far_out=False, limit=24):
    outs = [jax.ShapeDtypeStruct(s, d) for s, d in outs]
    spec = pl.BlockSpec(memory_space=pltpu.VMEM)
    anywhere = pl.BlockSpec(memory_space=pl.ANY)
    hbm = pl.BlockSpec(memory_space=pltpu.HBM)

    def after_them(*refs):
        body(*refs[len(after) :])

    return pl.pallas_call(
        after_them,
        out_shape=outs,
        in_specs=[anywhere] * len(after)
        + [hbm] * len(far)
        + [pl.BlockSpec(memory_space=pltpu.SMEM) if a.ndim == 1 else spec for a in args],
        out_specs=[hbm if far_out and i == 0 else spec for i in range(len(outs))],
        scratch_shapes=list(scratch),
        compiler_params=pltpu.CompilerParams(vmem_limit_bytes=limit << 20),
    )(*after, *far, *args)


def chunk_rows(packed):
    rows, width = packed.shape
    parts = width // COLS
    size = rows // STEPS

    def body(src, out, came, wide, goes, in_sems, out_sems):
        ins = [
            pltpu.make_async_copy(src.at[pl.ds(g * size, size)], came.at[pl.ds(g * size, size)], in_sems.at[g])
            for g in range(STEPS)
        ]
        for copy in ins:
            copy.start()
        outs = []
        for g in range(STEPS):
            ins[g].wait()
            at = g * size * parts
            for j in range(parts):
                block = came[g * size : (g + 1) * size, j * COLS : (j + 1) * COLS]
                wide[pl.ds(at + j, size, stride=parts), :] = block.astype(F32)
            goes[at : at + size * parts, :] = wide[at : at + size * parts, :].astype(BF)
            to = pl.ds(at, size * parts)
            outs.append(pltpu.make_async_copy(goes.at[to], out.at[to], out_sems.at[g]))
            outs[-1].start()
        for copy in outs:
            copy.wait()

    long = (rows * parts, COLS)
    sems = pltpu.SemaphoreType.DMA((STEPS,))
    scratch = [pltpu.VMEM(packed.shape, BF), pltpu.VMEM(long, F32), pltpu.VMEM(long, BF), sems, sems]
    return call(body, [(long, BF)], far=(packed,), far_out=True, scratch=scratch, limit=60)[0]


def sideways(x, by):
    lanes = lax.broadcasted_iota(jnp.int32, (x.shape[0], COLS), 1)
    edge = 0 if by == 1 else COLS - 1
    parts = []
    for lo in range(0, x.shape[1], COLS):
        turned = pltpu.roll(x[:, lo : lo + COLS], by % COLS, 1)
        parts.append(jnp.where(lanes == edge, 0.0, turned))
    return jnp.concatenate(parts, axis=1)


def place(lengths, owner):
    owners = owner.shape[0]
    other = lax.broadcasted_iota(jnp.int32, (owners, owners), 1)
    held = jnp.broadcast_to(lengths[...], (owners, owners)).astype(F32)
    begins = jnp.sum(jnp.where(other < owner, held, 0.0), axis=1, keepdims=True)
    count = jnp.sum(jnp.where(other == owner, held, 0.0), axis=1, keepdims=True)
    return begins, count


def unpack_body(capacity, arrived, lengths, cot3, to_tm, wide, turned):
    owners = lengths.shape[1]
    parts = arrived.shape[0] // owners
    channels = parts * COLS // capacity
    begins, count = place(lengths, lax.broadcasted_iota(jnp.int32, (owners, owners), 0))
    wide[...] = arrived[...].astype(F32)
    for j in range(parts):
        turned[j * COLS : (j + 1) * COLS, :] = wide[pl.ds(j, owners, stride=parts), :].T.astype(BF)
    group = capacity // 3
    for f in range(3):
        voxel = lax.broadcasted_iota(jnp.int32, (owners, 512), 1).astype(F32) + float(f * 512)
        slot = voxel - begins
        slot = jnp.where((slot >= 0.0) & (slot < count), slot, -1.0).astype(BF)
        total = jnp.zeros((channels, 512), F32)
        for k in range(0, capacity, group):
            left = jnp.concatenate(
                [turned[(k + i) * channels : (k + i + 1) * channels, :] for i in range(group)], axis=1
            )
            right = jnp.concatenate(
                [jnp.where(slot == jnp.asarray(k + i, BF), jnp.asarray(1, BF), jnp.asarray(0, BF)) for i in range(group)],
                axis=0,
            )
            total += jnp.dot(left, right, preferred_element_type=F32)
        lo = f * 512
        cot = total.astype(BF)
        cot3[0:channels, lo : lo + 512] = sideways(total, -1).astype(BF)
        cot3[channels : 2 * channels, lo : lo + 512] = cot
        cot3[2 * channels : 3 * channels, lo : lo + 512] = sideways(total, 1).astype(BF)
        if f < 2:
            to_tm[:, lo : lo + 512] = cot


def unpack(arrived, lengths, capacity, after):
    owners = lengths.shape[1]
    size = arrived.shape[0] * COLS // owners
    channels = size // capacity

    def body(*refs):
        unpack_body(capacity, *refs)

    return call(
        body,
        [((3 * channels, 1536), BF), ((channels, 1024), BF)],
        arrived,
        lengths,
        scratch=[pltpu.VMEM(arrived.shape, F32), pltpu.VMEM((size, owners), BF)],
        after=after,
    )


def edges_kernel(own, to_tm, top, bot, dtop, dbot):
    to_tm[...] = own[:, 512:]
    for f in range(3):
        first = own[:, f * 512 : f * 512 + COLS]
        last = own[:, f * 512 + 3 * COLS : (f + 1) * 512]
        top[:, f * COLS : (f + 1) * COLS] = first
        bot[:, f * COLS : (f + 1) * COLS] = last
        if f:
            dtop[:, (f - 1) * COLS : f * COLS] = first
            dbot[:, (f - 1) * COLS : f * COLS] = last


def rims_kernel(cot3, by_tm, top, bot):
    for f in range(5):
        if f < 3:
            frame = cot3[192:384, f * 512 : (f + 1) * 512]
        else:
            frame = by_tm[:, (f - 3) * 512 : (f - 2) * 512]
        top[:, f * COLS : (f + 1) * COLS] = frame[:, :COLS]
        bot[:, f * COLS : (f + 1) * COLS] = frame[:, 3 * COLS :]


def turn_weights_kernel(src, out, done):
    done[...] = jnp.zeros(done.shape, F32)

    def turned(tap):
        wide = jnp.concatenate([src[26 - tap].astype(F32), jnp.zeros((64, 192), F32)], axis=0)
        wide = jnp.concatenate([wide, jnp.zeros((256, 64), F32)], axis=1).T
        return wide[:192, :192].astype(BF)

    for q in range(3):
        for ab in range(0, 9, 2):
            left = turned(ab * 3 + q)
            right = turned((ab + 1) * 3 + q) if ab < 8 else jnp.zeros((192, 64), BF)
            pair = jnp.concatenate([left, right], axis=1)
            out[q * 192 : (q + 1) * 192, ab * 192 : ab * 192 + pair.shape[1]] = pair


def add_kernel(kept, *rest):
    got, out, total = rest[:-2], rest[-2], rest[-1]
    at = 0
    for piece in got:
        rows = slice(at, at + piece.shape[0])
        at += piece.shape[0]
        total[rows, :] = kept[rows, :].astype(F32) + piece[...].astype(F32)
    spare = jnp.zeros((SHARE - DATA, COLS), F32)
    for i in range(out.shape[0] // SHARE):
        block = jnp.concatenate([total[i * DATA : (i + 1) * DATA, :], spare], axis=0)
        out[i * SHARE : (i + 1) * SHARE, :] = block.astype(BF)


def gain_lines(tail):
    at = DATA - SHARE + 16
    return tail[at : at + 2] + tail[at + 2 : at + 4]


def with_gain(total, lines):
    high = lines.astype(BF).astype(F32)
    low = lines - high
    at = lax.broadcasted_iota(jnp.int32, (SHARE, COLS), 0)
    for i, line in enumerate((high[0:1], high[1:2], low[0:1], low[1:2])):
        total = jnp.where(at == DATA + i, line, total)
    return total.astype(BF)


def sum_of(got):
    total = got[0].astype(F32)
    for i in range(1, got.shape[0]):
        total += got[i].astype(F32)
    return total


def share_kernel(got, lines, out):
    block = with_gain(sum_of(got), lines[...])
    for i in range(out.shape[0]):
        out[i] = block


def gather_kernel(got, out):
    total = sum_of(got)
    block = with_gain(total, gain_lines(total[SHARE - 16 :]))
    for i in range(out.shape[0]):
        out[i] = block


def spread_out(around, gain, out, wanted):
    own, by_tm, top, bot, dtop, dbot = around
    for fe in range(5):
        mid, above, below, f = (by_tm, dtop, dbot, fe) if fe < 2 else (own, top, bot, fe - 2)
        row = slice(f * COLS, (f + 1) * COLS)
        x = jnp.concatenate([above[:, row], mid[:, f * 512 : (f + 1) * 512], below[:, row]], axis=1).astype(F32)
        normed = x * lax.rsqrt(jnp.mean(x * x, axis=0, keepdims=True) + EPSILON)
        preact = normed * gain[...]
        value = wanted(normed, preact, jax.nn.sigmoid(preact))
        wide = jnp.concatenate([value, jnp.zeros((64, 768), F32)], axis=0)
        out[fe * 768 : (fe + 1) * 768, :] = wide.T[:, :192].astype(BF)


def window(ext, ab):
    a, b = divmod(ab, 3)
    parts = [ext[((f + a) * 6 + b) * COLS : ((f + a) * 6 + b + 4) * COLS, :] for f in range(3)]
    return jnp.concatenate(parts, axis=0)


def gain_kernel(weights, gain, cot3, *rest):
    out, factor = rest[-2:]
    spread_out(rest[:-2], gain, factor, lambda normed, preact, s: s * (1.0 + preact * (1.0 - s)) * normed)
    total = jnp.zeros((1, 192), F32)
    for ab in range(9):
        part = jnp.dot(cot3[...], window(factor, ab), preferred_element_type=F32)
        for q in range(3):
            term = part[q * 192 : (q + 1) * 192] * weights[ab * 3 + q].astype(F32)
            total += jnp.sum(term, axis=0, keepdims=True)
    wide = jnp.concatenate([total, jnp.zeros((1, 64), F32)], axis=1)
    out[0:1, :] = wide[:, :COLS]
    out[1:2, :] = wide[:, COLS:]


def weight_kernel(clip, gain, cot3, *rest):
    around, keep, give, (out, hid) = rest[:6], rest[6], rest[7:-2], rest[-2:]
    spread_out(around, gain, hid, lambda normed, preact, s: preact * s)
    held = None
    for ab in range(9):
        part = jnp.dot(cot3[...], window(hid, ab), preferred_element_type=F32).astype(BF)
        out[ab * 576 : (ab + 1) * 576, :] = part[:, :COLS]
        side = part[:, COLS:192]
        if ab == 8:
            out[MAIN + 4 * 576 : MAIN + 4 * 576 + 288, :] = jnp.concatenate([side[:288], side[288:]], axis=1)
        elif ab % 2:
            at = MAIN + (ab // 2) * 576
            out[at : at + 576, :] = jnp.concatenate([held, side], axis=1)
        else:
            held = side
    out[MAIN + MAIN // 2 :, :] = jnp.zeros((out.shape[0] - MAIN - MAIN // 2, COLS), BF)
    half = out.shape[0] // 2
    keep[...] = out[pl.ds(pl.multiple_of(clip[0] * half, 16), half), :]
    at = (1 - clip[0]) * half
    for piece in give:
        size = piece.shape[0]
        piece[...] = out[pl.ds(pl.multiple_of(at, 16), size), :]
        at += size


def input_kernel(own, gain, cot3, by_tm, top, bot, weights, out, ext, rhs):
    for fe in range(5):
        lo = fe * 768
        ext[:, lo : lo + COLS] = top[:, fe * COLS : (fe + 1) * COLS]
        if fe < 3:
            ext[:, lo + COLS : lo + 5 * COLS] = cot3[192:384, fe * 512 : (fe + 1) * 512]
        else:
            ext[:, lo + COLS : lo + 5 * COLS] = by_tm[:, (fe - 3) * 512 : (fe - 2) * 512]
        ext[:, lo + 5 * COLS : lo + 6 * COLS] = bot[:, fe * COLS : (fe + 1) * COLS]
    rhs[1728:, :] = jnp.zeros((64, 512), BF)
    for f in range(3):
        for ab in range(9):
            a, b = divmod(ab, 3)
            lo = ((f + a) * 6 + b) * COLS
            rhs[ab * 192 : (ab + 1) * 192, :] = ext[:, lo : lo + 512]
        spread = jnp.dot(weights[...], rhs[...], preferred_element_type=F32)
        grad = sideways(spread[0:192], 1) + spread[192:384] + sideways(spread[384:576], -1)
        x = own[:, f * 512 : (f + 1) * 512].astype(F32)
        inverse = lax.rsqrt(jnp.mean(x * x, axis=0, keepdims=True) + EPSILON)
        normed = x * inverse
        preact = normed * gain[...]
        s = jax.nn.sigmoid(preact)
        preact_grad = grad * s * (1.0 + preact * (1.0 - s))
        projection = jnp.mean(preact_grad * normed * gain[...], axis=0, keepdims=True)
        cot = cot3[192:384, f * 512 : (f + 1) * 512].astype(F32)
        result = inverse * (preact_grad * gain[...] - normed * projection) + cot
        out[:, f * 512 : (f + 1) * 512] = result.astype(BF)


def final_kernel(scale, clip, mine, other, out, gain_out, buf):
    n = mine.shape[0]

    def build(halves):
        gains = jnp.zeros((2, COLS), F32)
        for h, half in enumerate(halves):
            for i in range(n):
                block = half[i].astype(F32)
                at = (h * n + i) * DATA
                buf[at : at + DATA, :] = block[:DATA]
                gains += gain_lines(block[SHARE - 16 :])
        gain_out[...] = gains * scale

    @pl.when(clip[0] == 0)
    def _():
        build((mine, other))

    @pl.when(clip[0] != 0)
    def _():
        build((other, mine))

    for tap in range(27):
        ab, q = divmod(tap, 3)
        main = buf[tap * 192 : (tap + 1) * 192, :]
        if ab < 8:
            row = MAIN + (ab // 2) * 576 + q * 192
            side = buf[row : row + 192, 64 * (ab % 2) : 64 * (ab % 2) + 64]
        else:
            row = MAIN + 4 * 576
            first, second = buf[row : row + 288, 0:64], buf[row : row + 288, 64:128]
            if q == 0:
                side = first[0:192]
            elif q == 1:
                side = jnp.concatenate([first[192:288], second[0:96]], axis=0)
            else:
                side = second[96:288]
        out[tap, :, :] = jnp.concatenate([main, side], axis=1) * scale


def shifted(shard, axis, by):
    count = lax.axis_size(axis)
    return lax.ppermute(shard, axis, [(i, i + by) for i in range(count) if 0 <= i + by < count])


def diagonal(shard, rows_by):
    n_tm, n_rows = lax.axis_size("tm"), lax.axis_size("rows")
    pairs = [
        (i * n_rows + j, (i + 1) * n_rows + j + rows_by)
        for i in range(n_tm - 1)
        for j in range(n_rows)
        if 0 <= j + rows_by < n_rows
    ]
    return lax.ppermute(shard, ("tm", "rows"), pairs)


def exchange(x, axis):
    return lax.all_to_all(x, axis, split_axis=0, concat_axis=0, tiled=True)


def shards(activations, norm_gain, conv_weights, packed_grads, piece_lengths):
    n_tm, n_rows, n_clip = lax.axis_size("tm"), lax.axis_size("rows"), lax.axis_size("clip")
    channels, frames, row_count, col_count = activations.shape[1:]
    voxels = frames * row_count * col_count
    owners = piece_lengths.shape[2]
    width = packed_grads.shape[3]
    capacity = width // channels
    grad_scale = 1.0 / math.sqrt(voxels * n_tm * n_rows * n_clip)
    gain_col = norm_gain[:, None]

    packed = packed_grads.reshape(owners, width)
    sent = chunk_rows(packed).reshape(owners, width // 512, 4, COLS)
    arrived = exchange(sent, ("tm", "rows")).reshape(owners * width // COLS, COLS)

    own = activations.reshape(channels, voxels)
    edge = [(channels, 1024), (channels, 384), (channels, 384), (channels, 256), (channels, 256)]
    a_tm, a_top, a_bot, a_dtop, a_dbot = call(edges_kernel, [(s, BF) for s in edge], own)
    around = (
        own,
        shifted(a_tm, "tm", 1),
        shifted(a_bot, "rows", 1),
        shifted(a_top, "rows", -1),
        diagonal(a_dbot, 1),
        diagonal(a_dtop, -1),
    )
    flag = ((8, COLS), F32)
    taps = conv_weights.transpose(1, 0, 2)
    weights, had_weights = call(turn_weights_kernel, [((576, 1792), BF), flag], taps)

    cot3, c_frames = unpack(arrived, piece_lengths.reshape(1, owners), capacity, (had_weights,))
    cot_tm = shifted(c_frames, "tm", -1)

    clip = lax.axis_index("clip").astype(jnp.int32).reshape(1)
    swap_clip = [(0, 1), (1, 0)]
    half = n_tm * DATA
    outs = [((half, COLS), BF)] + [((size, COLS), BF) for size in GIVEN]
    ext = pltpu.VMEM((30 * COLS, channels), BF)
    scratch = [pltpu.VMEM((n_clip * half, COLS), BF), ext]
    keep, *give = call(weight_kernel, outs, clip, gain_col, cot3, *around, scratch=scratch)
    given = [lax.ppermute(piece, "clip", swap_clip) for piece in give]
    scratch = [pltpu.VMEM((half, COLS), F32)]
    part = call(add_kernel, [((n_tm * SHARE, COLS), BF)], keep, *given, scratch=scratch, after=(cot_tm,))[0]
    got = exchange(part.reshape(n_tm, SHARE, COLS), "tm")

    gain_sum = call(gain_kernel, [((2, COLS), F32)], taps, gain_col, cot3, *around, scratch=[ext])[0]

    c_top, c_bot = call(rims_kernel, [((channels, 640), BF)] * 2, cot3, cot_tm)
    cot_bot = shifted(c_top, "rows", -1)
    cot_top = shifted(c_bot, "rows", 1)
    input_grad = call(
        input_kernel,
        [((channels, voxels), BF)],
        own,
        gain_col,
        cot3,
        cot_tm,
        cot_top,
        cot_bot,
        weights,
        scratch=[pltpu.VMEM((channels, 30 * COLS), BF), pltpu.VMEM((1792, 512), BF)],
    )[0]

    had_rims = cot_top[:8, :COLS] + cot_bot[:8, :COLS]

    sent = call(share_kernel, [((n_rows, SHARE, COLS), BF)], got, gain_sum, after=(had_rims,))[0]
    got = exchange(sent, "rows")
    had_grad = input_grad[:8, :COLS]
    sent = call(gather_kernel, [((n_tm, SHARE, COLS), BF)], got, after=(had_grad,))[0]
    mine = exchange(sent, "tm")
    other = lax.ppermute(mine.reshape(n_tm * SHARE, COLS), "clip", swap_clip).reshape(mine.shape)

    def finish(*refs):
        final_kernel(grad_scale, *refs)

    shape = (27, channels, channels)
    scratch = [pltpu.VMEM((n_clip * half, COLS), F32)]
    weight_grad, gain_grad = call(
        finish, [(shape, F32), ((2, COLS), F32)], clip, mine, other, scratch=scratch
    )
    gain_grad = gain_grad.reshape(2 * COLS)[:channels]
    return (input_grad.reshape(activations.shape), weight_grad.transpose(1, 0, 2), gain_grad)


def solution(mesh):
    return jax.shard_map(
        shards,
        mesh=mesh,
        in_specs=(
            P("clip", None, "tm", "rows", None),
            P(),
            P(),
            P("clip", ("tm", "rows"), None, None),
            P("clip", ("tm", "rows"), None),
        ),
        out_specs=(P("clip", None, "tm", "rows", None), P(), P()),
        check_vma=False,
    )
```

```python
import math

import jax
import jax.numpy as jnp
from jax import lax
from jax.experimental import pallas as pl
from jax.experimental.pallas import tpu as pltpu
from jax.sharding import PartitionSpec as P

EPSILON = 1e-06
BF = jnp.bfloat16
F32 = jnp.float32
COLS = 128
MAIN = 5184
GIVEN = (1328, 1328, 1312)
DATA = 248
STEPS = 8
SHARE = 256


def call(body, outs, *args, scratch=(), after=(), far=(), far_out=False, limit=24):
    outs = [jax.ShapeDtypeStruct(s, d) for s, d in outs]
    spec = pl.BlockSpec(memory_space=pltpu.VMEM)
    anywhere = pl.BlockSpec(memory_space=pl.ANY)
    hbm = pl.BlockSpec(memory_space=pltpu.HBM)

    def after_them(*refs):
        body(*refs[len(after) :])

    return pl.pallas_call(
        after_them,
        out_shape=outs,
        in_specs=[anywhere] * len(after)
        + [hbm] * len(far)
        + [pl.BlockSpec(memory_space=pltpu.SMEM) if a.ndim == 1 else spec for a in args],
        out_specs=[hbm if far_out and i == 0 else spec for i in range(len(outs))],
        scratch_shapes=list(scratch),
        compiler_params=pltpu.CompilerParams(vmem_limit_bytes=limit << 20),
    )(*after, *far, *args)


def chunk_rows(packed):
    rows, width = packed.shape
    parts = width // COLS
    size = rows // STEPS

    def body(src, out, came, wide, goes, in_sems, out_sems):
        ins = [
            pltpu.make_async_copy(src.at[pl.ds(g * size, size)], came.at[pl.ds(g * size, size)], in_sems.at[g])
            for g in range(STEPS)
        ]
        for copy in ins:
            copy.start()
        outs = []
        for g in range(STEPS):
            ins[g].wait()
            at = g * size * parts
            for j in range(parts):
                block = came[g * size : (g + 1) * size, j * COLS : (j + 1) * COLS]
                wide[pl.ds(at + j, size, stride=parts), :] = block.astype(F32)
            goes[at : at + size * parts, :] = wide[at : at + size * parts, :].astype(BF)
            to = pl.ds(at, size * parts)
            outs.append(pltpu.make_async_copy(goes.at[to], out.at[to], out_sems.at[g]))
            outs[-1].start()
        for copy in outs:
            copy.wait()

    long = (rows * parts, COLS)
    sems = pltpu.SemaphoreType.DMA((STEPS,))
    scratch = [pltpu.VMEM(packed.shape, BF), pltpu.VMEM((rows * parts + 64, COLS), F32), pltpu.VMEM(long, BF), sems, sems]
    return call(body, [(long, BF)], far=(packed,), far_out=True, scratch=scratch, limit=60)[0]


def sideways(x, by):
    lanes = lax.broadcasted_iota(jnp.int32, (x.shape[0], COLS), 1)
    edge = 0 if by == 1 else COLS - 1
    parts = []
    for lo in range(0, x.shape[1], COLS):
        turned = pltpu.roll(x[:, lo : lo + COLS], by % COLS, 1)
        parts.append(jnp.where(lanes == edge, 0.0, turned))
    return jnp.concatenate(parts, axis=1)


def place(lengths, owner):
    owners = owner.shape[0]
    other = lax.broadcasted_iota(jnp.int32, (owners, owners), 1)
    held = jnp.broadcast_to(lengths[...], (owners, owners)).astype(F32)
    begins = jnp.sum(jnp.where(other < owner, held, 0.0), axis=1, keepdims=True)
    count = jnp.sum(jnp.where(other == owner, held, 0.0), axis=1, keepdims=True)
    return begins, count


def unpack_body(capacity, arrived, lengths, cot3, to_tm, wide, turned):
    owners = lengths.shape[1]
    parts = arrived.shape[0] // owners
    channels = parts * COLS // capacity
    begins, count = place(lengths, lax.broadcasted_iota(jnp.int32, (owners, owners), 0))
    wide[: arrived.shape[0], :] = arrived[...].astype(F32)
    for j in range(parts):
        turned[j * COLS : (j + 1) * COLS, :] = wide[pl.ds(j, owners, stride=parts), :].T.astype(BF)
    group = capacity // 3
    for f in range(3):
        voxel = lax.broadcasted_iota(jnp.int32, (owners, 512), 1).astype(F32) + float(f * 512)
        slot = voxel - begins
        slot = jnp.where((slot >= 0.0) & (slot < count), slot, -1.0).astype(BF)
        total = jnp.zeros((channels, 512), F32)
        for k in range(0, capacity, group):
            left = jnp.concatenate(
                [turned[(k + i) * channels : (k + i + 1) * channels, :] for i in range(group)], axis=1
            )
            right = jnp.concatenate(
                [jnp.where(slot == jnp.asarray(k + i, BF), jnp.asarray(1, BF), jnp.asarray(0, BF)) for i in range(group)],
                axis=0,
            )
            total += jnp.dot(left, right, preferred_element_type=F32)
        lo = f * 512
        cot = total.astype(BF)
        cot3[0:channels, lo : lo + 512] = sideways(total, -1).astype(BF)
        cot3[channels : 2 * channels, lo : lo + 512] = cot
        cot3[2 * channels : 3 * channels, lo : lo + 512] = sideways(total, 1).astype(BF)
        if f < 2:
            to_tm[:, lo : lo + 512] = cot


def unpack(arrived, lengths, capacity, after):
    owners = lengths.shape[1]
    size = arrived.shape[0] * COLS // owners
    channels = size // capacity

    def body(*refs):
        unpack_body(capacity, *refs)

    return call(
        body,
        [((3 * channels, 1536), BF), ((channels, 1024), BF)],
        arrived,
        lengths,
        scratch=[pltpu.VMEM((arrived.shape[0] + 64, COLS), F32), pltpu.VMEM((size, owners), BF)],
        after=after,
    )


def edges_kernel(own, to_tm, top, bot, dtop, dbot):
    to_tm[...] = own[:, 512:]
    for f in range(3):
        first = own[:, f * 512 : f * 512 + COLS]
        last = own[:, f * 512 + 3 * COLS : (f + 1) * 512]
        top[:, f * COLS : (f + 1) * COLS] = first
        bot[:, f * COLS : (f + 1) * COLS] = last
        if f:
            dtop[:, (f - 1) * COLS : f * COLS] = first
            dbot[:, (f - 1) * COLS : f * COLS] = last


def rims_kernel(cot3, by_tm, top, bot):
    for f in range(5):
        if f < 3:
            frame = cot3[192:384, f * 512 : (f + 1) * 512]
        else:
            frame = by_tm[:, (f - 3) * 512 : (f - 2) * 512]
        top[:, f * COLS : (f + 1) * COLS] = frame[:, :COLS]
        bot[:, f * COLS : (f + 1) * COLS] = frame[:, 3 * COLS :]


def turn_weights_kernel(src, out, done):
    done[...] = jnp.zeros(done.shape, F32)

    def turned(tap):
        wide = jnp.concatenate([src[26 - tap].astype(F32), jnp.zeros((64, 192), F32)], axis=0)
        wide = jnp.concatenate([wide, jnp.zeros((256, 64), F32)], axis=1).T
        return wide[:192, :192].astype(BF)

    for q in range(3):
        for ab in range(0, 9, 2):
            left = turned(ab * 3 + q)
            right = turned((ab + 1) * 3 + q) if ab < 8 else jnp.zeros((192, 64), BF)
            pair = jnp.concatenate([left, right], axis=1)
            out[q * 192 : (q + 1) * 192, ab * 192 : ab * 192 + pair.shape[1]] = pair


def add_kernel(kept, *rest):
    got, out, total = rest[:-2], rest[-2], rest[-1]
    at = 0
    for piece in got:
        rows = slice(at, at + piece.shape[0])
        at += piece.shape[0]
        total[rows, :] = kept[rows, :].astype(F32) + piece[...].astype(F32)
    spare = jnp.zeros((SHARE - DATA, COLS), F32)
    for i in range(out.shape[0] // SHARE):
        block = jnp.concatenate([total[i * DATA : (i + 1) * DATA, :], spare], axis=0)
        out[i * SHARE : (i + 1) * SHARE, :] = block.astype(BF)


def gain_lines(tail):
    at = DATA - SHARE + 16
    return tail[at : at + 2] + tail[at + 2 : at + 4]


def with_gain(total, lines):
    high = lines.astype(BF).astype(F32)
    low = lines - high
    at = lax.broadcasted_iota(jnp.int32, (SHARE, COLS), 0)
    for i, line in enumerate((high[0:1], high[1:2], low[0:1], low[1:2])):
        total = jnp.where(at == DATA + i, line, total)
    return total.astype(BF)


def sum_of(got):
    total = got[0].astype(F32)
    for i in range(1, got.shape[0]):
        total += got[i].astype(F32)
    return total


def share_kernel(got, lines, out):
    block = with_gain(sum_of(got), lines[...])
    for i in range(out.shape[0]):
        out[i] = block


def gather_kernel(got, out):
    total = sum_of(got)
    block = with_gain(total, gain_lines(total[SHARE - 16 :]))
    for i in range(out.shape[0]):
        out[i] = block


def spread_out(around, gain, out, wanted):
    own, by_tm, top, bot, dtop, dbot = around
    for fe in range(5):
        mid, above, below, f = (by_tm, dtop, dbot, fe) if fe < 2 else (own, top, bot, fe - 2)
        row = slice(f * COLS, (f + 1) * COLS)
        x = jnp.concatenate([above[:, row], mid[:, f * 512 : (f + 1) * 512], below[:, row]], axis=1).astype(F32)
        normed = x * lax.rsqrt(jnp.mean(x * x, axis=0, keepdims=True) + EPSILON)
        preact = normed * gain[...]
        value = wanted(normed, preact, jax.nn.sigmoid(preact))
        wide = jnp.concatenate([value, jnp.zeros((64, 768), F32)], axis=0)
        out[fe * 768 : (fe + 1) * 768, :] = wide.T[:, :192].astype(BF)


def window(ext, ab):
    a, b = divmod(ab, 3)
    parts = [ext[((f + a) * 6 + b) * COLS : ((f + a) * 6 + b + 4) * COLS, :] for f in range(3)]
    return jnp.concatenate(parts, axis=0)


def gain_kernel(weights, gain, cot3, *rest):
    out, factor = rest[-2:]
    spread_out(rest[:-2], gain, factor, lambda normed, preact, s: s * (1.0 + preact * (1.0 - s)) * normed)
    total = jnp.zeros((1, 192), F32)
    for ab in range(9):
        part = jnp.dot(cot3[...], window(factor, ab), preferred_element_type=F32)
        for q in range(3):
            term = part[q * 192 : (q + 1) * 192] * weights[ab * 3 + q].astype(F32)
            total += jnp.sum(term, axis=0, keepdims=True)
    wide = jnp.concatenate([total, jnp.zeros((1, 64), F32)], axis=1)
    out[0:1, :] = wide[:, :COLS]
    out[1:2, :] = wide[:, COLS:]


def weight_kernel(clip, gain, cot3, *rest):
    around, keep, give, (out, hid) = rest[:6], rest[6], rest[7:-2], rest[-2:]
    spread_out(around, gain, hid, lambda normed, preact, s: preact * s)
    held = None
    for ab in range(9):
        part = jnp.dot(cot3[...], window(hid, ab), preferred_element_type=F32).astype(BF)
        out[ab * 576 : (ab + 1) * 576, :] = part[:, :COLS]
        side = part[:, COLS:192]
        if ab == 8:
            out[MAIN + 4 * 576 : MAIN + 4 * 576 + 288, :] = jnp.concatenate([side[:288], side[288:]], axis=1)
        elif ab % 2:
            at = MAIN + (ab // 2) * 576
            out[at : at + 576, :] = jnp.concatenate([held, side], axis=1)
        else:
            held = side
    out[MAIN + MAIN // 2 :, :] = jnp.zeros((out.shape[0] - MAIN - MAIN // 2, COLS), BF)
    half = out.shape[0] // 2
    keep[...] = out[pl.ds(pl.multiple_of(clip[0] * half, 16), half), :]
    at = (1 - clip[0]) * half
    for piece in give:
        size = piece.shape[0]
        piece[...] = out[pl.ds(pl.multiple_of(at, 16), size), :]
        at += size


def input_kernel(own, gain, cot3, by_tm, top, bot, weights, out, ext, rhs):
    for fe in range(5):
        lo = fe * 768
        ext[:, lo : lo + COLS] = top[:, fe * COLS : (fe + 1) * COLS]
        if fe < 3:
            ext[:, lo + COLS : lo + 5 * COLS] = cot3[192:384, fe * 512 : (fe + 1) * 512]
        else:
            ext[:, lo + COLS : lo + 5 * COLS] = by_tm[:, (fe - 3) * 512 : (fe - 2) * 512]
        ext[:, lo + 5 * COLS : lo + 6 * COLS] = bot[:, fe * COLS : (fe + 1) * COLS]
    rhs[1728:, :] = jnp.zeros((64, 512), BF)
    for f in range(3):
        for ab in range(9):
            a, b = divmod(ab, 3)
            lo = ((f + a) * 6 + b) * COLS
            rhs[ab * 192 : (ab + 1) * 192, :] = ext[:, lo : lo + 512]
        spread = jnp.dot(weights[...], rhs[...], preferred_element_type=F32)
        grad = sideways(spread[0:192], 1) + spread[192:384] + sideways(spread[384:576], -1)
        x = own[:, f * 512 : (f + 1) * 512].astype(F32)
        inverse = lax.rsqrt(jnp.mean(x * x, axis=0, keepdims=True) + EPSILON)
        normed = x * inverse
        preact = normed * gain[...]
        s = jax.nn.sigmoid(preact)
        preact_grad = grad * s * (1.0 + preact * (1.0 - s))
        projection = jnp.mean(preact_grad * normed * gain[...], axis=0, keepdims=True)
        cot = cot3[192:384, f * 512 : (f + 1) * 512].astype(F32)
        result = inverse * (preact_grad * gain[...] - normed * projection) + cot
        out[:, f * 512 : (f + 1) * 512] = result.astype(BF)


def final_kernel(scale, clip, mine, other, out, gain_out, buf):
    n = mine.shape[0]

    def build(halves):
        gains = jnp.zeros((2, COLS), F32)
        for h, half in enumerate(halves):
            for i in range(n):
                block = half[i].astype(F32)
                at = (h * n + i) * DATA
                buf[at : at + DATA, :] = block[:DATA]
                gains += gain_lines(block[SHARE - 16 :])
        gain_out[...] = gains * scale

    @pl.when(clip[0] == 0)
    def _():
        build((mine, other))

    @pl.when(clip[0] != 0)
    def _():
        build((other, mine))

    for tap in range(27):
        ab, q = divmod(tap, 3)
        main = buf[tap * 192 : (tap + 1) * 192, :]
        if ab < 8:
            row = MAIN + (ab // 2) * 576 + q * 192
            side = buf[row : row + 192, 64 * (ab % 2) : 64 * (ab % 2) + 64]
        else:
            row = MAIN + 4 * 576
            first, second = buf[row : row + 288, 0:64], buf[row : row + 288, 64:128]
            if q == 0:
                side = first[0:192]
            elif q == 1:
                side = jnp.concatenate([first[192:288], second[0:96]], axis=0)
            else:
                side = second[96:288]
        out[tap, :, :] = jnp.concatenate([main, side], axis=1) * scale


def shifted(shard, axis, by):
    count = lax.axis_size(axis)
    return lax.ppermute(shard, axis, [(i, i + by) for i in range(count) if 0 <= i + by < count])


def diagonal(shard, rows_by):
    n_tm, n_rows = lax.axis_size("tm"), lax.axis_size("rows")
    pairs = [
        (i * n_rows + j, (i + 1) * n_rows + j + rows_by)
        for i in range(n_tm - 1)
        for j in range(n_rows)
        if 0 <= j + rows_by < n_rows
    ]
    return lax.ppermute(shard, ("tm", "rows"), pairs)


def exchange(x, axis):
    return lax.all_to_all(x, axis, split_axis=0, concat_axis=0, tiled=True)


def shards(activations, norm_gain, conv_weights, packed_grads, piece_lengths):
    n_tm, n_rows, n_clip = lax.axis_size("tm"), lax.axis_size("rows"), lax.axis_size("clip")
    channels, frames, row_count, col_count = activations.shape[1:]
    voxels = frames * row_count * col_count
    owners = piece_lengths.shape[2]
    width = packed_grads.shape[3]
    capacity = width // channels
    grad_scale = 1.0 / math.sqrt(voxels * n_tm * n_rows * n_clip)
    gain_col = norm_gain[:, None]

    packed = packed_grads.reshape(owners, width)
    sent = chunk_rows(packed).reshape(owners, width // 512, 4, COLS)
    arrived = exchange(sent, ("tm", "rows")).reshape(owners * width // COLS, COLS)

    own = activations.reshape(channels, voxels)
    edge = [(channels, 1024), (channels, 384), (channels, 384), (channels, 256), (channels, 256)]
    a_tm, a_top, a_bot, a_dtop, a_dbot = call(edges_kernel, [(s, BF) for s in edge], own)
    around = (
        own,
        shifted(a_tm, "tm", 1),
        shifted(a_bot, "rows", 1),
        shifted(a_top, "rows", -1),
        diagonal(a_dbot, 1),
        diagonal(a_dtop, -1),
    )
    flag = ((8, COLS), F32)
    taps = conv_weights.transpose(1, 0, 2)
    weights, had_weights = call(turn_weights_kernel, [((576, 1792), BF), flag], taps)

    cot3, c_frames = unpack(arrived, piece_lengths.reshape(1, owners), capacity, (had_weights,))
    cot_tm = shifted(c_frames, "tm", -1)

    clip = lax.axis_index("clip").astype(jnp.int32).reshape(1)
    swap_clip = [(0, 1), (1, 0)]
    half = n_tm * DATA
    outs = [((half, COLS), BF)] + [((size, COLS), BF) for size in GIVEN]
    ext = pltpu.VMEM((30 * COLS, channels), BF)
    scratch = [pltpu.VMEM((n_clip * half, COLS), BF), ext]
    keep, *give = call(weight_kernel, outs, clip, gain_col, cot3, *around, scratch=scratch)
    given = [lax.ppermute(piece, "clip", swap_clip) for piece in give]
    scratch = [pltpu.VMEM((half, COLS), F32)]
    part = call(add_kernel, [((n_tm * SHARE, COLS), BF)], keep, *given, scratch=scratch, after=(cot_tm,))[0]
    got = exchange(part.reshape(n_tm, SHARE, COLS), "tm")

    gain_sum = call(gain_kernel, [((2, COLS), F32)], taps, gain_col, cot3, *around, scratch=[ext])[0]

    c_top, c_bot = call(rims_kernel, [((channels, 640), BF)] * 2, cot3, cot_tm)
    cot_bot = shifted(c_top, "rows", -1)
    cot_top = shifted(c_bot, "rows", 1)
    input_grad = call(
        input_kernel,
        [((channels, voxels), BF)],
        own,
        gain_col,
        cot3,
        cot_tm,
        cot_top,
        cot_bot,
        weights,
        scratch=[pltpu.VMEM((channels, 30 * COLS), BF), pltpu.VMEM((1792, 512), BF)],
    )[0]

    had_rims = cot_top[:8, :COLS] + cot_bot[:8, :COLS]

    sent = call(share_kernel, [((n_rows, SHARE, COLS), BF)], got, gain_sum, after=(had_rims,))[0]
    got = exchange(sent, "rows")
    had_grad = input_grad[:8, :COLS]
    sent = call(gather_kernel, [((n_tm, SHARE, COLS), BF)], got, after=(had_grad,))[0]
    mine = exchange(sent, "tm")
    other = lax.ppermute(mine.reshape(n_tm * SHARE, COLS), "clip", swap_clip).reshape(mine.shape)

    def finish(*refs):
        final_kernel(grad_scale, *refs)

    shape = (27, channels, channels)
    scratch = [pltpu.VMEM((n_clip * half, COLS), F32)]
    weight_grad, gain_grad = call(
        finish, [(shape, F32), ((2, COLS), F32)], clip, mine, other, scratch=scratch
    )
    gain_grad = gain_grad.reshape(2 * COLS)[:channels]
    return (input_grad.reshape(activations.shape), weight_grad.transpose(1, 0, 2), gain_grad)


def solution(mesh):
    return jax.shard_map(
        shards,
        mesh=mesh,
        in_specs=(
            P("clip", None, "tm", "rows", None),
            P(),
            P(),
            P("clip", ("tm", "rows"), None, None),
            P("clip", ("tm", "rows"), None),
        ),
        out_specs=(P("clip", None, "tm", "rows", None), P(), P()),
        check_vma=False,
    )
```
